128 devices in a mesh: sub: 4 (over y), tok: 32 (over z, x, core).
Axes of the slice: x: 4, y: 4, z: 4, core: 2. Of those that a mesh axis runs over, the one named last changes fastest.
Arguments:
- token_ids: int32 [8192], P('tok'), may hold values from 0 to 32767
- target_ids: int32 [4096], P('tok'), may hold values from 0 to 32767
- doc_lengths: int32 [512], P('tok'), may hold values from 0 to 128, as said below
- width_tiles: int32 [4, 5], replicated, may hold values from 0 to 1, as said below
- head_mask: int32 [4, 8], replicated, may hold values from 0 to 1, as said below
- ffn_tiles: int32 [4, 24], replicated, may hold values from 0 to 1, as said below
- slot_block: int32 [800], replicated, may hold values from 0 to 780, as said below
- master: float32 [800, 128, 128], P('tok')
- momentum: float32 [800, 128, 128], P('tok'), may hold values from -1.9073486e-05 to 1.9073486e-05
- left_stat: float32 [800, 128, 128], P('tok')
- right_stat: float32 [800, 128, 128], P('tok')
- left_root: float32 [800, 128, 128], P('tok')
- right_root: float32 [800, 128, 128], P('tok')
- table: float32 [32768, 640], P('tok')
- table_m: float32 [32768, 640], P('tok'), may hold values from -2.3841858e-06 to 2.3841858e-06
- table_v: float32 [32768, 640], P('tok'), may hold values from 2.4177034e-13 to 9.658962e-13
- vec: float32 [14, 640], replicated
- vec_m: float32 [14, 640], replicated, may hold values from -2.2888184e-05 to 2.2888184e-05
- vec_v: float32 [14, 640], replicated, may hold values from 2.4177032e-11 to 9.658962e-11
Outputs:
- loss_sum: float32 [], replicated
- token_count: float32 [], replicated
- grad_norm: float32 [], replicated
- new_master: float32 [800, 128, 128], P('tok')
- new_momentum: float32 [800, 128, 128], P('tok')
- new_left: float32 [800, 128, 128], P('tok')
- new_right: float32 [800, 128, 128], P('tok')
- new_table: float32 [32768, 640], P('tok')
- new_table_m: float32 [32768, 640], P('tok')
- new_table_v: float32 [32768, 640], P('tok')
- new_vec: float32 [14, 640], replicated
- new_vec_m: float32 [14, 640], replicated
- new_vec_v: float32 [14, 640], replicated
The draws below stay inside these ranges and needn't reach their ends.
Inputs may be any that keep to these rules, and one draw needn't show every extreme that they name: `doc_lengths`: the lengths of one block sum to at most 128; the last block holds one document of 128. `width_tiles`: each row is a run of ones then zeros; row 0 is all ones; row 4 - 1 has the fewest ones, 4. `head_mask`: each row is a run of ones then zeros; row 0 is all ones; row 4 - 1 has 4 ones. `ffn_tiles`: each row is a run of ones then zeros; row 0 is all ones; row 4 - 1 has 8 ones. `slot_block`: every block number below 780 stands in exactly one slot; the other slots hold 780.
All inputs are finite; a program needn't handle non-finite values.
Results may differ from the reference program's by a relative error of at most 0.0025.
The reference program's roundings to bfloat16 on the way count: a program that leaves them out, or rounds other values in their place, can miss the bound.
Values may be sent and summed in bfloat16 or wider, within the bound.
A program may use at most 384 MiB of HBM per device.

```python
import math
from functools import partial
import jax
import jax.numpy as jnp
import numpy as np
from jax import lax

D = 640
HEADS = 8
HEAD = 80
FF = 3072
V = 32768
BLK = 128
TOK_DEV = 256
DOCS = 16
STEP = 10
HALF = 128
TOKENS = 8192
NBLK = 780
SLOTS = 800
N_SUB = 4
N_TOK = 32


def grad_scale():
    return 0.02 * (V * D + 12 * D * D + 4 * D * FF) ** (-0.5)


def stat_level():
    return (1.0 - 0.95) / 0.95 * BLK * grad_scale() ** 2


def slot_table(key):
    order = jax.random.permutation(key, SLOTS)
    return jnp.minimum(order, NBLK).astype(jnp.int32)


def prefix_rows(key, tiles_count, lowest):
    counts = jax.random.randint(key, (N_SUB,), lowest, tiles_count + 1)
    group = jnp.arange(N_SUB)
    counts = jnp.where(group == 0, tiles_count, jnp.where(group == N_SUB - 1, lowest, counts))
    return (jnp.arange(tiles_count)[None, :] < counts[:, None]).astype(jnp.int32)


def diagonal_stat(key):
    diagonal = jax.random.uniform(key, (SLOTS, BLK), minval=1.0, maxval=4.0) * stat_level()
    return (diagonal[:, :, None] * jnp.eye(BLK, dtype=jnp.float32)[None]).astype(jnp.float32)


def root_matrix(key):
    first, second = jax.random.split(key)
    base = stat_level() ** (-0.25)
    diagonal = jax.random.uniform(first, (SLOTS, BLK), minval=0.5, maxval=2.0) * base
    spread = jax.random.normal(second, (SLOTS, BLK, BLK)) * (0.02 * base)
    return (diagonal[:, :, None] * jnp.eye(BLK, dtype=jnp.float32)[None] + spread).astype(jnp.float32)


def block_scales():
    wide = D // BLK
    deep = FF // BLK
    inner = D ** (-0.5)
    outer = 3.0 * D ** (-0.5)
    lower = FF ** (-0.5)
    shapes = [(wide * 3 * wide, inner), (wide * wide, outer), (wide * deep, inner), (deep * wide, lower), (wide * 3 * wide, inner), (wide * wide, outer), (wide * wide, inner), (wide * 2 * wide, inner), (wide * wide, outer), (wide * deep, inner), (deep * wide, lower), (1, 1.0)]
    return jnp.concatenate([jnp.full((count,), value, jnp.float32) for count, value in shapes])


def draw_doc_lengths(key, part):
    key = jax.random.fold_in(key, 1)
    first, second = jax.random.split(key)
    device = jnp.arange(N_TOK, dtype=jnp.int32)
    extra = jax.random.randint(first, (N_TOK,), 0, HALF // 8 + 1)
    totals = jnp.minimum(HALF // 3 + 2 * HALF * device // (3 * (N_TOK - 1)) + extra, HALF)
    totals = jnp.where(device == N_TOK - 1, HALF, totals)
    short = jax.random.randint(second, (N_TOK, DOCS - 1), 1, 40)
    short = jnp.where(device[:, None] == N_TOK - 1, 0, short)
    before = jnp.cumsum(short, axis=1) - short
    kept = jnp.clip(totals[:, None] - 1 - before, 0, short)
    long_part = totals - jnp.sum(kept, 1)
    return jnp.concatenate([kept, long_part[:, None]], 1).reshape(-1).astype(jnp.int32)


def draw_width_tiles(key, part):
    key = jax.random.fold_in(key, 2)
    return prefix_rows(key, D // BLK, max(1, D // BLK - 1))


def draw_head_mask(key, part):
    key = jax.random.fold_in(key, 3)
    return prefix_rows(key, HEADS, HEADS // 2)


def draw_ffn_tiles(key, part):
    key = jax.random.fold_in(key, 4)
    return prefix_rows(key, FF // BLK, max(1, FF // BLK // 3))


def draw_slot_block(key, part):
    return slot_table(key)


def draw_master(key, part):
    holder = slot_table(key)
    key = jax.random.fold_in(key, 5)
    scale = block_scales()[holder]
    return (jax.random.normal(key, (SLOTS, BLK, BLK)) * scale[:, None, None]).astype(jnp.float32)


def draw_left_stat(key, part):
    key = jax.random.fold_in(key, 6)
    return diagonal_stat(key)


def draw_right_stat(key, part):
    key = jax.random.fold_in(key, 7)
    return diagonal_stat(key)


def draw_left_root(key, part):
    key = jax.random.fold_in(key, 8)
    return root_matrix(key)


def draw_right_root(key, part):
    key = jax.random.fold_in(key, 9)
    return root_matrix(key)


def draw_table(key, part):
    key = jax.random.fold_in(key, 10)
    shard = (jnp.arange(V) // (V // N_TOK)).astype(jnp.float32)
    rise = 1.0 + 2.0 * shard / (N_TOK - 1)
    values = jax.random.normal(key, (V, D))
    return (values * rise[:, None] * D ** (-0.5)).astype(jnp.float32)


def draw_vec(key, part):
    key = jax.random.fold_in(key, 11)
    first, second = jax.random.split(key)
    gains = jax.random.uniform(first, (7, D), minval=0.6, maxval=1.4)
    biases = 0.3 * jax.random.normal(second, (7, D))
    return jnp.stack([gains, biases], 1).reshape(14, D).astype(jnp.float32)


def with_ends(array, own_key, low, largest):
    dims = array.shape
    spot = [jax.random.randint(jax.random.fold_in(own_key, axis), (), 0, dims[axis]) for axis in range(len(dims))]
    array = array.at[tuple(spot)].set(low)
    longest = dims.index(max(dims))
    spot[longest] = (spot[longest] + 1) % dims[longest]
    return array.at[tuple(spot)].set(largest)


def block_scale(stream_key, dims, pieces, low, high):
    factor_of, own = 1.0, jax.random.fold_in(stream_key, 6)
    for position, shards_of in pieces:
        draws = jnp.exp(jax.random.uniform(jax.random.fold_in(own, position), (shards_of,), jnp.float32, low / len(pieces), high / len(pieces)))
        factor_of = factor_of * jnp.repeat(draws, dims[position] // shards_of).reshape([-1 if axis == position else 1 for axis in range(len(dims))])
    return factor_of


def cumulative_ranks(amount, skew):
    loads = [(1 << 20) // math.isqrt(grade ** skew) + 1 for grade in range(1, amount + 1)]
    deviation = 1 + sum(loads) // (1 << 30)
    return np.cumsum(np.array([max(1, weight // deviation) for weight in loads]))


def ranked(rng, dims, count, slope):
    grid = cumulative_ranks(count, slope)
    lot = jax.random.randint(jax.random.fold_in(rng, 1), dims, 0, int(grid[count - 1]))
    standing = jnp.searchsorted(jnp.asarray(grid, jnp.int32), lot, side="right")
    return jax.random.permutation(jax.random.fold_in(rng, 2), count)[standing].astype(jnp.int32)


def scatter_about(stream_key, shape, scale, most, cuts=(), kind=jnp.bfloat16):
    array = scale * jax.random.normal(stream_key, shape, jnp.float32)
    if cuts:
        array = array * block_scale(stream_key, shape, cuts, -0.22, 0.18)
    return jnp.clip(array, -most, most).astype(kind)


def setup_inputs(seed: int = 0) -> dict:
    arg_keys = jax.random.split(jax.random.key(seed), 20)
    token_ids = with_ends(ranked(arg_keys[0], (TOKENS,), V, 2), jax.random.fold_in(arg_keys[0], 3), 0, V - 1).astype(jnp.int32)
    target_ids = with_ends(ranked(arg_keys[1], (TOKENS // 2,), V, 2), jax.random.fold_in(arg_keys[1], 3), 0, V - 1).astype(jnp.int32)
    doc_lengths = draw_doc_lengths(jax.random.fold_in(arg_keys[19], 71), 0)
    width_tiles = draw_width_tiles(jax.random.fold_in(arg_keys[19], 71), 0)
    head_mask = draw_head_mask(jax.random.fold_in(arg_keys[19], 71), 0)
    ffn_tiles = draw_ffn_tiles(jax.random.fold_in(arg_keys[19], 71), 0)
    slot_block = draw_slot_block(jax.random.fold_in(arg_keys[19], 71), 0)
    master = draw_master(jax.random.fold_in(arg_keys[19], 71), 0)
    momentum = scatter_about(arg_keys[8], (SLOTS, BLK, BLK), (0.02 * (V * D + 12 * D * D + 4 * D * FF) ** -0.5), 1.9073486328125e-05, ((0, 32),), jnp.float32)
    left_stat = draw_left_stat(jax.random.fold_in(arg_keys[19], 71), 0)
    right_stat = draw_right_stat(jax.random.fold_in(arg_keys[19], 71), 0)
    left_root = draw_left_root(jax.random.fold_in(arg_keys[19], 71), 0)
    right_root = draw_right_root(jax.random.fold_in(arg_keys[19], 71), 0)
    table = draw_table(jax.random.fold_in(arg_keys[19], 71), 0)
    table_m = scatter_about(arg_keys[14], (V, D), (0.0022 * (V * D + 12 * D * D + 4 * D * FF) ** -0.5), 2.384185791015625e-06, ((0, 32),), jnp.float32)
    table_v = jnp.clip(jnp.exp(math.log(9.658961998282312e-13) - 1.38506813 * jax.random.uniform(arg_keys[15], (V, D), jnp.float32) ** block_scale(arg_keys[15], (V, D), ((0, 32),), -0.2, 0.2)), 2.4177033530574377e-13, 9.658961998282312e-13)
    vec = draw_vec(jax.random.fold_in(arg_keys[19], 71), 0)
    vec_m = scatter_about(arg_keys[17], (14, D), (0.022 * (V * D + 12 * D * D + 4 * D * FF) ** -0.5), 2.288818359375e-05, (), jnp.float32)
    vec_v = jnp.clip(jnp.exp(jax.random.uniform(arg_keys[18], (14, D), jnp.float32, math.log(2.4177031904271118e-11), math.log(9.658961824809964e-11))), 2.4177031904271118e-11, 9.658961824809964e-11)
    return dict(token_ids=token_ids, target_ids=target_ids, doc_lengths=doc_lengths, width_tiles=width_tiles, head_mask=head_mask, ffn_tiles=ffn_tiles, slot_block=slot_block, master=master, momentum=momentum, left_stat=left_stat, right_stat=right_stat, left_root=left_root, right_root=right_root, table=table, table_m=table_m, table_v=table_v, vec=vec, vec_m=vec_m, vec_v=vec_v)


@jax.custom_vjp
def low(v):
    return lax.optimization_barrier(v.astype(jnp.bfloat16)).astype(jnp.float32)

@jax.custom_vjp
def low_back(v):
    return v

def low_keep(v):
    return (low(v), None)

def low_pass(kept, grad):
    return (grad,)

def back_keep(v):
    return (v, None)

def back_low(kept, grad):
    return (low(grad),)
low.defvjp(low_keep, low_pass)
low_back.defvjp(back_keep, back_low)
eps_norm = 1e-05
clip_limit = 0.02
beta_one = 0.9
beta_two = 0.98
beta_stat = 0.95
decay_rate = 0.01
adam_eps = 1e-08
rate_table = 0.05
rate_gains = 0.3
rate_blocks = 0.05
high = lax.Precision.HIGHEST

def doc_layout(lengths):
    ends = jnp.cumsum(lengths, axis=-1)
    starts = ends - lengths
    place = jnp.arange(HALF, dtype=jnp.int32)
    member = ((place[:, None] >= starts[..., None, :]) & (place[:, None] < ends[..., None, :])).astype(jnp.int32)
    inside = lax.optimization_barrier(jnp.sum(member, -1))
    doc_of = lax.optimization_barrier(jnp.sum(member * jnp.arange(DOCS, dtype=jnp.int32), -1)) + DOCS * (1 - inside)
    offset = place - lax.optimization_barrier(jnp.sum(member * starts[..., None, :], -1))
    return (doc_of, offset, inside)

def sinusoid(offset):
    half = D // 2
    freq = jnp.exp(jnp.arange(half, dtype=jnp.float32) * (-2.0 * math.log(10000.0) / D))
    angle = offset.astype(jnp.float32)[..., None] * freq
    return jnp.stack([jnp.sin(angle), jnp.cos(angle)], -1).reshape(offset.shape + (D,))

def norm(stream, gain, bias, width, active):
    centre = lax.optimization_barrier(jnp.sum(stream * width, -1, keepdims=True)) / active
    centred = (stream - centre) * width
    spread = lax.optimization_barrier(jnp.sum(centred * centred, -1, keepdims=True)) / active
    return (centred * lax.rsqrt(spread + eps_norm) * gain + bias) * width

def layout():
    wide = D // BLK
    deep = FF // BLK
    return [(wide, 3 * wide), (wide, wide), (wide, deep), (deep, wide), (wide, 3 * wide), (wide, wide), (wide, wide), (wide, 2 * wide), (wide, wide), (wide, deep), (deep, wide)]

def unpack(blocks):
    result = []
    start = 0
    for rows, cols in layout():
        part = blocks[start:start + rows * cols]
        start = start + rows * cols
        result.append(part.reshape(rows, cols, BLK, BLK).transpose(0, 2, 1, 3).reshape(rows * BLK, cols * BLK))
    return result

def project(inputs, matrix):
    return jnp.einsum('tpd,de->tpe', inputs, matrix, precision=high)

def split_heads(inputs, count):
    return inputs.reshape(N_TOK, HALF, count, HEADS, HEAD)

def attend(query, keys, values, allowed, head_keep):
    scores = low_back(jnp.einsum('tqhc,tkhc->thqk', query, keys, precision=high) * HEAD ** (-0.5))
    scores = jnp.where(allowed[:, None], scores, -1e+30)
    probs = low(jax.nn.softmax(scores, axis=-1))
    mixed = low_back(jnp.einsum('thqk,tkhc->tqhc', probs, values, precision=high))
    return low((mixed * head_keep[:, None]).reshape(N_TOK, HALF, D))

def group_forward(table_low, blocks, vec, ids, doc_of, offset, widths, heads, units):
    mats = unpack(blocks)
    width = jnp.repeat(widths, BLK).astype(jnp.float32)
    active = jnp.sum(width)
    head_keep = heads.astype(jnp.float32)
    unit_keep = jnp.repeat(units, BLK).astype(jnp.float32)
    rows = low_back(table_low[ids])
    wave = sinusoid(offset)
    source = (math.sqrt(D) * rows[:, :HALF] + wave) * width
    target = (math.sqrt(D) * rows[:, HALF:] + wave) * width
    same = doc_of[:, :, None] == doc_of[:, None, :]
    causal = same & (offset[:, None, :] <= offset[:, :, None])

    def self_part(stream, index, w_qkv, w_out, allowed):
        normed = low(norm(stream, vec[index], vec[index + 1], width, active))
        packed = split_heads(low_back(low(project(normed, w_qkv))), 3)
        mixed = attend(packed[:, :, 0], packed[:, :, 1], packed[:, :, 2], allowed, head_keep)
        return stream + low_back(project(mixed, w_out)) * width

    def feed_part(stream, index, w_up, w_down):
        normed = low(norm(stream, vec[index], vec[index + 1], width, active))
        hidden_pre = low_back(project(normed, w_up))
        activated = low(jax.nn.gelu(hidden_pre) * unit_keep)
        return stream + low_back(project(activated, w_down)) * width
    encoded = feed_part(self_part(source, 0, mats[0], mats[1], same), 2, mats[2], mats[3])
    memory = low(norm(encoded, vec[4], vec[5], width, active))
    decoded = self_part(target, 6, mats[4], mats[5], causal)
    normed = low(norm(decoded, vec[8], vec[9], width, active))
    query = split_heads(low_back(low(project(normed, mats[6]))), 1)[:, :, 0]
    paired = split_heads(low_back(low(project(memory, mats[7]))), 2)
    mixed = attend(query, paired[:, :, 0], paired[:, :, 1], same, head_keep)
    decoded = decoded + low_back(project(mixed, mats[8])) * width
    decoded = feed_part(decoded, 10, mats[9], mats[10])
    return low(norm(decoded, vec[12], vec[13], width, active)).reshape(N_TOK * HALF, D)

def log_total(logits):
    peak = lax.optimization_barrier(jnp.max(logits, -1, keepdims=True))
    return peak[:, 0] + jnp.log(lax.optimization_barrier(jnp.sum(jnp.exp(logits - peak), -1)))

def head_block(items, table_low, table_fixed, teach):
    hidden, teacher_hidden, target, weight = items
    logits = low_back(jnp.dot(hidden, table_low.T, precision=high))
    student_total = log_total(logits)
    if teach:
        teacher = jnp.dot(teacher_hidden, table_fixed.T, precision=high)
        teacher_total = log_total(teacher)
        target_dist = jnp.exp(teacher - teacher_total[:, None])
        loss = student_total + lax.optimization_barrier(jnp.sum(target_dist * (teacher - logits), -1)) - teacher_total
    else:
        hits = (jnp.arange(V, dtype=jnp.int32)[None, :] == target[:, None]).astype(jnp.float32)
        loss = student_total - lax.optimization_barrier(jnp.sum(hits * logits, -1))
    return jnp.sum(loss * weight)

def adamw(param, grad, first, second, rate):
    first = beta_one * first + (1.0 - beta_one) * grad
    second = beta_two * second + (1.0 - beta_two) * grad * grad
    fixed_first = first / (1.0 - beta_one ** STEP)
    fixed_second = second / (1.0 - beta_two ** STEP)
    return (param - rate * (fixed_first / (jnp.sqrt(fixed_second) + adam_eps) + decay_rate * param), first, second)

def reference(token_ids, target_ids, doc_lengths, width_tiles, head_mask, ffn_tiles, slot_block, master, momentum, left_stat, right_stat, left_root, right_root, table, table_m, table_v, vec, vec_m, vec_v):
    doc_of, offset, inside = doc_layout(doc_lengths.reshape(N_TOK, DOCS))
    ids = token_ids.reshape(N_TOK, TOK_DEV)
    weight = inside.reshape(N_TOK * HALF).astype(jnp.float32)
    token_count = jnp.sum(weight)
    inverse = jnp.zeros((NBLK + 1,), jnp.int32).at[slot_block].set(jnp.arange(SLOTS, dtype=jnp.int32))[:NBLK]
    table_fixed = table.astype(jnp.bfloat16).astype(jnp.float32)

    def hidden_of(table_low, master_low, vec_f, group):
        return group_forward(table_low, master_low[inverse], vec_f, ids, doc_of, offset, width_tiles[group], head_mask[group], ffn_tiles[group])
    teacher_hidden = hidden_of(low(table), low(master), vec, 0)
    rows_all = N_TOK * HALF
    block = min(rows_all, 1024)
    count_blocks = rows_all // block

    def total(table_f, master_f, vec_f):
        table_low = low(table_f)
        master_low = low(master_f)
        summed = jnp.zeros((), jnp.float32)
        for group in range(N_SUB):
            hidden = hidden_of(table_low, master_low, vec_f, group)
            items = (hidden.reshape(count_blocks, block, D), teacher_hidden.reshape(count_blocks, block, D), target_ids.reshape(count_blocks, block), weight.reshape(count_blocks, block))
            step_fn = jax.checkpoint(partial(head_block, table_low=table_low, table_fixed=table_fixed, teach=min(group, 1)))
            summed = summed + jnp.sum(lax.map(step_fn, items))
        return summed
    loss_sum, pull = jax.vjp(total, table, master, vec)
    grad_table, grad_master, grad_vec = pull(1.0 / token_count)
    square = jnp.sum(grad_table * grad_table) + jnp.sum(grad_master * grad_master) + jnp.sum(grad_vec * grad_vec)
    grad_norm = jnp.sqrt(square)
    scale = jnp.minimum(1.0, clip_limit / grad_norm)
    grad = grad_master * scale
    new_left = beta_stat * left_stat + (1.0 - beta_stat) * jnp.einsum('sij,skj->sik', grad, grad, precision=high)
    new_right = beta_stat * right_stat + (1.0 - beta_stat) * jnp.einsum('sji,sjk->sik', grad, grad, precision=high)
    new_momentum = beta_one * momentum + (1.0 - beta_one) * grad
    direction = jnp.einsum('sij,sjk->sik', left_root, new_momentum, precision=high)
    direction = jnp.einsum('sik,skl->sil', direction, right_root, precision=high)
    new_master = master - rate_blocks * (direction + decay_rate * master)
    new_table, new_table_m, new_table_v = adamw(table, grad_table * scale, table_m, table_v, rate_table)
    new_vec, new_vec_m, new_vec_v = adamw(vec, grad_vec * scale, vec_m, vec_v, rate_gains)
    return (loss_sum, token_count, grad_norm, new_master, new_momentum, new_left, new_right, new_table, new_table_m, new_table_v, new_vec, new_vec_m, new_vec_v)
```

```python
import math

import jax
import jax.numpy as jnp
from jax import lax
from jax.sharding import Mesh
from jax.sharding import PartitionSpec as P

D = 640
HEADS = 8
HEAD = 80
FF = 3072
BLK = 128
DOCS = 16
STEP = 10
HALF = 128
NBLK = 780
TOK = ("tok_0", "tok_1", "tok_2")


eps_norm = 1e-05
clip_limit = 0.02
beta_one = 0.9
beta_two = 0.98
beta_stat = 0.95
decay_rate = 0.01
adam_eps = 1e-08
rate_table = 0.05
rate_gains = 0.3
rate_blocks = 0.05
high = lax.Precision.HIGHEST
low_type = jnp.bfloat16
wide_type = jnp.float32


def quarter(value, part, count):
    return lax.dynamic_slice_in_dim(value, part * count, count, 0)


def gather_tok(value):
    return lax.all_gather(value, TOK, axis=0)


def scatter_tok(value):
    return lax.psum_scatter(value, TOK, scatter_dimension=0)


def swap_sub(value):
    return lax.all_to_all(value, "sub", split_axis=0, concat_axis=0, tiled=True)


def doc_layout(lengths):
    ends = jnp.cumsum(lengths, axis=-1)
    starts = ends - lengths
    place = jnp.arange(HALF, dtype=jnp.int32)
    member = (
        (place[:, None] >= starts[..., None, :]) & (place[:, None] < ends[..., None, :])
    ).astype(jnp.int32)
    inside = jnp.sum(member, -1)
    doc_of = jnp.sum(member * jnp.arange(DOCS, dtype=jnp.int32), -1) + DOCS * (1 - inside)
    offset = place - jnp.sum(member * starts[..., None, :], -1)
    return (doc_of, offset, inside)


def sinusoid(offset):
    half = D // 2
    freq = jnp.exp(jnp.arange(half, dtype=jnp.float32) * (-2.0 * math.log(10000.0) / D))
    angle = offset.astype(jnp.float32)[..., None] * freq
    return jnp.stack([jnp.sin(angle), jnp.cos(angle)], -1).reshape(offset.shape + (D,))


def norm(stream, gain, bias, width, active):
    centre = jnp.sum(stream * width, -1, keepdims=True) / active
    centred = (stream - centre) * width
    spread = jnp.sum(centred * centred, -1, keepdims=True) / active
    return (centred * lax.rsqrt(spread + eps_norm) * gain + bias) * width


def norm_pull(stream, gain, bias, width, active, cotangent):
    _, pull = jax.vjp(
        lambda first, second, third: norm(first, second, third, width, active), stream, gain, bias
    )
    return pull(cotangent)


def layout():
    wide = D // BLK
    deep = FF // BLK
    return [
        (wide, 3 * wide),
        (wide, wide),
        (wide, deep),
        (deep, wide),
        (wide, 3 * wide),
        (wide, wide),
        (wide, wide),
        (wide, 2 * wide),
        (wide, wide),
        (wide, deep),
        (deep, wide),
    ]


def unpack(blocks):
    result = []
    start = 0
    for rows, cols in layout():
        part = blocks[start : start + rows * cols]
        start = start + rows * cols
        result.append(
            part.reshape(rows, cols, BLK, BLK).transpose(0, 2, 1, 3).reshape(rows * BLK, cols * BLK)
        )
    return result


def pack(matrices):
    pieces = []
    for matrix in matrices:
        rows = matrix.shape[0] // BLK
        cols = matrix.shape[1] // BLK
        pieces.append(
            matrix.reshape(rows, BLK, cols, BLK)
            .transpose(0, 2, 1, 3)
            .reshape(rows * cols, BLK, BLK)
        )
    return jnp.concatenate(pieces, 0)


def matmul(left, right):
    return jnp.dot(left, right, preferred_element_type=wide_type)


def attend(query, keys, values, allowed, head_keep):
    scores = jnp.einsum("qhc,khc->hqk", query, keys, preferred_element_type=wide_type) * HEAD ** (
        -0.5
    )
    scores = jnp.where(allowed[None], scores, -1e30)
    peak = jnp.max(scores, -1, keepdims=True)
    expo = jnp.exp(scores - peak)
    probs = expo / jnp.sum(expo, -1, keepdims=True)
    probs_low = probs.astype(low_type)
    mixed = jnp.einsum("hqk,khc->qhc", probs_low, values, preferred_element_type=wide_type)
    mixed = (mixed * head_keep[:, None]).reshape(query.shape[0], D).astype(low_type)
    return (mixed, (query, keys, values, probs, probs_low))


def attend_back(d_rows, inner, head_keep):
    query, keys, values, probs, probs_low = inner
    d_mixed = (d_rows.reshape(query.shape) * head_keep[:, None]).astype(low_type)
    g_probs = jnp.einsum("qhc,khc->hqk", d_mixed, values, preferred_element_type=wide_type)
    d_values = jnp.einsum("hqk,qhc->khc", probs_low, d_mixed, preferred_element_type=wide_type)
    d_scores = (probs * (g_probs - jnp.sum(probs * g_probs, -1, keepdims=True))).astype(low_type)
    scale = HEAD ** (-0.5)
    d_query = jnp.einsum("hqk,khc->qhc", d_scores, keys, preferred_element_type=wide_type) * scale
    d_keys = jnp.einsum("hqk,qhc->khc", d_scores, query, preferred_element_type=wide_type) * scale
    return (d_query, d_keys, d_values)


def branch_back(d_out, inputs, w_out, width):
    d_branch = (d_out * width).astype(low_type)
    g_out = jnp.einsum("td,te->de", inputs, d_branch, preferred_element_type=wide_type)
    d_inputs = jnp.einsum("te,de->td", d_branch, w_out, preferred_element_type=wide_type)
    return (g_out, d_inputs)


def self_block(stream, gain, bias, w_qkv, w_out, masks, allowed):
    width, active, head_keep, unit_keep = masks
    span = stream.shape[0]
    normed = norm(stream, gain, bias, width, active).astype(low_type)
    packed = matmul(normed, w_qkv).astype(low_type).reshape(span, 3, HEADS, HEAD)
    mixed, inner = attend(packed[:, 0], packed[:, 1], packed[:, 2], allowed, head_keep)
    return (stream + matmul(mixed, w_out) * width, (stream, normed, mixed, inner))


def self_back(d_out, kept, gain, bias, w_qkv, w_out, masks):
    width, active, head_keep, unit_keep = masks
    stream, normed, mixed, inner = kept
    span = stream.shape[0]
    g_out, d_mixed = branch_back(d_out, mixed, w_out, width)
    d_query, d_keys, d_values = attend_back(d_mixed, inner, head_keep)
    d_packed = jnp.stack([d_query, d_keys, d_values], 1).reshape(span, 3 * D).astype(low_type)
    g_qkv = jnp.einsum("td,te->de", normed, d_packed, preferred_element_type=wide_type)
    d_first = jnp.einsum("te,de->td", d_packed, w_qkv, preferred_element_type=wide_type)
    d_in, g_gain, g_bias = norm_pull(stream, gain, bias, width, active, d_first)
    return (d_out + d_in, [g_qkv, g_out], [g_gain, g_bias])


def cross_block(stream, memory, gain, bias, w_query, w_pair, w_out, masks, allowed):
    width, active, head_keep, unit_keep = masks
    span = stream.shape[0]
    normed = norm(stream, gain, bias, width, active).astype(low_type)
    query = matmul(normed, w_query).astype(low_type).reshape(span, HEADS, HEAD)
    paired = matmul(memory, w_pair).astype(low_type).reshape(memory.shape[0], 2, HEADS, HEAD)
    mixed, inner = attend(query, paired[:, 0], paired[:, 1], allowed, head_keep)
    return (stream + matmul(mixed, w_out) * width, (stream, normed, mixed, inner))


def cross_back(d_out, kept, memory, gain, bias, w_query, w_pair, w_out, masks):
    width, active, head_keep, unit_keep = masks
    stream, normed, mixed, inner = kept
    span = stream.shape[0]
    g_out, d_mixed = branch_back(d_out, mixed, w_out, width)
    d_query, d_keys, d_values = attend_back(d_mixed, inner, head_keep)
    d_query = d_query.reshape(span, D).astype(low_type)
    d_pair = jnp.stack([d_keys, d_values], 1).reshape(memory.shape[0], 2 * D).astype(low_type)
    g_query = jnp.einsum("td,te->de", normed, d_query, preferred_element_type=wide_type)
    g_pair = jnp.einsum("td,te->de", memory, d_pair, preferred_element_type=wide_type)
    d_memory = jnp.einsum("te,de->td", d_pair, w_pair, preferred_element_type=wide_type)
    d_first = jnp.einsum("te,de->td", d_query, w_query, preferred_element_type=wide_type)
    d_in, g_gain, g_bias = norm_pull(stream, gain, bias, width, active, d_first)
    return (d_out + d_in, d_memory, [g_query, g_pair, g_out], [g_gain, g_bias])


def feed_block(stream, gain, bias, w_up, w_down, masks):
    width, active, head_keep, unit_keep = masks
    normed = norm(stream, gain, bias, width, active).astype(low_type)
    hidden_pre = matmul(normed, w_up)
    activated = (jax.nn.gelu(hidden_pre) * unit_keep).astype(low_type)
    return (stream + matmul(activated, w_down) * width, (stream, normed, hidden_pre, activated))


def feed_back(d_out, kept, gain, bias, w_up, w_down, masks):
    width, active, head_keep, unit_keep = masks
    stream, normed, hidden_pre, activated = kept
    g_down, d_act = branch_back(d_out, activated, w_down, width)
    _, gelu_pull = jax.vjp(jax.nn.gelu, hidden_pre)
    d_pre = gelu_pull(d_act * unit_keep)[0].astype(low_type)
    g_up = jnp.einsum("td,tf->df", normed, d_pre, preferred_element_type=wide_type)
    d_normed = jnp.einsum("tf,df->td", d_pre, w_up, preferred_element_type=wide_type)
    d_in, g_gain, g_bias = norm_pull(stream, gain, bias, width, active, d_normed)
    return (d_out + d_in, [g_up, g_down], [g_gain, g_bias])


def adamw(param, grad, first, second, rate):
    first = beta_one * first + (1.0 - beta_one) * grad
    second = beta_two * second + (1.0 - beta_two) * grad * grad
    fixed_first = first / (1.0 - beta_one**STEP)
    fixed_second = second / (1.0 - beta_two**STEP)
    return (
        param - rate * (fixed_first / (jnp.sqrt(fixed_second) + adam_eps) + decay_rate * param),
        first,
        second,
    )


def on_device(
    token_ids,
    target_ids,
    doc_lengths,
    width_tiles,
    head_mask,
    ffn_tiles,
    slot_block,
    master,
    momentum,
    left_stat,
    right_stat,
    left_root,
    right_root,
    table,
    table_m,
    table_v,
    vec,
    vec_m,
    vec_v,
):
    group = lax.axis_index("sub")
    place = lax.axis_index(TOK)
    groups = lax.axis_size("sub")
    shards = lax.axis_size(TOK)
    shard_rows = table.shape[0]
    piece = HALF // groups
    doc_of, offset, inside = doc_layout(doc_lengths)
    mine = jnp.concatenate(
        [
            quarter(token_ids[:HALF], group, piece),
            quarter(token_ids[HALF:], group, piece),
            quarter(jnp.where(inside > 0, target_ids, -1), group, piece),
            jnp.broadcast_to(jnp.sum(inside), (HALF - 3 * piece,)),
        ]
    )
    table_low = table.astype(low_type)
    heads_up = gather_tok(mine)
    slots = gather_tok(master.astype(low_type)).reshape(-1, BLK, BLK)
    all_targets = heads_up[:, 2 * piece : 3 * piece]
    weight = (all_targets >= 0).astype(jnp.float32)
    token_count = jnp.sum(heads_up[:, 3 * piece]).astype(jnp.float32)
    first_row = place * shard_rows
    local = (heads_up[:, : 2 * piece] - first_row).reshape(-1)
    picks = (local[:, None] == jnp.arange(shard_rows, dtype=jnp.int32)).astype(low_type)
    picked = matmul(picks, table_low).astype(low_type).reshape(shards, 2 * piece, D)
    rows = lax.all_gather(scatter_tok(picked), "sub").astype(jnp.float32)
    rows = rows.reshape(groups, 2, piece, D).transpose(1, 0, 2, 3).reshape(2, HALF, D)
    inverse = jnp.sum(
        jnp.where(
            slot_block[None, :] == jnp.arange(NBLK, dtype=jnp.int32)[:, None],
            jnp.arange(slot_block.shape[0], dtype=jnp.int32)[None, :],
            0,
        ),
        1,
    )
    mats = unpack(slots[inverse])
    width = jnp.repeat(width_tiles[group], BLK).astype(jnp.float32)
    active = jnp.sum(width)
    head_keep = head_mask[group].astype(jnp.float32)
    unit_keep = jnp.repeat(ffn_tiles[group], BLK).astype(jnp.float32)
    masks = (width, active, head_keep, unit_keep)
    wave = sinusoid(offset)
    source = (math.sqrt(D) * rows[0] + wave) * width
    target = (math.sqrt(D) * rows[1] + wave) * width
    same = doc_of[:, None] == doc_of[None, :]
    causal = same & (offset[None, :] <= offset[:, None])
    enc_one, kept_one = self_block(source, vec[0], vec[1], mats[0], mats[1], masks, same)
    enc_two, kept_two = feed_block(enc_one, vec[2], vec[3], mats[2], mats[3], masks)
    memory = norm(enc_two, vec[4], vec[5], width, active).astype(low_type)
    dec_one, kept_three = self_block(target, vec[6], vec[7], mats[4], mats[5], masks, causal)
    dec_two, kept_four = cross_block(
        dec_one, memory, vec[8], vec[9], mats[6], mats[7], mats[8], masks, same
    )
    dec_three, kept_five = feed_block(dec_two, vec[10], vec[11], mats[9], mats[10], masks)
    final = norm(dec_three, vec[12], vec[13], width, active).astype(low_type)
    hidden = gather_tok(swap_sub(final.reshape(groups, piece, D))).reshape(-1, D)
    logits = jnp.einsum("td,vd->tv", hidden, table_low, preferred_element_type=wide_type)
    logits = logits.reshape(shards, groups, piece, shard_rows)
    teacher = logits[:, :1]
    peak = jnp.max(logits, -1)
    total = jnp.sum(jnp.exp(logits - peak[..., None]), -1)
    hits = all_targets[..., None] - first_row == jnp.arange(shard_rows, dtype=jnp.int32)
    hit = jnp.sum(jnp.where(hits, logits[:, 0], 0.0), -1)
    gap = jnp.sum(jnp.exp(teacher - peak[:, :1, :, None]) * (teacher - logits[:, 1:]), -1)
    stats = gather_tok(jnp.concatenate([peak, total, hit[:, None], gap], 1))
    peaks, totals, extra = jnp.split(stats, [groups, 2 * groups], 2)
    peak = jnp.max(peaks, 0)
    rescale = jnp.exp(peaks - peak)
    total = jnp.sum(totals * rescale, 0)
    logs = peak + jnp.log(total)
    hit = jnp.sum(extra[:, :, 0], 0)
    gap = jnp.sum(extra[:, :, 1:] * rescale[:, :, :1], 0) / total[:, :1]
    token_loss = logs[:, 0] - hit + jnp.sum(logs[:, 1:] + gap - logs[:, :1], 1)
    loss_part = jnp.sum(token_loss * weight)
    target_dist = jnp.concatenate(
        [
            hits.astype(jnp.float32)[:, None],
            jnp.broadcast_to(
                jnp.exp(teacher - logs[:, :1, :, None]),
                (shards, groups - 1, piece, shard_rows),
            ),
        ],
        1,
    )
    back = (jnp.exp(logits - logs[..., None]) - target_dist) * (weight / token_count)[
        :, None, :, None
    ]
    back = back.astype(low_type).reshape(-1, shard_rows)
    d_hidden = matmul(back, table_low).astype(low_type).reshape(shards, groups * piece, D)
    d_final = scatter_tok(d_hidden).reshape(groups, piece, D)
    d_final = swap_sub(d_final).reshape(HALF, D).astype(jnp.float32)
    table_grad = jnp.einsum("tv,td->vd", back, hidden, preferred_element_type=wide_type)
    d_three, g_twelve, g_thirteen = norm_pull(dec_three, vec[12], vec[13], width, active, d_final)
    d_two, grads_dec_feed, gains_five = feed_back(
        d_three, kept_five, vec[10], vec[11], mats[9], mats[10], masks
    )
    d_one, d_memory, grads_cross, gains_four = cross_back(
        d_two, kept_four, memory, vec[8], vec[9], mats[6], mats[7], mats[8], masks
    )
    d_target, grads_dec_self, gains_three = self_back(
        d_one, kept_three, vec[6], vec[7], mats[4], mats[5], masks
    )
    d_enc_two, g_four, g_five = norm_pull(enc_two, vec[4], vec[5], width, active, d_memory)
    d_enc_one, grads_enc_feed, gains_two = feed_back(
        d_enc_two, kept_two, vec[2], vec[3], mats[2], mats[3], masks
    )
    d_source, grads_enc_self, gains_one = self_back(
        d_enc_one, kept_one, vec[0], vec[1], mats[0], mats[1], masks
    )
    d_rows = (jnp.stack([d_source, d_target], 0) * width * math.sqrt(D)).astype(low_type)
    d_rows = d_rows.reshape(2, groups, piece, D).transpose(1, 0, 2, 3)
    d_rows = jnp.sum(swap_sub(d_rows).astype(jnp.float32), 0).astype(low_type)
    all_rows = gather_tok(d_rows).reshape(-1, D)
    table_grad = table_grad + jnp.einsum(
        "rv,rd->vd", picks, all_rows, preferred_element_type=wide_type
    )
    block_grads = pack(
        grads_enc_self + grads_enc_feed + grads_dec_self + grads_cross + grads_dec_feed
    ).astype(low_type)
    slot_grads = jnp.take(block_grads, slot_block, axis=0, mode="fill", fill_value=0.0)
    vec_grad = jnp.stack(
        gains_one
        + gains_two
        + [g_four, g_five]
        + gains_three
        + gains_four
        + gains_five
        + [g_twelve, g_thirteen],
        0,
    )
    own = scatter_tok(slot_grads.reshape(shards, -1, BLK, BLK)).astype(jnp.float32)
    own, table_grad, vec_grad, loss_sum = lax.psum((own, table_grad, vec_grad, loss_part), "sub")
    square = jnp.sum(own * own) + jnp.sum(table_grad * table_grad)
    small = jnp.concatenate([vec_grad.reshape(-1), jnp.broadcast_to(square, (BLK,))])
    small = jnp.sum(gather_tok(small), 0)
    vec_grad = small[: vec.size].reshape(vec.shape)
    grad_norm = jnp.sqrt(small[vec.size] + jnp.sum(vec_grad * vec_grad))
    scale = jnp.minimum(1.0, clip_limit / grad_norm)
    grad = own * scale
    new_left = beta_stat * left_stat + (1.0 - beta_stat) * jnp.einsum(
        "sij,skj->sik", grad, grad, precision=high
    )
    new_right = beta_stat * right_stat + (1.0 - beta_stat) * jnp.einsum(
        "sji,sjk->sik", grad, grad, precision=high
    )
    new_momentum = beta_one * momentum + (1.0 - beta_one) * grad
    direction = jnp.einsum("sij,sjk->sik", left_root, new_momentum, precision=high)
    direction = jnp.einsum("sik,skl->sil", direction, right_root, precision=high)
    new_master = master - rate_blocks * (direction + decay_rate * master)
    new_table, new_table_m, new_table_v = adamw(
        table, table_grad * scale, table_m, table_v, rate_table
    )
    new_vec, new_vec_m, new_vec_v = adamw(vec, vec_grad * scale, vec_m, vec_v, rate_gains)
    return (
        loss_sum,
        token_count,
        grad_norm,
        new_master,
        new_momentum,
        new_left,
        new_right,
        new_table,
        new_table_m,
        new_table_v,
        new_vec,
        new_vec_m,
        new_vec_v,
    )


def solution(mesh):
    split = Mesh(
        mesh.devices.reshape(mesh.shape["sub"], 4, 4, 2), ("sub", "tok_0", "tok_1", "tok_2")
    )
    placed = (
        P(TOK),
        P(TOK),
        P(TOK),
        P(),
        P(),
        P(),
        P(),
        P(TOK, None, None),
        P(TOK, None, None),
        P(TOK, None, None),
        P(TOK, None, None),
        P(TOK, None, None),
        P(TOK, None, None),
        P(TOK, None),
        P(TOK, None),
        P(TOK, None),
        P(),
        P(),
        P(),
    )
    return jax.shard_map(
        on_device,
        mesh=split,
        in_specs=placed,
        out_specs=(
            P(),
            P(),
            P(),
            P(TOK, None, None),
            P(TOK, None, None),
            P(TOK, None, None),
            P(TOK, None, None),
            P(TOK, None),
            P(TOK, None),
            P(TOK, None),
            P(),
            P(),
            P(),
        ),
        check_vma=False,
    )
```

```python
import functools
import math

import jax
import jax.numpy as jnp
from jax import lax
from jax.experimental import pallas as pl
from jax.experimental.pallas import tpu as pltpu
from jax.sharding import Mesh
from jax.sharding import PartitionSpec as P

D = 640
HEADS = 8
HEAD = 80
FF = 3072
BLK = 128
DOCS = 16
STEP = 10
HALF = 128
NBLK = 780
TOK = ("tok_0", "tok_1", "tok_2")


eps_norm = 1e-05
clip_limit = 0.02
beta_one = 0.9
beta_two = 0.98
beta_stat = 0.95
decay_rate = 0.01
adam_eps = 1e-08
rate_table = 0.05
rate_gains = 0.3
rate_blocks = 0.05
high = lax.Precision.HIGHEST
low_type = jnp.bfloat16
wide_type = jnp.float32


def quarter(value, part, count):
    return lax.dynamic_slice_in_dim(value, part * count, count, 0)


MESH = pl.DeviceIdType.MESH
RING = {"z": "tok_0", "x": "tok_1", "y": "sub"}
CORE = "tok_2"
MIB = 1 << 20


def around(axis):
    count = lax.axis_size(axis)
    me = lax.axis_index(axis)
    return me, lax.rem(me + 1, count), lax.rem(me + count - 1, count), lax.rem(me + 2, count)


def greet(axes):
    barrier = pltpu.get_barrier_semaphore()
    peers = 0
    for axis in axes:
        me = lax.axis_index(axis)
        count = lax.axis_size(axis)
        for k in range(1, count):
            pl.semaphore_signal(
                barrier,
                inc=1,
                device_id={axis: lax.rem(me + k, count)},
                device_id_type=MESH,
            )
        peers += count - 1
    pl.semaphore_wait(barrier, peers)


class Copies:
    def __init__(self, send, recv, local):
        self.send, self.recv, self.local = send, recv, local
        self.sent, self.inside = [], 0

    def push(self, source, target, axis, peer):
        k = len(self.sent)
        copy = pltpu.make_async_remote_copy(
            src_ref=source,
            dst_ref=target,
            send_sem=self.send.at[k],
            recv_sem=self.recv.at[k],
            device_id={axis: peer},
            device_id_type=MESH,
        )
        copy.start()
        self.sent.append(copy)
        return copy

    def move(self, source, target):
        copy = pltpu.make_async_copy(source, target, self.local.at[self.inside])
        self.inside += 1
        copy.start()
        return copy

    def finish(self):
        for copy in self.sent:
            copy.wait_send()


def in_turn(steps):
    steps = list(steps)
    while steps:
        kept = []
        for step in steps:
            try:
                next(step)
                kept.append(step)
            except StopIteration:
                pass
        steps = kept


def rows_of(start, count, half):
    if half is None:
        return start, count
    return start + half * (count // 2), count // 2


def view(ref, lead, rows):
    start, count = rows
    if not isinstance(start, int):
        start = pl.multiple_of(start, 16)
    return ref.at[(*lead, pl.ds(start, count))]


def places(order, stage, rows, by_sub):
    start, count = rows
    axis = order[stage]

    def part(i, half, settled):
        lead = []
        for name in ("z", "x"):
            if name == axis:
                lead.append(i)
            elif (name in order[:stage]) == settled:
                lead.append(slice(None))
            else:
                lead.append(lax.axis_index(RING[name]))
        if not by_sub:
            span = rows_of(start, count, half)
        else:
            piece = count // 4
            if axis == "y":
                span = rows_of(start + i * piece, piece, half)
            elif ("y" in order[:stage]) == settled:
                span = rows_of(start, count, half)
            else:
                span = rows_of(start + lax.axis_index("sub") * piece, piece, half)
        return tuple(lead), span

    return part


def ring_gather(part, axis, copies, arrived):
    me, right, left, far = around(axis)
    first = copies.push(part(me, None), part(me, None), axis, right)
    second = copies.push(part(me, None), part(me, None), axis, left)
    yield
    first.wait_recv()
    third = copies.push(part(left, 0), part(left, 0), axis, right)
    arrived(part(left, None))
    yield
    second.wait_recv()
    fourth = copies.push(part(right, 1), part(right, 1), axis, left)
    arrived(part(right, None))
    yield
    third.wait_recv()
    fourth.wait_recv()
    arrived(part(far, None))
    yield


def gather_kernel(colours, swap, axes, value, *refs):
    if swap:
        out, mine, joined, *refs = refs
    else:
        out, *refs = refs
    copies = Copies(*refs)
    z, x, c = (lax.axis_index(a) for a in ("tok_0", "tok_1", CORE))
    greet(axes)
    if swap:
        me = lax.axis_index("sub")
        piece = value.shape[0] // 4

        def part_of(ref, k):
            return ref.at[pl.ds(pl.multiple_of(k * piece, 16), piece)]

        local = copies.move(part_of(value, me), part_of(mine, me))
        arrivals = [
            copies.push(part_of(value, peer), part_of(mine, me), "sub", peer)
            for peer in (lax.rem(me + k, 4) for k in (1, 3, 2))
        ]
        local.wait()
        for copy in arrivals:
            copy.wait_recv()
        value = mine
        if swap == "sum":
            added = mine[pl.ds(0, piece)].astype(jnp.float32)
            for k in range(1, 4):
                added = added + mine[pl.ds(k * piece, piece)].astype(jnp.float32)
            joined[...] = added.astype(joined.dtype)
            value = joined
    crossing = []

    def arrived(ref):
        crossing.append(copies.push(ref, ref, CORE, 1 - c))

    own = []
    for order, (start, count) in colours:
        if "y" in order:
            count = count // 4
            start = start + lax.axis_index("sub") * count
        own.append(
            (
                view(value, (), (start, count)),
                view(out, (z, x, c), (start, count)),
            )
        )
    for copy in [copies.move(*pair) for pair in own]:
        copy.wait()

    def run(order, rows):
        by_sub = "y" in order
        for stage, name in enumerate(order):
            part = places(order, stage, rows, by_sub)

            def here(i, half, part=part):
                (first, second), span = part(i, half, True)
                return view(out, (first, second, c), span)

            yield from ring_gather(here, RING[name], copies, arrived)

    steps = [run(order, rows) for order, rows in colours]
    for step in steps:
        next(step)
    for _, ref in own:
        arrived(ref)
    in_turn(steps)
    for copy in crossing:
        copy.wait_recv()
    copies.finish()


def semaphores(count, inside):
    return [
        pltpu.SemaphoreType.DMA((count,)),
        pltpu.SemaphoreType.DMA((count,)),
        pltpu.SemaphoreType.DMA((inside,)),
    ]


def gather_tok(value, number, colours, swap=None):
    stages = sum(len(order) for order, _ in colours)
    rows, lanes = value.shape
    scratch = []
    if swap:
        scratch = [pltpu.VMEM((n, lanes), value.dtype) for n in (rows, rows // 4)]
        rows = rows // 4 if swap == "sum" else rows
    axes = (CORE, "tok_0", "tok_1")
    if swap or any("y" in order for order, _ in colours):
        axes += ("sub",)
    return pl.pallas_call(
        functools.partial(gather_kernel, colours, swap, axes),
        out_shape=jax.ShapeDtypeStruct((4, 4, 2, rows, lanes), value.dtype),
        in_specs=[pl.BlockSpec(memory_space=pltpu.HBM)],
        out_specs=pl.BlockSpec(memory_space=pltpu.HBM),
        scratch_shapes=scratch + semaphores(7 * stages + 8, 4),
        compiler_params=pltpu.CompilerParams(
            collective_id=number, has_side_effects=True, vmem_limit_bytes=16 * MIB
        ),
    )(value)


def add_to(target, *sources):
    lead = target.shape[:-2]
    total = math.prod(lead)

    def step(k, carry):
        spot = []
        for size in reversed(lead):
            spot.append(lax.rem(k, size))
            k = lax.div(k, size)
        spot = tuple(reversed(spot))
        value = target[spot]
        for source in sources:
            value = value + source[spot]
        target[spot] = value
        return carry

    if lead:
        lax.fori_loop(0, total, step, 0)
    else:
        value = target[...]
        for source in sources:
            value = value + source[...]
        target[...] = value


def scatter_kernel(colours, ending, value, out, total, other, *refs):
    count = sum(len(order) for order, _ in colours) * 6
    slots, refs = refs[:count], refs[count:]
    if ending != "gather":
        mine, *refs = refs
    copies = Copies(*refs)
    c = lax.axis_index(CORE)
    me_y = lax.axis_index("sub")
    greet((CORE, "tok_0", "tok_1", "sub"))
    pending = {}
    for turn in range(4):
        for k, (order, rows) in enumerate(colours):
            part = places(order, 0, rows, "y" in order)
            i = around(RING[order[0]])[(3, 1, 2, 0)[turn]]
            (first, second), span = part(i, None, False)
            pending[k, turn] = (
                copies.push(
                    view(value, (first, second, 1 - c), span),
                    view(other, (first, second), span),
                    CORE,
                    1 - c,
                ),
                copies.move(
                    view(value, (first, second, c), span), view(total, (first, second), span)
                ),
                view(total, (first, second), span),
                view(other, (first, second), span),
            )

    def ready(k, turn):
        across, inside, ours, theirs = pending[k, turn]
        inside.wait()
        across.wait_recv()
        add_to(ours, theirs)

    def run(k, order, rows):
        at = 6 * sum(len(o) for o, _ in colours[:k])
        for stage, name in enumerate(order):
            part = places(order, stage, rows, "y" in order)
            axis = RING[name]
            me, right, left, far = around(axis)
            r1_in, l1_in, r2_in, l2_in, r3_in, l3_in = slots[at : at + 6]
            at += 6

            def here(i, half, part=part):
                lead, span = part(i, half, False)
                return view(total, lead, span)

            if stage == 0:
                ready(k, 0)
            r1 = copies.push(here(far, 0), r1_in, axis, right)
            l1 = copies.push(here(far, 1), l1_in, axis, left)
            yield
            if stage == 0:
                ready(k, 1)
            r2 = copies.push(here(right, 1), r2_in, axis, right)
            if stage == 0:
                ready(k, 2)
            l2 = copies.push(here(left, 0), l2_in, axis, left)
            yield
            r1.wait_recv()
            add_to(here(right, 0), r1_in)
            r3 = copies.push(here(right, 0), r3_in, axis, right)
            l1.wait_recv()
            add_to(here(left, 1), l1_in)
            l3 = copies.push(here(left, 1), l3_in, axis, left)
            yield
            if stage == 0:
                ready(k, 3)
            l2.wait_recv()
            r2.wait_recv()
            yield
            r3.wait_recv()
            l3.wait_recv()
            last = stage == len(order) - 1
            for half, one, two in ((0, l2_in, r3_in), (1, r2_in, l3_in)):
                if not last:
                    add_to(here(me, half), one, two)
                    continue
                lead, (start, size) = part(me, half, False)
                value = here(me, half)[...].astype(jnp.float32)
                value = value + one[...].astype(jnp.float32) + two[...].astype(jnp.float32)
                if not isinstance(start, int):
                    start = pl.multiple_of(start, 16)
                if ending != "gather":
                    mine[pl.ds(start, size)] = value.astype(mine.dtype)
                else:
                    out[pl.ds(start, size)] = value
            yield
        if ending == "gather":
            start, size = rows
            piece = size // 4

            def held(i, half):
                return view(out, (), rows_of(start + i * piece, piece, half))

            yield from ring_gather(held, "sub", copies, lambda ref: None)

    in_turn([run(k, order, rows) for k, (order, rows) in enumerate(colours)])
    if ending != "gather":
        piece = mine.shape[0] // 4

        def given(peer):
            if ending == "spread":
                return mine
            return mine.at[pl.ds(pl.multiple_of(peer * piece, 16), piece)]

        local = copies.move(given(me_y), out.at[me_y])
        arrivals = [
            copies.push(given(peer), out.at[me_y], "sub", peer)
            for peer in (lax.rem(me_y + k, 4) for k in (1, 3, 2))
        ]
        local.wait()
        for copy in arrivals:
            copy.wait_recv()
    copies.finish()


def scatter_tok(value, number, colours, ending, limit):
    rows, lanes = value.shape[3:]
    slots = []
    for order, (_, size) in colours:
        piece = size // 4 if "y" in order else size
        lead = {"z": 4, "x": 4}
        seen_y = "y" not in order
        for name in order:
            lead.pop(name, None)
            seen_y = seen_y or name == "y"
            height = (piece if seen_y else size) // 2
            slots += [pltpu.VMEM((*lead.values(), height, lanes), value.dtype)] * 6
    stages = len(slots) // 6
    mine = [] if ending == "gather" else [pltpu.VMEM((rows, lanes), value.dtype)]
    shape = {"gather": (rows, lanes), "spread": (4, rows, lanes), "swap": (4, rows // 4, lanes)}
    kind = jnp.float32 if ending == "gather" else value.dtype
    return pl.pallas_call(
        functools.partial(scatter_kernel, colours, ending),
        out_shape=jax.ShapeDtypeStruct(shape[ending], kind),
        in_specs=[pl.BlockSpec(memory_space=pltpu.HBM)],
        out_specs=pl.BlockSpec(memory_space=pltpu.VMEM),
        scratch_shapes=[pltpu.VMEM((4, 4, rows, lanes), value.dtype)] * 2
        + slots
        + mine
        + semaphores(6 * stages + 8 * len(colours) + 4, 4 * len(colours) + 1),
        compiler_params=pltpu.CompilerParams(
            collective_id=number, has_side_effects=True, vmem_limit_bytes=limit
        ),
    )(value)


def added(values):
    total = values[0]
    for value in values[1:]:
        total = total + value
    return total


def merged(values):
    peaks = [value[0:32] for value in values]
    peak = functools.reduce(jnp.maximum, peaks)
    scales = [jnp.exp(p - peak) for p in peaks]
    total = added([value[32:64] * scale for value, scale in zip(values, scales)])
    hit = added([value[64:72] for value in values])
    gaps = [
        added([value[k : k + 8] * scale[0:8] for value, scale in zip(values, scales)])
        for k in (72, 80, 88)
    ]
    return jnp.concatenate([peak, total, hit, *gaps], 0)


def sum_kernel(axes, combine, value, out, *refs):
    slots, (send, recv) = refs[: len(axes)], refs[len(axes) :]
    greet(axes)
    copies = Copies(send, recv, None)
    out[...] = value[...]
    for axis, slot in zip(axes, slots):
        count = lax.axis_size(axis)
        me = lax.axis_index(axis)
        slot[me] = out[...]
        arrivals = [
            copies.push(slot.at[me], slot.at[me], axis, lax.rem(me + k, count))
            for k in range(1, count)
        ]
        for copy in arrivals:
            copy.wait_recv()
        out[...] = combine([slot[k] for k in range(count)])
    copies.finish()


def sum_all(value, number, axes, combine=added):
    counts = [lax.axis_size(axis) for axis in axes]
    sends = sum(counts) - len(axes)
    return pl.pallas_call(
        functools.partial(sum_kernel, axes, combine),
        out_shape=jax.ShapeDtypeStruct(value.shape, value.dtype),
        in_specs=[pl.BlockSpec(memory_space=pltpu.VMEM)],
        out_specs=pl.BlockSpec(memory_space=pltpu.VMEM),
        scratch_shapes=[pltpu.VMEM((n, *value.shape), value.dtype) for n in counts]
        + [pltpu.SemaphoreType.DMA((sends,))] * 2,
        compiler_params=pltpu.CompilerParams(
            collective_id=number, has_side_effects=True, vmem_limit_bytes=16 * MIB
        ),
    )(value)


def push_kernel(axes, value, out, send, recv, local):
    greet(axes)
    copies = Copies(send, recv, local)
    spot = tuple(lax.axis_index(axis) for axis in axes)
    copies.move(value, out.at[spot]).wait()
    for depth in reversed(range(len(axes))):
        axis = axes[depth]
        held = out.at[spot[: depth + 1]]
        arrivals = [
            copies.push(held, held, axis, lax.rem(spot[depth] + k, lax.axis_size(axis)))
            for k in range(1, lax.axis_size(axis))
        ]
        for copy in arrivals:
            copy.wait_recv()
    copies.finish()


def push_all(value, number, axes):
    counts = [lax.axis_size(axis) for axis in axes]
    sends = sum(counts) - len(axes)
    return pl.pallas_call(
        functools.partial(push_kernel, axes),
        out_shape=jax.ShapeDtypeStruct((*counts, *value.shape), value.dtype),
        in_specs=[pl.BlockSpec(memory_space=pltpu.VMEM)],
        out_specs=pl.BlockSpec(memory_space=pltpu.VMEM),
        scratch_shapes=semaphores(sends, 1),
        compiler_params=pltpu.CompilerParams(
            collective_id=number, has_side_effects=True, vmem_limit_bytes=16 * MIB
        ),
    )(value)


def both_ways(rows):
    return ((("z", "x"), (0, rows // 2)), (("x", "z"), (rows // 2, rows // 2)))


def three_ways(first, second, last, orders):
    starts = (0, first, first + second)
    return tuple((o, (s, n)) for o, s, n in zip(orders, starts, (first, second, last)))


WEIGHT_WAYS = three_ways(896, 896, 1408, (("z", "x"), ("x", "z"), ("x", "z", "y")))
GRAD_WAYS = three_ways(1024, 1024, 1152, (("z", "x", "y"), ("x", "y", "z"), ("y", "z", "x")))


def doc_layout(lengths):
    ends = jnp.cumsum(lengths, axis=-1)
    starts = ends - lengths
    place = jnp.arange(HALF, dtype=jnp.int32)
    member = (
        (place[:, None] >= starts[..., None, :]) & (place[:, None] < ends[..., None, :])
    ).astype(jnp.int32)
    inside = jnp.sum(member, -1)
    doc_of = jnp.sum(member * jnp.arange(DOCS, dtype=jnp.int32), -1) + DOCS * (1 - inside)
    offset = place - jnp.sum(member * starts[..., None, :], -1)
    return (doc_of, offset, inside)


def sinusoid(offset):
    half = D // 2
    freq = jnp.exp(jnp.arange(half, dtype=jnp.float32) * (-2.0 * math.log(10000.0) / D))
    angle = offset.astype(jnp.float32)[..., None] * freq
    return jnp.stack([jnp.sin(angle), jnp.cos(angle)], -1).reshape(offset.shape + (D,))


def norm(stream, gain, bias, width, active):
    centre = jnp.sum(stream * width, -1, keepdims=True) / active
    centred = (stream - centre) * width
    spread = jnp.sum(centred * centred, -1, keepdims=True) / active
    return (centred * lax.rsqrt(spread + eps_norm) * gain + bias) * width


def norm_pull(stream, gain, bias, width, active, cotangent):
    _, pull = jax.vjp(
        lambda first, second, third: norm(first, second, third, width, active), stream, gain, bias
    )
    return pull(cotangent)


def layout():
    wide = D // BLK
    deep = FF // BLK
    return [
        (wide, 3 * wide),
        (wide, wide),
        (wide, deep),
        (deep, wide),
        (wide, 3 * wide),
        (wide, wide),
        (wide, wide),
        (wide, 2 * wide),
        (wide, wide),
        (wide, deep),
        (deep, wide),
    ]


def unpack(blocks):
    result = []
    start = 0
    for rows, cols in layout():
        part = blocks[start : start + rows * cols]
        start = start + rows * cols
        result.append(
            part.reshape(rows, cols, BLK, BLK).transpose(0, 2, 1, 3).reshape(rows * BLK, cols * BLK)
        )
    return result


def pack(matrices):
    pieces = []
    for matrix in matrices:
        rows = matrix.shape[0] // BLK
        cols = matrix.shape[1] // BLK
        pieces.append(
            matrix.reshape(rows, BLK, cols, BLK)
            .transpose(0, 2, 1, 3)
            .reshape(rows * cols, BLK, BLK)
        )
    return jnp.concatenate(pieces, 0)


def matmul(left, right):
    return jnp.dot(left, right, preferred_element_type=wide_type)


def attend(query, keys, values, allowed, head_keep):
    scores = jnp.einsum("qhc,khc->hqk", query, keys, preferred_element_type=wide_type) * HEAD ** (
        -0.5
    )
    scores = jnp.where(allowed[None], scores, -1e30)
    peak = jnp.max(scores, -1, keepdims=True)
    expo = jnp.exp(scores - peak)
    probs = expo / jnp.sum(expo, -1, keepdims=True)
    probs_low = probs.astype(low_type)
    mixed = jnp.einsum("hqk,khc->qhc", probs_low, values, preferred_element_type=wide_type)
    mixed = (mixed * head_keep[:, None]).reshape(query.shape[0], D).astype(low_type)
    return (mixed, (query, keys, values, probs, probs_low))


def attend_back(d_rows, inner, head_keep):
    query, keys, values, probs, probs_low = inner
    d_mixed = (d_rows.reshape(query.shape) * head_keep[:, None]).astype(low_type)
    g_probs = jnp.einsum("qhc,khc->hqk", d_mixed, values, preferred_element_type=wide_type)
    d_values = jnp.einsum("hqk,qhc->khc", probs_low, d_mixed, preferred_element_type=wide_type)
    d_scores = (probs * (g_probs - jnp.sum(probs * g_probs, -1, keepdims=True))).astype(low_type)
    scale = HEAD ** (-0.5)
    d_query = jnp.einsum("hqk,khc->qhc", d_scores, keys, preferred_element_type=wide_type) * scale
    d_keys = jnp.einsum("hqk,qhc->khc", d_scores, query, preferred_element_type=wide_type) * scale
    return (d_query, d_keys, d_values)


def branch_back(d_out, inputs, w_out, width):
    d_branch = (d_out * width).astype(low_type)
    g_out = jnp.einsum("td,te->de", inputs, d_branch, preferred_element_type=wide_type)
    d_inputs = jnp.einsum("te,de->td", d_branch, w_out, preferred_element_type=wide_type)
    return (g_out, d_inputs)


def self_block(stream, gain, bias, w_qkv, w_out, masks, allowed):
    width, active, head_keep, unit_keep = masks
    span = stream.shape[0]
    normed = norm(stream, gain, bias, width, active).astype(low_type)
    packed = matmul(normed, w_qkv).astype(low_type).reshape(span, 3, HEADS, HEAD)
    mixed, inner = attend(packed[:, 0], packed[:, 1], packed[:, 2], allowed, head_keep)
    return (stream + matmul(mixed, w_out) * width, (stream, normed, mixed, inner))


def self_back(d_out, kept, gain, bias, w_qkv, w_out, masks):
    width, active, head_keep, unit_keep = masks
    stream, normed, mixed, inner = kept
    span = stream.shape[0]
    g_out, d_mixed = branch_back(d_out, mixed, w_out, width)
    d_query, d_keys, d_values = attend_back(d_mixed, inner, head_keep)
    d_packed = jnp.stack([d_query, d_keys, d_values], 1).reshape(span, 3 * D).astype(low_type)
    g_qkv = jnp.einsum("td,te->de", normed, d_packed, preferred_element_type=wide_type)
    d_first = jnp.einsum("te,de->td", d_packed, w_qkv, preferred_element_type=wide_type)
    d_in, g_gain, g_bias = norm_pull(stream, gain, bias, width, active, d_first)
    return (d_out + d_in, [g_qkv, g_out], [g_gain, g_bias])


def cross_block(stream, memory, gain, bias, w_query, w_pair, w_out, masks, allowed):
    width, active, head_keep, unit_keep = masks
    span = stream.shape[0]
    normed = norm(stream, gain, bias, width, active).astype(low_type)
    query = matmul(normed, w_query).astype(low_type).reshape(span, HEADS, HEAD)
    paired = matmul(memory, w_pair).astype(low_type).reshape(memory.shape[0], 2, HEADS, HEAD)
    mixed, inner = attend(query, paired[:, 0], paired[:, 1], allowed, head_keep)
    return (stream + matmul(mixed, w_out) * width, (stream, normed, mixed, inner))


def cross_back(d_out, kept, memory, gain, bias, w_query, w_pair, w_out, masks):
    width, active, head_keep, unit_keep = masks
    stream, normed, mixed, inner = kept
    span = stream.shape[0]
    g_out, d_mixed = branch_back(d_out, mixed, w_out, width)
    d_query, d_keys, d_values = attend_back(d_mixed, inner, head_keep)
    d_query = d_query.reshape(span, D).astype(low_type)
    d_pair = jnp.stack([d_keys, d_values], 1).reshape(memory.shape[0], 2 * D).astype(low_type)
    g_query = jnp.einsum("td,te->de", normed, d_query, preferred_element_type=wide_type)
    g_pair = jnp.einsum("td,te->de", memory, d_pair, preferred_element_type=wide_type)
    d_memory = jnp.einsum("te,de->td", d_pair, w_pair, preferred_element_type=wide_type)
    d_first = jnp.einsum("te,de->td", d_query, w_query, preferred_element_type=wide_type)
    d_in, g_gain, g_bias = norm_pull(stream, gain, bias, width, active, d_first)
    return (d_out + d_in, d_memory, [g_query, g_pair, g_out], [g_gain, g_bias])


def feed_block(stream, gain, bias, w_up, w_down, masks):
    width, active, head_keep, unit_keep = masks
    normed = norm(stream, gain, bias, width, active).astype(low_type)
    hidden_pre = matmul(normed, w_up)
    activated = (jax.nn.gelu(hidden_pre) * unit_keep).astype(low_type)
    return (stream + matmul(activated, w_down) * width, (stream, normed, hidden_pre, activated))


def feed_back(d_out, kept, gain, bias, w_up, w_down, masks):
    width, active, head_keep, unit_keep = masks
    stream, normed, hidden_pre, activated = kept
    g_down, d_act = branch_back(d_out, activated, w_down, width)
    _, gelu_pull = jax.vjp(jax.nn.gelu, hidden_pre)
    d_pre = gelu_pull(d_act * unit_keep)[0].astype(low_type)
    g_up = jnp.einsum("td,tf->df", normed, d_pre, preferred_element_type=wide_type)
    d_normed = jnp.einsum("tf,df->td", d_pre, w_up, preferred_element_type=wide_type)
    d_in, g_gain, g_bias = norm_pull(stream, gain, bias, width, active, d_normed)
    return (d_out + d_in, [g_up, g_down], [g_gain, g_bias])


def adamw(param, grad, first, second, rate):
    first = beta_one * first + (1.0 - beta_one) * grad
    second = beta_two * second + (1.0 - beta_two) * grad * grad
    fixed_first = first / (1.0 - beta_one**STEP)
    fixed_second = second / (1.0 - beta_two**STEP)
    return (
        param - rate * (fixed_first / (jnp.sqrt(fixed_second) + adam_eps) + decay_rate * param),
        first,
        second,
    )


def on_device(
    token_ids,
    target_ids,
    doc_lengths,
    width_tiles,
    head_mask,
    ffn_tiles,
    slot_block,
    master,
    momentum,
    left_stat,
    right_stat,
    left_root,
    right_root,
    table,
    table_m,
    table_v,
    vec,
    vec_m,
    vec_v,
):
    group = lax.axis_index("sub")
    place = lax.axis_index(TOK)
    groups = lax.axis_size("sub")
    shards = lax.axis_size(TOK)
    shard_rows = table.shape[0]
    piece = HALF // groups
    doc_of, offset, inside = doc_layout(doc_lengths)
    mine = jnp.concatenate(
        [
            quarter(token_ids[:HALF], group, piece),
            quarter(token_ids[HALF:], group, piece),
            quarter(jnp.where(inside > 0, target_ids, -1), group, piece),
            jnp.broadcast_to(jnp.sum(inside), (HALF - 3 * piece,)),
        ]
    )
    table_low = table.astype(low_type)
    heads_up = push_all(mine.reshape(1, HALF), 1, TOK).reshape(shards, HALF)
    slots = gather_tok(master.astype(low_type).reshape(-1, BLK), 2, WEIGHT_WAYS)
    slots = slots.reshape(-1, BLK, BLK)
    all_targets = heads_up[:, 2 * piece : 3 * piece]
    weight = (all_targets >= 0).astype(jnp.float32)
    token_count = jnp.sum(heads_up[:, 3 * piece]).astype(jnp.float32)
    first_row = place * shard_rows
    local = (heads_up[:, : 2 * piece] - first_row).reshape(-1)
    picks = (local[:, None] == jnp.arange(shard_rows, dtype=jnp.int32)).astype(low_type)
    picked = matmul(picks, table_low).astype(low_type).reshape(4, 4, 2, 2 * piece, D)
    rows = scatter_tok(picked, 3, both_ways(2 * piece), "spread", 32 * MIB).astype(jnp.float32)
    rows = rows.reshape(groups, 2, piece, D).transpose(1, 0, 2, 3).reshape(2, HALF, D)
    inverse = jnp.sum(
        jnp.where(
            slot_block[None, :] == jnp.arange(NBLK, dtype=jnp.int32)[:, None],
            jnp.arange(slot_block.shape[0], dtype=jnp.int32)[None, :],
            0,
        ),
        1,
    )
    mats = lax.optimization_barrier(unpack(slots[inverse]))
    width = jnp.repeat(width_tiles[group], BLK).astype(jnp.float32)
    active = jnp.sum(width)
    head_keep = head_mask[group].astype(jnp.float32)
    unit_keep = jnp.repeat(ffn_tiles[group], BLK).astype(jnp.float32)
    masks = (width, active, head_keep, unit_keep)
    wave = sinusoid(offset)
    source = (math.sqrt(D) * rows[0] + wave) * width
    target = (math.sqrt(D) * rows[1] + wave) * width
    same = doc_of[:, None] == doc_of[None, :]
    causal = same & (offset[None, :] <= offset[:, None])
    enc_one, kept_one = self_block(source, vec[0], vec[1], mats[0], mats[1], masks, same)
    enc_two, kept_two = feed_block(enc_one, vec[2], vec[3], mats[2], mats[3], masks)
    memory = norm(enc_two, vec[4], vec[5], width, active).astype(low_type)
    dec_one, kept_three = self_block(target, vec[6], vec[7], mats[4], mats[5], masks, causal)
    dec_two, kept_four = cross_block(
        dec_one, memory, vec[8], vec[9], mats[6], mats[7], mats[8], masks, same
    )
    dec_three, kept_five = feed_block(dec_two, vec[10], vec[11], mats[9], mats[10], masks)
    final = norm(dec_three, vec[12], vec[13], width, active).astype(low_type)
    hidden = gather_tok(final, 4, both_ways(HALF), "rows").reshape(-1, D)
    logits = jnp.einsum("td,vd->tv", hidden, table_low, preferred_element_type=wide_type)
    logits = logits.reshape(shards, groups, piece, shard_rows)
    teacher = logits[:, :1]
    peak = jnp.max(logits, -1)
    total = jnp.sum(jnp.exp(logits - peak[..., None]), -1)
    hits = all_targets[..., None] - first_row == jnp.arange(shard_rows, dtype=jnp.int32)
    hit = jnp.sum(jnp.where(hits, logits[:, 0], 0.0), -1)
    gap = jnp.sum(jnp.exp(teacher - peak[:, :1, :, None]) * (teacher - logits[:, 1:]), -1)
    stats = jnp.concatenate([peak, total, hit[:, None], gap], 1).transpose(1, 0, 2)
    stats = sum_all(stats.reshape(-1, BLK), 5, TOK[::-1], merged)
    stats = stats.reshape(-1, shards, piece).transpose(1, 0, 2)
    logs = stats[:, :groups] + jnp.log(stats[:, groups : 2 * groups])
    hit = stats[:, 2 * groups]
    gap = stats[:, 2 * groups + 1 :] / stats[:, groups : groups + 1]
    token_loss = logs[:, 0] - hit + jnp.sum(logs[:, 1:] + gap - logs[:, :1], 1)
    loss_part = jnp.sum(token_loss * weight)
    target_dist = jnp.concatenate(
        [
            hits.astype(jnp.float32)[:, None],
            jnp.broadcast_to(
                jnp.exp(teacher - logs[:, :1, :, None]),
                (shards, groups - 1, piece, shard_rows),
            ),
        ],
        1,
    )
    back = (jnp.exp(logits - logs[..., None]) - target_dist) * (weight / token_count)[
        :, None, :, None
    ]
    back = back.astype(low_type).reshape(-1, shard_rows)
    d_hidden = matmul(back, table_low).astype(low_type).reshape(4, 4, 2, groups * piece, D)
    d_final = scatter_tok(d_hidden, 6, both_ways(HALF), "swap", 32 * MIB)
    d_final = d_final.reshape(HALF, D).astype(jnp.float32)
    table_grad = jnp.einsum("tv,td->vd", back, hidden, preferred_element_type=wide_type)
    d_three, g_twelve, g_thirteen = norm_pull(dec_three, vec[12], vec[13], width, active, d_final)
    d_two, grads_dec_feed, gains_five = feed_back(
        d_three, kept_five, vec[10], vec[11], mats[9], mats[10], masks
    )
    d_one, d_memory, grads_cross, gains_four = cross_back(
        d_two, kept_four, memory, vec[8], vec[9], mats[6], mats[7], mats[8], masks
    )
    d_target, grads_dec_self, gains_three = self_back(
        d_one, kept_three, vec[6], vec[7], mats[4], mats[5], masks
    )
    d_enc_two, g_four, g_five = norm_pull(enc_two, vec[4], vec[5], width, active, d_memory)
    d_enc_one, grads_enc_feed, gains_two = feed_back(
        d_enc_two, kept_two, vec[2], vec[3], mats[2], mats[3], masks
    )
    d_source, grads_enc_self, gains_one = self_back(
        d_enc_one, kept_one, vec[0], vec[1], mats[0], mats[1], masks
    )
    d_rows = (jnp.stack([d_source, d_target], 0) * width * math.sqrt(D)).astype(low_type)
    d_rows = d_rows.reshape(2, groups, piece, D).transpose(1, 0, 2, 3)
    all_rows = gather_tok(d_rows.reshape(-1, D), 7, both_ways(2 * piece), "sum").reshape(-1, D)
    table_grad = table_grad + jnp.einsum(
        "rv,rd->vd", picks, all_rows, preferred_element_type=wide_type
    )
    block_grads = pack(
        grads_enc_self + grads_enc_feed + grads_dec_self + grads_cross + grads_dec_feed
    ).astype(low_type)
    slot_grads = jnp.take(block_grads, slot_block, axis=0, mode="fill", fill_value=0.0)
    vec_grad = jnp.stack(
        gains_one
        + gains_two
        + [g_four, g_five]
        + gains_three
        + gains_four
        + gains_five
        + [g_twelve, g_thirteen],
        0,
    )
    table_grad = lax.psum(table_grad, "sub")
    own = scatter_tok(
        slot_grads.reshape(4, 4, 2, -1, BLK), 8, GRAD_WAYS, "gather", 60 * MIB
    ).reshape(master.shape)
    square = jnp.sum(own * own) + jnp.sum(table_grad * table_grad)
    small = jnp.concatenate(
        [
            vec_grad.reshape(-1),
            jnp.broadcast_to(square / groups, (BLK,)),
            jnp.broadcast_to(loss_part / shards, (BLK,)),
        ]
    )
    small = sum_all(small.reshape(-1, BLK), 9, (*TOK[::-1], "sub")).reshape(-1)
    vec_grad = small[: vec.size].reshape(vec.shape)
    loss_sum = small[vec.size + BLK]
    grad_norm = jnp.sqrt(small[vec.size] + jnp.sum(vec_grad * vec_grad))
    scale = jnp.minimum(1.0, clip_limit / grad_norm)
    grad = own * scale
    new_left = beta_stat * left_stat + (1.0 - beta_stat) * jnp.einsum(
        "sij,skj->sik", grad, grad, precision=high
    )
    new_right = beta_stat * right_stat + (1.0 - beta_stat) * jnp.einsum(
        "sji,sjk->sik", grad, grad, precision=high
    )
    new_momentum = beta_one * momentum + (1.0 - beta_one) * grad
    direction = jnp.einsum("sij,sjk->sik", left_root, new_momentum, precision=high)
    direction = jnp.einsum("sik,skl->sil", direction, right_root, precision=high)
    new_master = master - rate_blocks * (direction + decay_rate * master)
    new_table, new_table_m, new_table_v = adamw(
        table, table_grad * scale, table_m, table_v, rate_table
    )
    new_vec, new_vec_m, new_vec_v = adamw(vec, vec_grad * scale, vec_m, vec_v, rate_gains)
    return (
        loss_sum,
        token_count,
        grad_norm,
        new_master,
        new_momentum,
        new_left,
        new_right,
        new_table,
        new_table_m,
        new_table_v,
        new_vec,
        new_vec_m,
        new_vec_v,
    )


def solution(mesh):
    split = Mesh(
        mesh.devices.reshape(mesh.shape["sub"], 4, 4, 2), ("sub", "tok_0", "tok_1", "tok_2")
    )
    placed = (
        P(TOK),
        P(TOK),
        P(TOK),
        P(),
        P(),
        P(),
        P(),
        P(TOK, None, None),
        P(TOK, None, None),
        P(TOK, None, None),
        P(TOK, None, None),
        P(TOK, None, None),
        P(TOK, None, None),
        P(TOK, None),
        P(TOK, None),
        P(TOK, None),
        P(),
        P(),
        P(),
    )
    return jax.shard_map(
        on_device,
        mesh=split,
        in_specs=placed,
        out_specs=(
            P(),
            P(),
            P(),
            P(TOK, None, None),
            P(TOK, None, None),
            P(TOK, None, None),
            P(TOK, None, None),
            P(TOK, None),
            P(TOK, None),
            P(TOK, None),
            P(),
            P(),
            P(),
        ),
        check_vma=False,
    )
```

```python
import functools
import math

import jax
import jax.numpy as jnp
from jax import lax
from jax.experimental import pallas as pl
from jax.experimental.pallas import tpu as pltpu
from jax.sharding import Mesh
from jax.sharding import PartitionSpec as P

D = 640
HEADS = 8
HEAD = 80
FF = 3072
BLK = 128
DOCS = 16
STEP = 10
HALF = 128
NBLK = 780
TOK = ("tok_0", "tok_1", "tok_2")


eps_norm = 1e-05
clip_limit = 0.02
beta_one = 0.9
beta_two = 0.98
beta_stat = 0.95
decay_rate = 0.01
adam_eps = 1e-08
rate_table = 0.05
rate_gains = 0.3
rate_blocks = 0.05
high = lax.Precision.HIGHEST
low_type = jnp.bfloat16
wide_type = jnp.float32


def quarter(value, part, count):
    return lax.dynamic_slice_in_dim(value, part * count, count, 0)


MESH = pl.DeviceIdType.MESH
RING = {"z": "tok_0", "x": "tok_1", "y": "sub"}
CORE = "tok_2"
MIB = 1 << 20


def around(axis):
    count = lax.axis_size(axis)
    me = lax.axis_index(axis)
    return me, lax.rem(me + 1, count), lax.rem(me + count - 1, count), lax.rem(me + 2, count)


def greet(axes):
    barrier = pltpu.get_barrier_semaphore()
    peers = 0
    for axis in axes:
        me = lax.axis_index(axis)
        count = lax.axis_size(axis)
        for k in range(1, count):
            pl.semaphore_signal(
                barrier,
                inc=1,
                device_id={axis: lax.rem(me + k, count)},
                device_id_type=MESH,
            )
        peers += count - 1
    pl.semaphore_wait(barrier, peers)


class Copies:
    def __init__(self, send, recv, local):
        self.send, self.recv, self.local = send, recv, local
        self.sent, self.inside = [], 0

    def push(self, source, target, axis, peer):
        k = len(self.sent)
        copy = pltpu.make_async_remote_copy(
            src_ref=source,
            dst_ref=target,
            send_sem=self.send.at[k],
            recv_sem=self.recv.at[k],
            device_id={axis: peer},
            device_id_type=MESH,
        )
        copy.start()
        self.sent.append(copy)
        return copy

    def move(self, source, target):
        copy = pltpu.make_async_copy(source, target, self.local.at[self.inside])
        self.inside += 1
        copy.start()
        return copy

    def finish(self):
        for copy in self.sent:
            copy.wait_send()


def in_turn(steps):
    steps = list(steps)
    while steps:
        kept = []
        for step in steps:
            try:
                next(step)
                kept.append(step)
            except StopIteration:
                pass
        steps = kept


def rows_of(start, count, half):
    if half is None:
        return start, count
    return start + half * (count // 2), count // 2


def view(ref, lead, rows):
    start, count = rows
    if not isinstance(start, int):
        start = pl.multiple_of(start, 16)
    return ref.at[(*lead, pl.ds(start, count))]


def places(order, stage, rows, by_sub):
    start, count = rows
    axis = order[stage]

    def part(i, half, settled):
        lead = []
        for name in ("z", "x"):
            if name == axis:
                lead.append(i)
            elif (name in order[:stage]) == settled:
                lead.append(slice(None))
            else:
                lead.append(lax.axis_index(RING[name]))
        if not by_sub:
            span = rows_of(start, count, half)
        else:
            piece = count // 4
            if axis == "y":
                span = rows_of(start + i * piece, piece, half)
            elif ("y" in order[:stage]) == settled:
                span = rows_of(start, count, half)
            else:
                span = rows_of(start + lax.axis_index("sub") * piece, piece, half)
        return tuple(lead), span

    return part


def ring_gather(part, axis, copies, arrived):
    me, right, left, far = around(axis)
    first = copies.push(part(me, None), part(me, None), axis, right)
    second = copies.push(part(me, None), part(me, None), axis, left)
    yield
    first.wait_recv()
    third = copies.push(part(left, 0), part(left, 0), axis, right)
    arrived(part(left, None))
    yield
    second.wait_recv()
    fourth = copies.push(part(right, 1), part(right, 1), axis, left)
    arrived(part(right, None))
    yield
    third.wait_recv()
    fourth.wait_recv()
    arrived(part(far, None))
    yield


def gather_kernel(colours, swap, axes, value, *refs):
    if swap:
        out, mine, joined, *refs = refs
    else:
        out, *refs = refs
    copies = Copies(*refs)
    z, x, c = (lax.axis_index(a) for a in ("tok_0", "tok_1", CORE))
    greet(axes)
    if swap:
        me = lax.axis_index("sub")
        piece = value.shape[0] // 4

        def part_of(ref, k):
            return ref.at[pl.ds(pl.multiple_of(k * piece, 16), piece)]

        local = copies.move(part_of(value, me), part_of(mine, me))
        arrivals = [
            copies.push(part_of(value, peer), part_of(mine, me), "sub", peer)
            for peer in (lax.rem(me + k, 4) for k in (1, 3, 2))
        ]
        local.wait()
        for copy in arrivals:
            copy.wait_recv()
        value = mine
        if swap == "sum":
            added = mine[pl.ds(0, piece)].astype(jnp.float32)
            for k in range(1, 4):
                added = added + mine[pl.ds(k * piece, piece)].astype(jnp.float32)
            joined[...] = added.astype(joined.dtype)
            value = joined
    crossing = []

    def arrived(ref):
        crossing.append(copies.push(ref, ref, CORE, 1 - c))

    own = []
    for order, (start, count) in colours:
        if "y" in order:
            count = count // 4
            start = start + lax.axis_index("sub") * count
        own.append(
            (
                view(value, (), (start, count)),
                view(out, (z, x, c), (start, count)),
            )
        )
    for copy in [copies.move(*pair) for pair in own]:
        copy.wait()

    def run(order, rows):
        by_sub = "y" in order
        for stage, name in enumerate(order):
            part = places(order, stage, rows, by_sub)

            def here(i, half, part=part):
                (first, second), span = part(i, half, True)
                return view(out, (first, second, c), span)

            yield from ring_gather(here, RING[name], copies, arrived)

    steps = [run(order, rows) for order, rows in colours]
    for step in steps:
        next(step)
    for _, ref in own:
        arrived(ref)
    in_turn(steps)
    for copy in crossing:
        copy.wait_recv()
    copies.finish()


def semaphores(count, inside):
    return [
        pltpu.SemaphoreType.DMA((count,)),
        pltpu.SemaphoreType.DMA((count,)),
        pltpu.SemaphoreType.DMA((inside,)),
    ]


def gather_tok(value, number, colours, swap=None):
    stages = sum(len(order) for order, _ in colours)
    rows, lanes = value.shape
    scratch = []
    if swap:
        scratch = [pltpu.VMEM((n, lanes), value.dtype) for n in (rows, rows // 4)]
        rows = rows // 4 if swap == "sum" else rows
    axes = (CORE, "tok_0", "tok_1")
    if swap or any("y" in order for order, _ in colours):
        axes += ("sub",)
    return pl.pallas_call(
        functools.partial(gather_kernel, colours, swap, axes),
        out_shape=jax.ShapeDtypeStruct((4, 4, 2, rows, lanes), value.dtype),
        in_specs=[pl.BlockSpec(memory_space=pltpu.HBM)],
        out_specs=pl.BlockSpec(memory_space=pltpu.HBM),
        scratch_shapes=scratch + semaphores(7 * stages + 8, 4),
        compiler_params=pltpu.CompilerParams(
            collective_id=number, has_side_effects=True, vmem_limit_bytes=16 * MIB
        ),
    )(value)


def add_to(target, *sources):
    lead = target.shape[:-2]
    total = math.prod(lead)

    def step(k, carry):
        spot = []
        for size in reversed(lead):
            spot.append(lax.rem(k, size))
            k = lax.div(k, size)
        spot = tuple(reversed(spot))
        value = target[spot]
        for source in sources:
            value = value + source[spot]
        target[spot] = value
        return carry

    if lead:
        lax.fori_loop(0, total, step, 0)
    else:
        value = target[...]
        for source in sources:
            value = value + source[...]
        target[...] = value


def scatter_kernel(colours, ending, value, out, total, other, *refs):
    count = sum(len(order) for order, _ in colours) * 6
    slots, refs = refs[:count], refs[count:]
    if ending != "gather":
        mine, *refs = refs
    copies = Copies(*refs)
    c = lax.axis_index(CORE)
    me_y = lax.axis_index("sub")
    greet((CORE, "tok_0", "tok_1", "sub"))
    pending = {}
    for turn in range(4):
        for k, (order, rows) in enumerate(colours):
            part = places(order, 0, rows, "y" in order)
            i = around(RING[order[0]])[(3, 1, 2, 0)[turn]]
            (first, second), span = part(i, None, False)
            pending[k, turn] = (
                copies.push(
                    view(value, (first, second, 1 - c), span),
                    view(other, (first, second), span),
                    CORE,
                    1 - c,
                ),
                copies.move(
                    view(value, (first, second, c), span), view(total, (first, second), span)
                ),
                view(total, (first, second), span),
                view(other, (first, second), span),
            )

    def ready(k, turn):
        across, inside, ours, theirs = pending[k, turn]
        inside.wait()
        across.wait_recv()
        add_to(ours, theirs)

    def run(k, order, rows):
        at = 6 * sum(len(o) for o, _ in colours[:k])
        for stage, name in enumerate(order):
            part = places(order, stage, rows, "y" in order)
            axis = RING[name]
            me, right, left, far = around(axis)
            r1_in, l1_in, r2_in, l2_in, r3_in, l3_in = slots[at : at + 6]
            at += 6

            def here(i, half, part=part):
                lead, span = part(i, half, False)
                return view(total, lead, span)

            if stage == 0:
                ready(k, 0)
            r1 = copies.push(here(far, 0), r1_in, axis, right)
            l1 = copies.push(here(far, 1), l1_in, axis, left)
            yield
            if stage == 0:
                ready(k, 1)
            r2 = copies.push(here(right, 1), r2_in, axis, right)
            if stage == 0:
                ready(k, 2)
            l2 = copies.push(here(left, 0), l2_in, axis, left)
            yield
            r1.wait_recv()
            add_to(here(right, 0), r1_in)
            r3 = copies.push(here(right, 0), r3_in, axis, right)
            l1.wait_recv()
            add_to(here(left, 1), l1_in)
            l3 = copies.push(here(left, 1), l3_in, axis, left)
            yield
            if stage == 0:
                ready(k, 3)
            l2.wait_recv()
            r2.wait_recv()
            yield
            r3.wait_recv()
            l3.wait_recv()
            last = stage == len(order) - 1
            for half, one, two in ((0, l2_in, r3_in), (1, r2_in, l3_in)):
                if not last:
                    add_to(here(me, half), one, two)
                    continue
                lead, (start, size) = part(me, half, False)
                value = here(me, half)[...].astype(jnp.float32)
                value = value + one[...].astype(jnp.float32) + two[...].astype(jnp.float32)
                if not isinstance(start, int):
                    start = pl.multiple_of(start, 16)
                if ending != "gather":
                    mine[pl.ds(start, size)] = value.astype(mine.dtype)
                else:
                    out[pl.ds(start, size)] = value
            yield
        if ending == "gather":
            start, size = rows
            piece = size // 4

            def held(i, half):
                return view(out, (), rows_of(start + i * piece, piece, half))

            yield from ring_gather(held, "sub", copies, lambda ref: None)

    in_turn([run(k, order, rows) for k, (order, rows) in enumerate(colours)])
    if ending != "gather":
        piece = mine.shape[0] // 4

        def given(peer):
            if ending == "spread":
                return mine
            return mine.at[pl.ds(pl.multiple_of(peer * piece, 16), piece)]

        local = copies.move(given(me_y), out.at[me_y])
        arrivals = [
            copies.push(given(peer), out.at[me_y], "sub", peer)
            for peer in (lax.rem(me_y + k, 4) for k in (1, 3, 2))
        ]
        local.wait()
        for copy in arrivals:
            copy.wait_recv()
    copies.finish()


def scatter_tok(value, number, colours, ending, limit):
    rows, lanes = value.shape[3:]
    slots = []
    for order, (_, size) in colours:
        piece = size // 4 if "y" in order else size
        lead = {"z": 4, "x": 4}
        seen_y = "y" not in order
        for name in order:
            lead.pop(name, None)
            seen_y = seen_y or name == "y"
            height = (piece if seen_y else size) // 2
            slots += [pltpu.VMEM((*lead.values(), height, lanes), value.dtype)] * 6
    stages = len(slots) // 6
    mine = [] if ending == "gather" else [pltpu.VMEM((rows, lanes), value.dtype)]
    shape = {"gather": (rows, lanes), "spread": (4, rows, lanes), "swap": (4, rows // 4, lanes)}
    kind = jnp.float32 if ending == "gather" else value.dtype
    return pl.pallas_call(
        functools.partial(scatter_kernel, colours, ending),
        out_shape=jax.ShapeDtypeStruct(shape[ending], kind),
        in_specs=[pl.BlockSpec(memory_space=pltpu.HBM)],
        out_specs=pl.BlockSpec(memory_space=pltpu.VMEM),
        scratch_shapes=[pltpu.VMEM((4, 4, rows, lanes), value.dtype)] * 2
        + slots
        + mine
        + semaphores(6 * stages + 8 * len(colours) + 4, 4 * len(colours) + 1),
        compiler_params=pltpu.CompilerParams(
            collective_id=number, has_side_effects=True, vmem_limit_bytes=limit
        ),
    )(value)


def added(values):
    total = values[0]
    for value in values[1:]:
        total = total + value
    return total


def merged(values):
    peaks = [value[0:32] for value in values]
    peak = functools.reduce(jnp.maximum, peaks)
    scales = [jnp.exp(p - peak) for p in peaks]
    total = added([value[32:64] * scale for value, scale in zip(values, scales)])
    hit = added([value[64:72] for value in values])
    gaps = [
        added([value[k : k + 8] * scale[0:8] for value, scale in zip(values, scales)])
        for k in (72, 80, 88)
    ]
    return jnp.concatenate([peak, total, hit, *gaps], 0)


def sum_kernel(axes, combine, value, out, *refs):
    slots, (send, recv) = refs[: len(axes)], refs[len(axes) :]
    greet(axes)
    copies = Copies(send, recv, None)
    out[...] = value[...]
    for axis, slot in zip(axes, slots):
        count = lax.axis_size(axis)
        me = lax.axis_index(axis)
        slot[me] = out[...]
        arrivals = [
            copies.push(slot.at[me], slot.at[me], axis, lax.rem(me + k, count))
            for k in range(1, count)
        ]
        for copy in arrivals:
            copy.wait_recv()
        out[...] = combine([slot[k] for k in range(count)])
    copies.finish()


def sum_all(value, number, axes, combine=added):
    counts = [lax.axis_size(axis) for axis in axes]
    sends = sum(counts) - len(axes)
    return pl.pallas_call(
        functools.partial(sum_kernel, axes, combine),
        out_shape=jax.ShapeDtypeStruct(value.shape, value.dtype),
        in_specs=[pl.BlockSpec(memory_space=pltpu.VMEM)],
        out_specs=pl.BlockSpec(memory_space=pltpu.VMEM),
        scratch_shapes=[pltpu.VMEM((n, *value.shape), value.dtype) for n in counts]
        + [pltpu.SemaphoreType.DMA((sends,))] * 2,
        compiler_params=pltpu.CompilerParams(
            collective_id=number, has_side_effects=True, vmem_limit_bytes=16 * MIB
        ),
    )(value)


def push_kernel(axes, value, out, send, recv, local):
    greet(axes)
    copies = Copies(send, recv, local)
    spot = tuple(lax.axis_index(axis) for axis in axes)
    copies.move(value, out.at[spot]).wait()
    for depth in reversed(range(len(axes))):
        axis = axes[depth]
        held = out.at[spot[: depth + 1]]
        arrivals = [
            copies.push(held, held, axis, lax.rem(spot[depth] + k, lax.axis_size(axis)))
            for k in range(1, lax.axis_size(axis))
        ]
        for copy in arrivals:
            copy.wait_recv()
    copies.finish()


def push_all(value, number, axes):
    counts = [lax.axis_size(axis) for axis in axes]
    sends = sum(counts) - len(axes)
    return pl.pallas_call(
        functools.partial(push_kernel, axes),
        out_shape=jax.ShapeDtypeStruct((*counts, *value.shape), value.dtype),
        in_specs=[pl.BlockSpec(memory_space=pltpu.VMEM)],
        out_specs=pl.BlockSpec(memory_space=pltpu.VMEM),
        scratch_shapes=semaphores(sends, 1),
        compiler_params=pltpu.CompilerParams(
            collective_id=number, has_side_effects=True, vmem_limit_bytes=16 * MIB
        ),
    )(value)


def both_ways(rows):
    return ((("z", "x"), (0, rows // 2)), (("x", "z"), (rows // 2, rows // 2)))


def three_ways(first, second, last, orders):
    starts = (0, first, first + second)
    return tuple((o, (s, n)) for o, s, n in zip(orders, starts, (first, second, last)))


WEIGHT_WAYS = three_ways(896, 896, 1408, (("z", "x"), ("x", "z"), ("x", "z", "y")))
GRAD_WAYS = three_ways(1024, 1024, 1152, (("z", "x", "y"), ("x", "y", "z"), ("y", "z", "x")))


def doc_layout(lengths):
    ends = jnp.cumsum(lengths, axis=-1)
    starts = ends - lengths
    place = jnp.arange(HALF, dtype=jnp.int32)
    member = (
        (place[:, None] >= starts[..., None, :]) & (place[:, None] < ends[..., None, :])
    ).astype(jnp.int32)
    inside = jnp.sum(member, -1)
    doc_of = jnp.sum(member * jnp.arange(DOCS, dtype=jnp.int32), -1) + DOCS * (1 - inside)
    offset = place - jnp.sum(member * starts[..., None, :], -1)
    return (doc_of, offset, inside)


def sinusoid(offset):
    half = D // 2
    freq = jnp.exp(jnp.arange(half, dtype=jnp.float32) * (-2.0 * math.log(10000.0) / D))
    angle = offset.astype(jnp.float32)[..., None] * freq
    return jnp.stack([jnp.sin(angle), jnp.cos(angle)], -1).reshape(offset.shape + (D,))


def layout():
    wide = D // BLK
    deep = FF // BLK
    return [
        (wide, 3 * wide),
        (wide, wide),
        (wide, deep),
        (deep, wide),
        (wide, 3 * wide),
        (wide, wide),
        (wide, wide),
        (wide, 2 * wide),
        (wide, wide),
        (wide, deep),
        (deep, wide),
    ]


def matmul(left, right):
    return jnp.dot(left, right, preferred_element_type=wide_type)


def shapes():
    return [(rows * BLK, cols * BLK) for rows, cols in layout()]


def first_block(number):
    return sum(rows * cols for rows, cols in layout()[:number])


def nt(left, right):
    return lax.dot_general(left, right, (((1,), (1,)), ((), ())), preferred_element_type=wide_type)


def tn(left, right):
    return lax.dot_general(left, right, (((0,), (0,)), ((), ())), preferred_element_type=wide_type)


def block_copies(number, slots, order, matrix, semaphore, outward):
    rows, cols = layout()[number]
    start = first_block(number)

    def step(k, carry):
        place = matrix.at[
            pl.ds(pl.multiple_of(lax.div(k, cols) * BLK, BLK), BLK),
            pl.ds(pl.multiple_of(lax.rem(k, cols) * BLK, BLK), BLK),
        ]
        slot = slots.at[order[start + k]]
        pair = (place, slot) if outward else (slot, place)
        pltpu.make_async_copy(*pair, semaphore).start()
        return carry

    lax.fori_loop(0, rows * cols, step, 0, unroll=5)


def mean_parts(stream, width, active):
    centre = jnp.sum(stream * width, -1, keepdims=True) / active
    centred = (stream - centre) * width
    spread = jnp.sum(centred * centred, -1, keepdims=True) / active
    return centred, lax.rsqrt(spread + eps_norm)


def normed(stream, vec, row, width, active):
    centred, rate = mean_parts(stream, width, active)
    return (centred * rate * vec[row : row + 1] + vec[row + 1 : row + 2]) * width


def normed_back(stream, vec, row, width, active, cotangent, vec_grad):
    centred, rate = mean_parts(stream, width, active)
    given = cotangent * width
    vec_grad[row : row + 1] = jnp.sum(given * centred * rate, 0, keepdims=True)
    vec_grad[row + 1 : row + 2] = jnp.sum(given, 0, keepdims=True)
    scaled = given * vec[row : row + 1]
    along = jnp.sum(scaled * centred, -1, keepdims=True) / active
    pulled = (scaled * rate - centred * (rate * rate * rate * along)) * width
    return pulled - width * (jnp.sum(pulled, -1, keepdims=True) / active)


def windows():
    for head in range(HEADS):
        low, high_end = head * HEAD, (head + 1) * HEAD
        first, last = low // BLK, (high_end - 1) // BLK + 1
        yield head, low, high_end, first, last


def lanes_between(low, high_end, first, last):
    lane = lax.broadcasted_iota(jnp.int32, (1, (last - first) * BLK), 1) + first * BLK
    return ((lane >= low) & (lane < high_end)).astype(jnp.float32).astype(low_type)


def tile_add(tiles, first, value):
    for k in range(value.shape[1] // BLK):
        part = value[:, k * BLK : (k + 1) * BLK]
        spot = first + k
        tiles[spot] = part if tiles[spot] is None else tiles[spot] + part


def weights_of(query, keys, mask, first, last, allowed):
    span = slice(first * BLK, last * BLK)
    scores = nt(query[:, span] * mask, keys[:, span]) * HEAD ** (-0.5)
    scores = jnp.where(allowed, scores, -1e30)
    expo = jnp.exp(scores - jnp.max(scores, -1, keepdims=True))
    return expo / jnp.sum(expo, -1, keepdims=True)


def attention(query, keys, values, allowed, keep):
    tiles = [None] * (D // BLK)
    for _, low, high_end, first, last in windows():
        mask = lanes_between(low, high_end, first, last)
        probs = weights_of(query, keys, mask, first, last, allowed).astype(low_type)
        tile_add(tiles, first, matmul(probs, values[:, first * BLK : last * BLK] * mask))
    return (jnp.concatenate(tiles, 1) * keep).astype(low_type)


def attention_back(d_rows, query, keys, values, allowed, keep):
    d_mixed = (d_rows * keep).astype(low_type)
    d_query, d_keys, d_values = ([None] * (D // BLK) for _ in range(3))
    for _, low, high_end, first, last in windows():
        mask = lanes_between(low, high_end, first, last)
        span = slice(first * BLK, last * BLK)
        probs = weights_of(query, keys, mask, first, last, allowed)
        given = d_mixed[:, span] * mask
        g_probs = nt(given, values[:, span])
        tile_add(d_values, first, tn(probs.astype(low_type), given))
        along = jnp.sum(probs * g_probs, -1, keepdims=True)
        d_scores = (probs * (g_probs - along)).astype(low_type)
        tile_add(d_query, first, matmul(d_scores, keys[:, span] * mask))
        tile_add(d_keys, first, tn(d_scores, query[:, span] * mask))
    scale = HEAD ** (-0.5)
    return (
        jnp.concatenate(d_query, 1) * scale,
        jnp.concatenate(d_keys, 1) * scale,
        jnp.concatenate(d_values, 1),
    )


GELU_RATE = math.sqrt(2.0 / math.pi)
CHUNK = 768


def gelu_parts(value):
    square = value * value
    bend = jnp.tanh(GELU_RATE * (value + 0.044715 * value * square))
    gate = 0.5 * (1.0 + bend)
    slope = gate + value * (
        0.5 * (1.0 - bend * bend) * GELU_RATE * (1.0 + 3.0 * 0.044715 * square)
    )
    return value * gate, slope


def forward_kernel(*refs):
    slots, order, x_zero, y_zero, vec, width, keep, unit, allowed = refs[:9]
    final, x_one, x_two, y_one, y_two, y_three = refs[9:15]
    qkv_enc, qkv_dec, q_cross, kv_cross, o_enc, o_dec, o_cross, memory = refs[15:23]
    h_enc, h_dec = refs[23:25]
    stored, held = refs[25:36], refs[36:47]
    act, arrive, leave = refs[47:]
    for number in (0, 1, 2, 3, 4, 5, 6, 7, 8, 9, 10):
        block_copies(number, slots, order, held[number], arrive.at[number], False)
    width, keep, vec = width[...], keep[...], vec[...]
    active = jnp.sum(width)
    same, causal = allowed[0] > 0.5, allowed[1] > 0.5

    def weight(number):
        pltpu.make_async_copy(stored[number], held[number], arrive.at[number]).wait()
        pltpu.make_async_copy(held[number], stored[number], leave.at[number]).start()
        return held[number]

    def self_part(stream, row, number, mask, qkv, mixed):
        near = normed(stream, vec, row, width, active).astype(low_type)
        matrix = weight(number)
        for k in range(3):
            part = slice(k * D, (k + 1) * D)
            qkv[:, part] = matmul(near, matrix[:, part]).astype(low_type)
        mixed[...] = attention(
            qkv[:, 0:D], qkv[:, D : 2 * D], qkv[:, 2 * D : 3 * D], mask, keep
        )
        return stream + matmul(mixed[...], weight(number + 1)[...]) * width

    def feed_part(stream, row, number, hidden):
        near = normed(stream, vec, row, width, active).astype(low_type)
        matrix = weight(number)
        for k in range(FF // CHUNK):
            part = slice(k * CHUNK, (k + 1) * CHUNK)
            value = matmul(near, matrix[:, part])
            hidden[:, part] = value
            act[:, part] = (gelu_parts(value)[0] * unit[:, part]).astype(low_type)
        return stream + matmul(act[...], weight(number + 1)[...]) * width

    x_one[...] = self_part(x_zero[...], 0, 0, same, qkv_enc, o_enc)
    x_two[...] = feed_part(x_one[...], 2, 2, h_enc)
    memory[...] = normed(x_two[...], vec, 4, width, active).astype(low_type)
    y_one[...] = self_part(y_zero[...], 6, 4, causal, qkv_dec, o_dec)
    near = normed(y_one[...], vec, 8, width, active).astype(low_type)
    q_cross[...] = matmul(near, weight(6)[...]).astype(low_type)
    kv_cross[...] = matmul(memory[...], weight(7)[...]).astype(low_type)
    o_cross[...] = attention(
        q_cross[...], kv_cross[:, 0:D], kv_cross[:, D : 2 * D], same, keep
    )
    y_two[...] = y_one[...] + matmul(o_cross[...], weight(8)[...]) * width
    y_three[...] = feed_part(y_two[...], 10, 9, h_dec)
    final[...] = normed(y_three[...], vec, 12, width, active).astype(low_type)
    for number in range(11):
        pltpu.make_async_copy(held[number], stored[number], leave.at[number]).wait()


def in_vmem(count):
    return [pl.BlockSpec(memory_space=pltpu.VMEM)] * count


def in_hbm(count):
    return [pl.BlockSpec(memory_space=pltpu.HBM)] * count


SMEM = pl.BlockSpec(memory_space=pltpu.SMEM)


def run_forward(slots, order, x_zero, y_zero, vec, width, keep, unit, allowed):
    def like(cols, kind):
        return jax.ShapeDtypeStruct((HALF, cols), kind)

    small = (
        [like(D, low_type)]
        + [like(D, wide_type)] * 5
        + [like(3 * D, low_type)] * 2
        + [like(D, low_type), like(2 * D, low_type)]
        + [like(D, low_type)] * 4
        + [like(FF, wide_type)] * 2
    )
    mats = [jax.ShapeDtypeStruct(shape, low_type) for shape in shapes()]
    return pl.pallas_call(
        forward_kernel,
        out_shape=small + mats,
        in_specs=in_hbm(1) + [SMEM] + in_vmem(7),
        out_specs=in_vmem(len(small)) + in_hbm(len(mats)),
        scratch_shapes=[pltpu.VMEM(shape, low_type) for shape in shapes()]
        + [pltpu.VMEM((HALF, FF), low_type)]
        + [pltpu.SemaphoreType.DMA((11,))] * 2,
        compiler_params=pltpu.CompilerParams(vmem_limit_bytes=56 * MIB),
    )(slots, order, x_zero, y_zero, vec, width, keep, unit, allowed)


def backward_kernel(*refs):
    order, d_final, x_zero, y_zero, vec, width, keep, unit, allowed = refs[:9]
    x_one, x_two, y_one, y_two, y_three = refs[9:14]
    qkv_enc, qkv_dec, q_cross, kv_cross, o_enc, o_dec, o_cross, memory = refs[14:22]
    h_enc, h_dec = refs[22:24]
    stored = refs[24:35]
    slots, vec_grad, d_rows = refs[35:38]
    held = refs[38:49]
    zeros, d_pack, arrive, leave, blank = refs[49:]
    uses = (10, 9, 8, 7, 6, 5, 4, 3, 2, 1, 0)
    for number in uses:
        pltpu.make_async_copy(stored[number], held[number], arrive.at[number]).start()
    zeros[...] = jnp.zeros_like(zeros)
    empty = order.shape[0] - NBLK
    for k in range(empty):
        pltpu.make_async_copy(zeros, slots.at[order[NBLK + k]], blank).start()
    width, keep, vec = width[...], keep[...], vec[...]
    active = jnp.sum(width)
    same, causal = allowed[0] > 0.5, allowed[1] > 0.5

    def weight(number):
        pltpu.make_async_copy(stored[number], held[number], arrive.at[number]).wait()
        return held[number]

    def send(number):
        block_copies(number, slots, order, held[number], leave.at[number], True)

    def keep_grad(number, value):
        held[number][...] = value.astype(low_type)
        send(number)

    def feed_back(given, stream, row, number, hidden):
        near = normed(stream, vec, row, width, active).astype(low_type)
        branch = (given * width).astype(low_type)
        up, down = weight(number), weight(number + 1)
        pulled = jnp.zeros((HALF, D), wide_type)
        for k in range(FF // CHUNK):
            part = slice(k * CHUNK, (k + 1) * CHUNK)
            d_act = nt(branch, down[part, :])
            value, slope = gelu_parts(hidden[:, part])
            act = (value * unit[:, part]).astype(low_type)
            down[part, :] = tn(act, branch).astype(low_type)
            d_hidden = (slope * (d_act * unit[:, part])).astype(low_type)
            pulled = pulled + nt(d_hidden, up[:, part])
            up[:, part] = tn(near, d_hidden).astype(low_type)
        send(number + 1)
        send(number)
        return given + normed_back(stream, vec, row, width, active, pulled, vec_grad)

    def self_back(given, stream, row, number, mask, qkv, mixed):
        near = normed(stream, vec, row, width, active).astype(low_type)
        branch = (given * width).astype(low_type)
        d_mixed = nt(branch, weight(number + 1)[...])
        keep_grad(number + 1, tn(mixed[...], branch))
        parts = attention_back(
            d_mixed, qkv[:, 0:D], qkv[:, D : 2 * D], qkv[:, 2 * D : 3 * D], mask, keep
        )
        for k in range(3):
            d_pack[:, k * D : (k + 1) * D] = parts[k].astype(low_type)
        matrix = weight(number)
        pulled = nt(d_pack[...], matrix[...])
        for k in range(3):
            part = slice(k * D, (k + 1) * D)
            matrix[:, part] = tn(near, d_pack[:, part]).astype(low_type)
        send(number)
        return given + normed_back(stream, vec, row, width, active, pulled, vec_grad)

    d_three = normed_back(
        y_three[...], vec, 12, width, active, d_final[...].astype(wide_type), vec_grad
    )
    d_two = feed_back(d_three, y_two[...], 10, 9, h_dec)
    near = normed(y_one[...], vec, 8, width, active).astype(low_type)
    branch = (d_two * width).astype(low_type)
    d_mixed = nt(branch, weight(8)[...])
    keep_grad(8, tn(o_cross[...], branch))
    parts = attention_back(
        d_mixed, q_cross[...], kv_cross[:, 0:D], kv_cross[:, D : 2 * D], same, keep
    )
    d_query = parts[0].astype(low_type)
    for k in range(2):
        d_pack[:, k * D : (k + 1) * D] = parts[k + 1].astype(low_type)
    d_memory = nt(d_pack[:, 0 : 2 * D], weight(7)[...])
    keep_grad(7, tn(memory[...], d_pack[:, 0 : 2 * D]))
    pulled = nt(d_query, weight(6)[...])
    keep_grad(6, tn(near, d_query))
    d_one = d_two + normed_back(y_one[...], vec, 8, width, active, pulled, vec_grad)
    d_target = self_back(d_one, y_zero[...], 6, 4, causal, qkv_dec, o_dec)
    d_enc = normed_back(x_two[...], vec, 4, width, active, d_memory, vec_grad)
    d_enc = feed_back(d_enc, x_one[...], 2, 2, h_enc)
    d_source = self_back(d_enc, x_zero[...], 0, 0, same, qkv_enc, o_enc)
    piece = HALF // 4
    for half, value in ((0, d_source), (1, d_target)):
        value = (value * width * math.sqrt(D)).astype(low_type)
        for k in range(4):
            at = (2 * k + half) * piece
            d_rows[at : at + piece] = value[k * piece : (k + 1) * piece]
    vec_grad[14:16] = jnp.zeros((2, D), wide_type)
    for number in range(11):
        pltpu.make_async_copy(held[number], stored[number], leave.at[number]).wait()
    blanks = slots.at[pl.ds(0, empty)]
    pltpu.make_async_copy(blanks, blanks, blank).wait()


def run_backward(order, d_final, x_zero, y_zero, vec, width, keep, unit, allowed, small, mats):
    return pl.pallas_call(
        backward_kernel,
        out_shape=[
            jax.ShapeDtypeStruct((order.shape[0], BLK, BLK), low_type),
            jax.ShapeDtypeStruct((16, D), wide_type),
            jax.ShapeDtypeStruct((2 * HALF, D), low_type),
        ],
        in_specs=[SMEM] + in_vmem(8 + len(small)) + in_hbm(len(mats)),
        out_specs=in_hbm(1) + in_vmem(2),
        scratch_shapes=[pltpu.VMEM(shape, low_type) for shape in shapes()]
        + [pltpu.VMEM((BLK, BLK), low_type), pltpu.VMEM((HALF, 3 * D), low_type)]
        + [pltpu.SemaphoreType.DMA((11,))] * 2
        + [pltpu.SemaphoreType.DMA],
        compiler_params=pltpu.CompilerParams(vmem_limit_bytes=56 * MIB),
    )(order, d_final, x_zero, y_zero, vec, width, keep, unit, allowed, *small, *mats)


def adamw(param, grad, first, second, rate):
    first = beta_one * first + (1.0 - beta_one) * grad
    second = beta_two * second + (1.0 - beta_two) * grad * grad
    fixed_first = first / (1.0 - beta_one**STEP)
    fixed_second = second / (1.0 - beta_two**STEP)
    return (
        param - rate * (fixed_first / (jnp.sqrt(fixed_second) + adam_eps) + decay_rate * param),
        first,
        second,
    )


def on_device(
    token_ids,
    target_ids,
    doc_lengths,
    width_tiles,
    head_mask,
    ffn_tiles,
    slot_block,
    master,
    momentum,
    left_stat,
    right_stat,
    left_root,
    right_root,
    table,
    table_m,
    table_v,
    vec,
    vec_m,
    vec_v,
):
    group = lax.axis_index("sub")
    place = lax.axis_index(TOK)
    groups = lax.axis_size("sub")
    shards = lax.axis_size(TOK)
    shard_rows = table.shape[0]
    piece = HALF // groups
    doc_of, offset, inside = doc_layout(doc_lengths)
    mine = jnp.concatenate(
        [
            quarter(token_ids[:HALF], group, piece),
            quarter(token_ids[HALF:], group, piece),
            quarter(jnp.where(inside > 0, target_ids, -1), group, piece),
            jnp.broadcast_to(jnp.sum(inside), (HALF - 3 * piece,)),
        ]
    )
    table_low = table.astype(low_type)
    heads_up = push_all(mine.reshape(1, HALF), 1, TOK).reshape(shards, HALF)
    slots = gather_tok(master.astype(low_type).reshape(-1, BLK), 2, WEIGHT_WAYS)
    slots = slots.reshape(-1, BLK, BLK)
    all_targets = heads_up[:, 2 * piece : 3 * piece]
    weight = (all_targets >= 0).astype(jnp.float32)
    token_count = jnp.sum(heads_up[:, 3 * piece]).astype(jnp.float32)
    first_row = place * shard_rows
    local = (heads_up[:, : 2 * piece] - first_row).reshape(-1)
    picks = (local[:, None] == jnp.arange(shard_rows, dtype=jnp.int32)).astype(low_type)
    picked = matmul(picks, table_low).astype(low_type).reshape(4, 4, 2, 2 * piece, D)
    rows = scatter_tok(picked, 3, both_ways(2 * piece), "spread", 32 * MIB).astype(jnp.float32)
    rows = rows.reshape(groups, 2, piece, D).transpose(1, 0, 2, 3).reshape(2, HALF, D)
    used = slot_block < NBLK
    ranks = jnp.cumsum(1 - used.astype(jnp.int32)) - 1
    keys = jnp.where(used, slot_block, NBLK + ranks)
    numbers = jnp.arange(slot_block.shape[0], dtype=jnp.int32)
    order = jnp.sum(jnp.where(keys[None, :] == numbers[:, None], numbers[None, :], 0), 1)
    width = jnp.repeat(width_tiles[group], BLK).astype(jnp.float32)[None]
    keep = jnp.repeat(head_mask[group], HEAD).astype(jnp.float32)[None]
    unit = jnp.repeat(ffn_tiles[group], BLK).astype(jnp.float32)[None]
    wave = sinusoid(offset)
    source = (math.sqrt(D) * rows[0] + wave) * width
    target = (math.sqrt(D) * rows[1] + wave) * width
    same = doc_of[:, None] == doc_of[None, :]
    causal = same & (offset[None, :] <= offset[:, None])
    allowed = jnp.stack([same, causal]).astype(jnp.float32)
    common = (source, target, vec, width, keep, unit, allowed)
    final, *kept = run_forward(slots, order, *common)
    kept, mats = kept[:-11], kept[-11:]
    hidden = gather_tok(final, 4, both_ways(HALF), "rows").reshape(-1, D)
    logits = jnp.einsum("td,vd->tv", hidden, table_low, preferred_element_type=wide_type)
    logits = logits.reshape(shards, groups, piece, shard_rows)
    teacher = logits[:, :1]
    peak = jnp.max(logits, -1)
    total = jnp.sum(jnp.exp(logits - peak[..., None]), -1)
    hits = all_targets[..., None] - first_row == jnp.arange(shard_rows, dtype=jnp.int32)
    hit = jnp.sum(jnp.where(hits, logits[:, 0], 0.0), -1)
    gap = jnp.sum(jnp.exp(teacher - peak[:, :1, :, None]) * (teacher - logits[:, 1:]), -1)
    stats = jnp.concatenate([peak, total, hit[:, None], gap], 1).transpose(1, 0, 2)
    stats = sum_all(stats.reshape(-1, BLK), 5, TOK[::-1], merged)
    stats = stats.reshape(-1, shards, piece).transpose(1, 0, 2)
    logs = stats[:, :groups] + jnp.log(stats[:, groups : 2 * groups])
    hit = stats[:, 2 * groups]
    gap = stats[:, 2 * groups + 1 :] / stats[:, groups : groups + 1]
    token_loss = logs[:, 0] - hit + jnp.sum(logs[:, 1:] + gap - logs[:, :1], 1)
    loss_part = jnp.sum(token_loss * weight)
    target_dist = jnp.concatenate(
        [
            hits.astype(jnp.float32)[:, None],
            jnp.broadcast_to(
                jnp.exp(teacher - logs[:, :1, :, None]),
                (shards, groups - 1, piece, shard_rows),
            ),
        ],
        1,
    )
    back = (jnp.exp(logits - logs[..., None]) - target_dist) * (weight / token_count)[
        :, None, :, None
    ]
    back = back.astype(low_type).reshape(-1, shard_rows)
    d_hidden = matmul(back, table_low).astype(low_type).reshape(4, 4, 2, groups * piece, D)
    d_final = scatter_tok(d_hidden, 6, both_ways(HALF), "swap", 32 * MIB)
    table_grad = jnp.einsum("tv,td->vd", back, hidden, preferred_element_type=wide_type)
    slot_grads, vec_grad, d_rows = run_backward(
        order, d_final.reshape(HALF, D), *common, kept, mats
    )
    vec_grad = vec_grad[: vec.shape[0]]
    all_rows = gather_tok(d_rows, 7, both_ways(2 * piece), "sum").reshape(-1, D)
    table_grad = table_grad + jnp.einsum(
        "rv,rd->vd", picks, all_rows, preferred_element_type=wide_type
    )
    table_grad = lax.psum(table_grad, "sub")
    own = scatter_tok(
        slot_grads.reshape(4, 4, 2, -1, BLK), 8, GRAD_WAYS, "gather", 60 * MIB
    ).reshape(master.shape)
    square = jnp.sum(own * own) + jnp.sum(table_grad * table_grad)
    small = jnp.concatenate(
        [
            vec_grad.reshape(-1),
            jnp.broadcast_to(square / groups, (BLK,)),
            jnp.broadcast_to(loss_part / shards, (BLK,)),
        ]
    )
    small = sum_all(small.reshape(-1, BLK), 9, (*TOK[::-1], "sub")).reshape(-1)
    vec_grad = small[: vec.size].reshape(vec.shape)
    loss_sum = small[vec.size + BLK]
    grad_norm = jnp.sqrt(small[vec.size] + jnp.sum(vec_grad * vec_grad))
    scale = jnp.minimum(1.0, clip_limit / grad_norm)
    grad = own * scale
    new_left = beta_stat * left_stat + (1.0 - beta_stat) * jnp.einsum(
        "sij,skj->sik", grad, grad, precision=high
    )
    new_right = beta_stat * right_stat + (1.0 - beta_stat) * jnp.einsum(
        "sji,sjk->sik", grad, grad, precision=high
    )
    new_momentum = beta_one * momentum + (1.0 - beta_one) * grad
    direction = jnp.einsum("sij,sjk->sik", left_root, new_momentum, precision=high)
    direction = jnp.einsum("sik,skl->sil", direction, right_root, precision=high)
    new_master = master - rate_blocks * (direction + decay_rate * master)
    new_table, new_table_m, new_table_v = adamw(
        table, table_grad * scale, table_m, table_v, rate_table
    )
    new_vec, new_vec_m, new_vec_v = adamw(vec, vec_grad * scale, vec_m, vec_v, rate_gains)
    return (
        loss_sum,
        token_count,
        grad_norm,
        new_master,
        new_momentum,
        new_left,
        new_right,
        new_table,
        new_table_m,
        new_table_v,
        new_vec,
        new_vec_m,
        new_vec_v,
    )


def solution(mesh):
    split = Mesh(
        mesh.devices.reshape(mesh.shape["sub"], 4, 4, 2), ("sub", "tok_0", "tok_1", "tok_2")
    )
    placed = (
        P(TOK),
        P(TOK),
        P(TOK),
        P(),
        P(),
        P(),
        P(),
        P(TOK, None, None),
        P(TOK, None, None),
        P(TOK, None, None),
        P(TOK, None, None),
        P(TOK, None, None),
        P(TOK, None, None),
        P(TOK, None),
        P(TOK, None),
        P(TOK, None),
        P(),
        P(),
        P(),
    )
    return jax.shard_map(
        on_device,
        mesh=split,
        in_specs=placed,
        out_specs=(
            P(),
            P(),
            P(),
            P(TOK, None, None),
            P(TOK, None, None),
            P(TOK, None, None),
            P(TOK, None, None),
            P(TOK, None),
            P(TOK, None),
            P(TOK, None),
            P(),
            P(),
            P(),
        ),
        check_vma=False,
    )
```

```python
import functools
import heapq
import math

import jax
import jax.numpy as jnp
from jax import lax
from jax.experimental import pallas as pl
from jax.experimental.pallas import tpu as pltpu
from jax.sharding import Mesh
from jax.sharding import PartitionSpec as P

D = 640
HEADS = 8
HEAD = 80
FF = 3072
BLK = 128
DOCS = 16
STEP = 10
HALF = 128
NBLK = 780
TOK = ("tok_0", "tok_1", "tok_2")


eps_norm = 1e-05
clip_limit = 0.02
beta_one = 0.9
beta_two = 0.98
beta_stat = 0.95
decay_rate = 0.01
adam_eps = 1e-08
rate_table = 0.05
rate_gains = 0.3
rate_blocks = 0.05
high = lax.Precision.HIGHEST
low_type = jnp.bfloat16
wide_type = jnp.float32


def quarter(value, part, count):
    return lax.dynamic_slice_in_dim(value, part * count, count, 0)


MESH = pl.DeviceIdType.MESH
RING = {"z": "tok_0", "x": "tok_1", "y": "sub"}
CORE = "tok_2"
MIB = 1 << 20


def around(axis):
    count = lax.axis_size(axis)
    me = lax.axis_index(axis)
    return me, lax.rem(me + 1, count), lax.rem(me + count - 1, count), lax.rem(me + 2, count)


def greet(axes):
    barrier = pltpu.get_barrier_semaphore()
    peers = 0
    for axis in axes:
        me = lax.axis_index(axis)
        count = lax.axis_size(axis)
        for k in range(1, count):
            pl.semaphore_signal(
                barrier,
                inc=1,
                device_id={axis: lax.rem(me + k, count)},
                device_id_type=MESH,
            )
        peers += count - 1
    pl.semaphore_wait(barrier, peers)


class Copies:
    def __init__(self, send, recv, local):
        self.send, self.recv, self.local = send, recv, local
        self.sent, self.inside = [], 0

    def push(self, source, target, axis, peer):
        k = len(self.sent)
        copy = pltpu.make_async_remote_copy(
            src_ref=source,
            dst_ref=target,
            send_sem=self.send.at[k],
            recv_sem=self.recv.at[k],
            device_id={axis: peer},
            device_id_type=MESH,
        )
        copy.start()
        self.sent.append(copy)
        return copy

    def move(self, source, target):
        copy = pltpu.make_async_copy(source, target, self.local.at[self.inside])
        self.inside += 1
        copy.start()
        return copy

    def finish(self):
        for copy in self.sent:
            copy.wait_send()


def in_turn(steps):
    heap, number, left = [], 0, {}
    for step in steps:
        heap.append((0, number, step, None))
        number += 1
    heapq.heapify(heap)
    while heap:
        now, own, step, parent = heapq.heappop(heap)
        try:
            given = next(step)
        except StopIteration:
            if parent is not None:
                left[parent][0] -= 1
                if left[parent][0] == 0:
                    heapq.heappush(heap, (now, *left.pop(parent)[1]))
            continue
        if isinstance(given, list):
            left[own] = [len(given), (own, step, parent)]
            for child in given:
                heapq.heappush(heap, (now, number, child, own))
                number += 1
        else:
            heapq.heappush(heap, (now + given, own, step, parent))


def size_of(ref):
    return math.prod(ref.shape) * jnp.dtype(ref.dtype).itemsize


def rows_of(start, count, half):
    if half is None:
        return start, count
    return start + half * (count // 2), count // 2


def view(ref, lead, rows):
    start, count = rows
    if not isinstance(start, int):
        start = pl.multiple_of(start, 16)
    return ref.at[(*lead, pl.ds(start, count))]


def places(order, stage, rows, by_sub):
    start, count = rows
    axis = order[stage]

    def part(i, half, settled):
        lead = []
        for name in ("z", "x"):
            if name == axis:
                lead.append(i)
            elif (name in order[:stage]) == settled:
                lead.append(slice(None))
            else:
                lead.append(lax.axis_index(RING[name]))
        if not by_sub:
            span = rows_of(start, count, half)
        else:
            piece = count // 4
            if axis == "y":
                span = rows_of(start + i * piece, piece, half)
            elif ("y" in order[:stage]) == settled:
                span = rows_of(start, count, half)
            else:
                span = rows_of(start + lax.axis_index("sub") * piece, piece, half)
        return tuple(lead), span

    return part


def ring_gather(part, axis, copies, arrived):
    me, right, left, far = around(axis)
    block = size_of(part(me, None))
    first = copies.push(part(me, None), part(me, None), axis, right)
    second = copies.push(part(me, None), part(me, None), axis, left)
    yield block
    first.wait_recv()
    third = copies.push(part(left, 0), part(left, 0), axis, right)
    arrived(part(left, None))
    yield 0
    second.wait_recv()
    fourth = copies.push(part(right, 1), part(right, 1), axis, left)
    arrived(part(right, None))
    yield block // 2
    third.wait_recv()
    fourth.wait_recv()
    arrived(part(far, None))
    yield 0


def gather_flows(colours, value, out, copies):
    z, x, c = (lax.axis_index(a) for a in ("tok_0", "tok_1", CORE))
    crossing = []

    def arrived(ref):
        crossing.append(copies.push(ref, ref, CORE, 1 - c))

    own = []
    for order, (start, count) in colours:
        if "y" in order:
            count = count // 4
            start = start + lax.axis_index("sub") * count
        own.append(
            (
                view(value, (), (start, count)),
                view(out, (z, x, c), (start, count)),
            )
        )
    for copy in [copies.move(*pair) for pair in own]:
        copy.wait()

    def run(order, rows, ref):
        by_sub = "y" in order
        for stage, name in enumerate(order):
            part = places(order, stage, rows, by_sub)

            def here(i, half, part=part):
                (first, second), span = part(i, half, True)
                return view(out, (first, second, c), span)

            steps = ring_gather(here, RING[name], copies, arrived)
            if stage == 0:
                yield next(steps)
                arrived(ref)
            yield from steps

    return [run(*colour, ref) for colour, (_, ref) in zip(colours, own)], crossing


def gather_kernel(colours, swap, axes, value, *refs):
    if swap:
        out, mine, joined, *refs = refs
    else:
        out, *refs = refs
    copies = Copies(*refs)
    greet(axes)
    if swap:
        me = lax.axis_index("sub")
        piece = value.shape[0] // 4

        def part_of(ref, k):
            return ref.at[pl.ds(pl.multiple_of(k * piece, 16), piece)]

        local = copies.move(part_of(value, me), part_of(mine, me))
        arrivals = [
            copies.push(part_of(value, peer), part_of(mine, me), "sub", peer)
            for peer in (lax.rem(me + k, 4) for k in (1, 3, 2))
        ]
        local.wait()
        for copy in arrivals:
            copy.wait_recv()
        value = mine
        if swap == "sum":
            added = mine[pl.ds(0, piece)].astype(jnp.float32)
            for k in range(1, 4):
                added = added + mine[pl.ds(k * piece, piece)].astype(jnp.float32)
            joined[...] = added.astype(joined.dtype)
            value = joined
    flows, crossing = gather_flows(colours, value, out, copies)
    in_turn(flows)
    for copy in crossing:
        copy.wait_recv()
    copies.finish()


def semaphores(count, inside):
    return [
        pltpu.SemaphoreType.DMA((count,)),
        pltpu.SemaphoreType.DMA((count,)),
        pltpu.SemaphoreType.DMA((inside,)),
    ]


def gather_tok(value, number, colours, swap=None):
    stages = sum(len(order) for order, _ in colours)
    rows, lanes = value.shape
    scratch = []
    if swap:
        scratch = [pltpu.VMEM((n, lanes), value.dtype) for n in (rows, rows // 4)]
        rows = rows // 4 if swap == "sum" else rows
    axes = (CORE, "tok_0", "tok_1")
    if swap or any("y" in order for order, _ in colours):
        axes += ("sub",)
    return pl.pallas_call(
        functools.partial(gather_kernel, colours, swap, axes),
        out_shape=jax.ShapeDtypeStruct((4, 4, 2, rows, lanes), value.dtype),
        in_specs=[pl.BlockSpec(memory_space=pltpu.HBM)],
        out_specs=pl.BlockSpec(memory_space=pltpu.HBM),
        scratch_shapes=scratch + semaphores(7 * stages + 8, 4),
        compiler_params=pltpu.CompilerParams(
            collective_id=number, has_side_effects=True, vmem_limit_bytes=16 * MIB
        ),
    )(value)


def add_to(target, *sources):
    lead = target.shape[:-2]
    total = math.prod(lead)

    def step(k, carry):
        spot = []
        for size in reversed(lead):
            spot.append(lax.rem(k, size))
            k = lax.div(k, size)
        spot = tuple(reversed(spot))
        value = target[spot]
        for source in sources:
            value = value + source[spot]
        target[spot] = value
        return carry

    if lead:
        lax.fori_loop(0, total, step, 0)
    else:
        value = target[...]
        for source in sources:
            value = value + source[...]
        target[...] = value


def ring_scatter(here, slots, axis, copies, ready, done):
    me, right, left, far = around(axis)
    r1_in, l1_in, r2_in, l2_in, r3_in, l3_in = slots
    half = size_of(r1_in)
    ready(0)
    r1 = copies.push(here(far, 0), r1_in, axis, right)
    l1 = copies.push(here(far, 1), l1_in, axis, left)
    yield 0
    ready(1)
    r2 = copies.push(here(right, 1), r2_in, axis, right)
    yield 0
    ready(2)
    l2 = copies.push(here(left, 0), l2_in, axis, left)
    yield half
    r1.wait_recv()
    add_to(here(right, 0), r1_in)
    r3 = copies.push(here(right, 0), r3_in, axis, right)
    yield 0
    l1.wait_recv()
    add_to(here(left, 1), l1_in)
    l3 = copies.push(here(left, 1), l3_in, axis, left)
    yield half
    ready(3)
    l2.wait_recv()
    r2.wait_recv()
    yield half
    r3.wait_recv()
    done(0, l2_in, r3_in)
    yield 0
    l3.wait_recv()
    done(1, r2_in, l3_in)
    yield 0


def scatter_flows(colours, ending, value, out, mine, total, other, slots, copies):
    c = lax.axis_index(CORE)
    pending = {}
    for turn in range(4):
        for k, (order, rows) in enumerate(colours):
            part = places(order, 0, rows, "y" in order)
            i = around(RING[order[0]])[(3, 1, 2, 0)[turn]]
            (first, second), span = part(i, None, False)
            pending[k, turn] = (
                copies.push(
                    view(value, (first, second, 1 - c), span),
                    view(other, (first, second), span),
                    CORE,
                    1 - c,
                ),
                copies.move(
                    view(value, (first, second, c), span), view(total, (first, second), span)
                ),
                view(total, (first, second), span),
                view(other, (first, second), span),
            )

    def run(k, order, rows):
        at = 6 * sum(len(o) for o, _ in colours[:k])

        def nothing(turn):
            pass

        def ready(turn):
            across, inside, ours, theirs = pending[k, turn]
            inside.wait()
            across.wait_recv()
            add_to(ours, theirs)

        for stage, name in enumerate(order):
            part = places(order, stage, rows, "y" in order)
            axis = RING[name]
            me = lax.axis_index(axis)

            def here(i, half, part=part):
                lead, span = part(i, half, False)
                return view(total, lead, span)

            def done(half, one, two, part=part, here=here, me=me, stage=stage):
                if stage < len(order) - 1:
                    add_to(here(me, half), one, two)
                    return
                _, (start, size) = part(me, half, False)
                value = here(me, half)[...].astype(jnp.float32)
                value = value + one[...].astype(jnp.float32) + two[...].astype(jnp.float32)
                if not isinstance(start, int):
                    start = pl.multiple_of(start, 16)
                if ending != "gather":
                    mine[pl.ds(start, size)] = value.astype(mine.dtype)
                else:
                    out[pl.ds(start, size)] = value

            yield from ring_scatter(
                here, slots[at : at + 6], axis, copies, nothing if stage else ready, done
            )
            at += 6
        if ending == "gather":
            start, size = rows
            piece = size // 4

            def held(i, half):
                return view(out, (), rows_of(start + i * piece, piece, half))

            yield from ring_gather(held, "sub", copies, lambda ref: None)

    return [run(k, order, rows) for k, (order, rows) in enumerate(colours)]


def to_sub(ending, mine, out, copies):
    me = lax.axis_index("sub")
    piece = mine.shape[0] // 4

    def given(peer):
        if ending == "spread":
            return mine
        return mine.at[pl.ds(pl.multiple_of(peer * piece, 16), piece)]

    local = copies.move(given(me), out.at[me])
    arrivals = [
        copies.push(given(peer), out.at[me], "sub", peer)
        for peer in (lax.rem(me + k, 4) for k in (1, 3, 2))
    ]
    yield size_of(mine)
    local.wait()
    for copy in arrivals:
        copy.wait_recv()


def scatter_kernel(colours, ending, value, *refs):
    if ending == "gather":
        table, out, table_out, total, other, table_in, *refs = refs
    else:
        out, total, other, *refs = refs
    count = sum(len(order) for order, _ in colours) * 6
    slots, refs = refs[:count], refs[count:]
    mine = None
    if ending == "gather":
        table_slots, refs = refs[:6], refs[6:]
    else:
        mine, *refs = refs
    copies = Copies(*refs)
    greet((CORE, "tok_0", "tok_1", "sub"))
    flows = scatter_flows(colours, ending, value, out, mine, total, other, slots, copies)
    if ending == "gather":
        loaded = copies.move(table, table_in)
        piece = table.shape[0] // 4

        def table_flow():
            me = lax.axis_index("sub")
            loaded.wait()

            def here(i, half):
                return view(table_in, (), rows_of(i * piece, piece, half))

            def there(i, half):
                return view(table_out, (), rows_of(i * piece, piece, half))

            def done(half, one, two):
                there(me, half)[...] = here(me, half)[...] + one[...] + two[...]

            yield from ring_scatter(here, table_slots, "sub", copies, lambda turn: None, done)
            yield from ring_gather(there, "sub", copies, lambda ref: None)

        flows = [table_flow(), *flows]
    in_turn(flows)
    if ending != "gather":
        in_turn([to_sub(ending, mine, out, copies)])
    copies.finish()


def scatter_slots(colours, lanes, kind):
    slots = []
    for order, (_, size) in colours:
        piece = size // 4 if "y" in order else size
        lead = {"z": 4, "x": 4}
        seen_y = "y" not in order
        for name in order:
            lead.pop(name, None)
            seen_y = seen_y or name == "y"
            height = (piece if seen_y else size) // 2
            slots += [pltpu.VMEM((*lead.values(), height, lanes), kind)] * 6
    return slots


def scatter_tok(value, number, colours, ending, limit, table=None):
    rows, lanes = value.shape[3:]
    slots = scatter_slots(colours, lanes, value.dtype)
    stages = len(slots) // 6
    shape = {"gather": (rows, lanes), "spread": (4, rows, lanes), "swap": (4, rows // 4, lanes)}
    kind = jnp.float32 if ending == "gather" else value.dtype
    outs = [jax.ShapeDtypeStruct(shape[ending], kind)]
    scratch = [pltpu.VMEM((4, 4, rows, lanes), value.dtype)] * 2
    given = [value]
    if table is None:
        scratch += slots + [pltpu.VMEM((rows, lanes), value.dtype)]
    else:
        height, across = table.shape
        given.append(table)
        outs.append(jax.ShapeDtypeStruct(table.shape, table.dtype))
        scratch += [pltpu.VMEM(table.shape, table.dtype)] + slots
        scratch += [pltpu.VMEM((height // 8, across), table.dtype)] * 6
    result = pl.pallas_call(
        functools.partial(scatter_kernel, colours, ending),
        out_shape=outs,
        in_specs=[pl.BlockSpec(memory_space=pltpu.HBM)] * len(given),
        out_specs=[pl.BlockSpec(memory_space=pltpu.VMEM)] * len(outs),
        scratch_shapes=scratch
        + semaphores(6 * stages + 8 * len(colours) + 14, 4 * len(colours) + 2),
        compiler_params=pltpu.CompilerParams(
            collective_id=number, has_side_effects=True, vmem_limit_bytes=limit
        ),
    )(*given)
    return result if table is not None else result[0]


def open_kernel(weight_ways, row_ways, mine, table, blocks, ids, rows, slots, *refs):
    picked, total, other, held, *refs = refs
    count = sum(len(order) for order, _ in row_ways) * 6
    inbox, refs = refs[:count], refs[count:]
    copies = Copies(*refs)
    greet((CORE, "tok_0", "tok_1", "sub"))
    flows, crossing = gather_flows(weight_ways, blocks, slots, copies)
    axes = ("tok_0", "tok_1", CORE)
    shard_rows = table.shape[0]
    slot_rows = picked.shape[3]

    def row_flow():
        spot = tuple(lax.axis_index(axis) for axis in axes)
        copies.move(mine, ids.at[spot]).wait()
        for depth in reversed(range(3)):
            axis = axes[depth]
            block = ids.at[spot[: depth + 1]]
            arrivals = [
                copies.push(block, block, axis, lax.rem(spot[depth] + k, lax.axis_size(axis)))
                for k in range(1, lax.axis_size(axis))
            ]
            yield 1
            for copy in arrivals:
                copy.wait_recv()
        first_row = lax.axis_index(axes) * shard_rows
        numbers = lax.broadcasted_iota(jnp.int32, (shard_rows, HALF), 0) + first_row

        def pick(k, carry):
            z, x, c = lax.div(k, 8), lax.rem(lax.div(k, 2), 4), lax.rem(k, 2)
            hits = (numbers == ids[z, x, c]).astype(jnp.float32).astype(low_type)
            found = tn(hits, table[...])
            picked[z, x, c] = found[:slot_rows].astype(low_type)
            return carry

        lax.fori_loop(0, 32, pick, 0)
        yield scatter_flows(row_ways, "spread", picked, None, held, total, other, inbox, copies)
        yield from to_sub("spread", held, rows, copies)

    in_turn([*flows, row_flow()])
    for copy in crossing:
        copy.wait_recv()
    copies.finish()


def open_exchange(mine, table, blocks, number, weight_ways, row_ways, slot_rows):
    lanes = table.shape[1]
    inbox = scatter_slots(row_ways, lanes, low_type)
    stages = sum(len(order) for order, _ in weight_ways)
    return pl.pallas_call(
        functools.partial(open_kernel, weight_ways, row_ways),
        out_shape=[
            jax.ShapeDtypeStruct((4, 4, 2, *mine.shape), mine.dtype),
            jax.ShapeDtypeStruct((4, slot_rows, lanes), low_type),
            jax.ShapeDtypeStruct((4, 4, 2, *blocks.shape), blocks.dtype),
        ],
        in_specs=[pl.BlockSpec(memory_space=pltpu.VMEM)] * 2
        + [pl.BlockSpec(memory_space=pltpu.HBM)],
        out_specs=[pl.BlockSpec(memory_space=pltpu.VMEM)] * 2
        + [pl.BlockSpec(memory_space=pltpu.HBM)],
        scratch_shapes=[
            pltpu.VMEM((4, 4, 2, slot_rows, lanes), low_type),
            pltpu.VMEM((4, 4, slot_rows, lanes), low_type),
            pltpu.VMEM((4, 4, slot_rows, lanes), low_type),
            pltpu.VMEM((slot_rows, lanes), low_type),
        ]
        + inbox
        + semaphores(7 * stages + 8 + 7 + len(inbox) + 8 + 4, 16),
        compiler_params=pltpu.CompilerParams(
            collective_id=number, has_side_effects=True, vmem_limit_bytes=56 * MIB
        ),
    )(mine, table, blocks)


def added(values):
    total = values[0]
    for value in values[1:]:
        total = total + value
    return total


def merged(values):
    peaks = [value[0:32] for value in values]
    peak = functools.reduce(jnp.maximum, peaks)
    scales = [jnp.exp(p - peak) for p in peaks]
    total = added([value[32:64] * scale for value, scale in zip(values, scales)])
    hit = added([value[64:72] for value in values])
    gaps = [
        added([value[k : k + 8] * scale[0:8] for value, scale in zip(values, scales)])
        for k in (72, 80, 88)
    ]
    return jnp.concatenate([peak, total, hit, *gaps], 0)


def sum_kernel(axes, combine, value, out, *refs):
    slots, (send, recv) = refs[: len(axes)], refs[len(axes) :]
    greet(axes)
    copies = Copies(send, recv, None)
    out[...] = value[...]
    for axis, slot in zip(axes, slots):
        count = lax.axis_size(axis)
        me = lax.axis_index(axis)
        slot[me] = out[...]
        arrivals = [
            copies.push(slot.at[me], slot.at[me], axis, lax.rem(me + k, count))
            for k in range(1, count)
        ]
        for copy in arrivals:
            copy.wait_recv()
        out[...] = combine([slot[k] for k in range(count)])
    copies.finish()


def sum_all(value, number, axes, combine=added):
    counts = [lax.axis_size(axis) for axis in axes]
    sends = sum(counts) - len(axes)
    return pl.pallas_call(
        functools.partial(sum_kernel, axes, combine),
        out_shape=jax.ShapeDtypeStruct(value.shape, value.dtype),
        in_specs=[pl.BlockSpec(memory_space=pltpu.VMEM)],
        out_specs=pl.BlockSpec(memory_space=pltpu.VMEM),
        scratch_shapes=[pltpu.VMEM((n, *value.shape), value.dtype) for n in counts]
        + [pltpu.SemaphoreType.DMA((sends,))] * 2,
        compiler_params=pltpu.CompilerParams(
            collective_id=number, has_side_effects=True, vmem_limit_bytes=16 * MIB
        ),
    )(value)


def both_ways(rows):
    return ((("z", "x"), (0, rows // 2)), (("x", "z"), (rows // 2, rows // 2)))


def three_ways(first, second, last, orders):
    starts = (0, first, first + second)
    return tuple((o, (s, n)) for o, s, n in zip(orders, starts, (first, second, last)))


WEIGHT_WAYS = three_ways(896, 896, 1408, (("z", "x"), ("x", "z"), ("x", "z", "y")))
GRAD_WAYS = ((("z", "x", "y"), (0, 1664)), (("x", "z", "y"), (1664, 1536)))


def doc_layout(lengths):
    ends = jnp.cumsum(lengths, axis=-1)
    starts = ends - lengths
    place = jnp.arange(HALF, dtype=jnp.int32)
    member = (
        (place[:, None] >= starts[..., None, :]) & (place[:, None] < ends[..., None, :])
    ).astype(jnp.int32)
    inside = jnp.sum(member, -1)
    doc_of = jnp.sum(member * jnp.arange(DOCS, dtype=jnp.int32), -1) + DOCS * (1 - inside)
    offset = place - jnp.sum(member * starts[..., None, :], -1)
    return (doc_of, offset, inside)


def sinusoid(offset):
    half = D // 2
    freq = jnp.exp(jnp.arange(half, dtype=jnp.float32) * (-2.0 * math.log(10000.0) / D))
    angle = offset.astype(jnp.float32)[..., None] * freq
    return jnp.stack([jnp.sin(angle), jnp.cos(angle)], -1).reshape(offset.shape + (D,))


def layout():
    wide = D // BLK
    deep = FF // BLK
    return [
        (wide, 3 * wide),
        (wide, wide),
        (wide, deep),
        (deep, wide),
        (wide, 3 * wide),
        (wide, wide),
        (wide, wide),
        (wide, 2 * wide),
        (wide, wide),
        (wide, deep),
        (deep, wide),
    ]


def matmul(left, right):
    return jnp.dot(left, right, preferred_element_type=wide_type)


def shapes():
    return [(rows * BLK, cols * BLK) for rows, cols in layout()]


def first_block(number):
    return sum(rows * cols for rows, cols in layout()[:number])


def nt(left, right):
    return lax.dot_general(left, right, (((1,), (1,)), ((), ())), preferred_element_type=wide_type)


def tn(left, right):
    return lax.dot_general(left, right, (((0,), (0,)), ((), ())), preferred_element_type=wide_type)


def block_copies(number, slots, order, matrix, semaphore, outward):
    rows, cols = layout()[number]
    start = first_block(number)

    def step(k, carry):
        place = matrix.at[
            pl.ds(pl.multiple_of(lax.div(k, cols) * BLK, BLK), BLK),
            pl.ds(pl.multiple_of(lax.rem(k, cols) * BLK, BLK), BLK),
        ]
        slot = slots.at[order[start + k]]
        pair = (place, slot) if outward else (slot, place)
        pltpu.make_async_copy(*pair, semaphore).start()
        return carry

    lax.fori_loop(0, rows * cols, step, 0, unroll=5)


def mean_parts(stream, width, active):
    centre = jnp.sum(stream * width, -1, keepdims=True) / active
    centred = (stream - centre) * width
    spread = jnp.sum(centred * centred, -1, keepdims=True) / active
    return centred, lax.rsqrt(spread + eps_norm)


def normed(stream, vec, row, width, active):
    centred, rate = mean_parts(stream, width, active)
    return (centred * rate * vec[row : row + 1] + vec[row + 1 : row + 2]) * width


def normed_back(stream, vec, row, width, active, cotangent, vec_grad):
    centred, rate = mean_parts(stream, width, active)
    given = cotangent * width
    vec_grad[row : row + 1] = jnp.sum(given * centred * rate, 0, keepdims=True)
    vec_grad[row + 1 : row + 2] = jnp.sum(given, 0, keepdims=True)
    scaled = given * vec[row : row + 1]
    along = jnp.sum(scaled * centred, -1, keepdims=True) / active
    pulled = (scaled * rate - centred * (rate * rate * rate * along)) * width
    return pulled - width * (jnp.sum(pulled, -1, keepdims=True) / active)


def windows():
    for head in range(HEADS):
        low, high_end = head * HEAD, (head + 1) * HEAD
        first, last = low // BLK, (high_end - 1) // BLK + 1
        yield head, low, high_end, first, last


def lanes_between(low, high_end, first, last):
    lane = lax.broadcasted_iota(jnp.int32, (1, (last - first) * BLK), 1) + first * BLK
    return ((lane >= low) & (lane < high_end)).astype(jnp.float32).astype(low_type)


def tile_add(tiles, first, value):
    for k in range(value.shape[1] // BLK):
        part = value[:, k * BLK : (k + 1) * BLK]
        spot = first + k
        tiles[spot] = part if tiles[spot] is None else tiles[spot] + part


def weights_of(query, keys, mask, first, last, allowed):
    span = slice(first * BLK, last * BLK)
    scores = nt(query[:, span] * mask, keys[:, span]) * HEAD ** (-0.5)
    scores = jnp.where(allowed, scores, -1e30)
    expo = jnp.exp(scores - jnp.max(scores, -1, keepdims=True))
    return expo / jnp.sum(expo, -1, keepdims=True)


def attention(query, keys, values, allowed, keep):
    tiles = [None] * (D // BLK)
    for _, low, high_end, first, last in windows():
        mask = lanes_between(low, high_end, first, last)
        probs = weights_of(query, keys, mask, first, last, allowed).astype(low_type)
        tile_add(tiles, first, matmul(probs, values[:, first * BLK : last * BLK] * mask))
    return (jnp.concatenate(tiles, 1) * keep).astype(low_type)


def attention_back(d_rows, query, keys, values, allowed, keep):
    d_mixed = (d_rows * keep).astype(low_type)
    d_query, d_keys, d_values = ([None] * (D // BLK) for _ in range(3))
    for _, low, high_end, first, last in windows():
        mask = lanes_between(low, high_end, first, last)
        span = slice(first * BLK, last * BLK)
        probs = weights_of(query, keys, mask, first, last, allowed)
        given = d_mixed[:, span] * mask
        g_probs = nt(given, values[:, span])
        tile_add(d_values, first, tn(probs.astype(low_type), given))
        along = jnp.sum(probs * g_probs, -1, keepdims=True)
        d_scores = (probs * (g_probs - along)).astype(low_type)
        tile_add(d_query, first, matmul(d_scores, keys[:, span] * mask))
        tile_add(d_keys, first, tn(d_scores, query[:, span] * mask))
    scale = HEAD ** (-0.5)
    return (
        jnp.concatenate(d_query, 1) * scale,
        jnp.concatenate(d_keys, 1) * scale,
        jnp.concatenate(d_values, 1),
    )


GELU_RATE = math.sqrt(2.0 / math.pi)
CHUNK = 768


def gelu_parts(value):
    square = value * value
    bend = jnp.tanh(GELU_RATE * (value + 0.044715 * value * square))
    gate = 0.5 * (1.0 + bend)
    slope = gate + value * (
        0.5 * (1.0 - bend * bend) * GELU_RATE * (1.0 + 3.0 * 0.044715 * square)
    )
    return value * gate, slope


def forward_kernel(*refs):
    slots, order, x_zero, y_zero, vec, width, keep, unit, allowed = refs[:9]
    final, x_one, x_two, y_one, y_two, y_three = refs[9:15]
    qkv_enc, qkv_dec, q_cross, kv_cross, o_enc, o_dec, o_cross, memory = refs[15:23]
    h_enc, h_dec = refs[23:25]
    stored, held = refs[25:36], refs[36:47]
    act, arrive, leave = refs[47:]
    for number in (0, 1, 2, 3, 4, 5, 6, 7, 8, 9, 10):
        block_copies(number, slots, order, held[number], arrive.at[number], False)
    width, keep, vec = width[...], keep[...], vec[...]
    active = jnp.sum(width)
    same, causal = allowed[0] > 0.5, allowed[1] > 0.5

    def weight(number):
        pltpu.make_async_copy(stored[number], held[number], arrive.at[number]).wait()
        pltpu.make_async_copy(held[number], stored[number], leave.at[number]).start()
        return held[number]

    def self_part(stream, row, number, mask, qkv, mixed):
        near = normed(stream, vec, row, width, active).astype(low_type)
        matrix = weight(number)
        for k in range(3):
            part = slice(k * D, (k + 1) * D)
            qkv[:, part] = matmul(near, matrix[:, part]).astype(low_type)
        mixed[...] = attention(
            qkv[:, 0:D], qkv[:, D : 2 * D], qkv[:, 2 * D : 3 * D], mask, keep
        )
        return stream + matmul(mixed[...], weight(number + 1)[...]) * width

    def feed_part(stream, row, number, hidden):
        near = normed(stream, vec, row, width, active).astype(low_type)
        matrix = weight(number)
        for k in range(FF // CHUNK):
            part = slice(k * CHUNK, (k + 1) * CHUNK)
            value = matmul(near, matrix[:, part])
            hidden[:, part] = value
            act[:, part] = (gelu_parts(value)[0] * unit[:, part]).astype(low_type)
        return stream + matmul(act[...], weight(number + 1)[...]) * width

    x_one[...] = self_part(x_zero[...], 0, 0, same, qkv_enc, o_enc)
    x_two[...] = feed_part(x_one[...], 2, 2, h_enc)
    memory[...] = normed(x_two[...], vec, 4, width, active).astype(low_type)
    y_one[...] = self_part(y_zero[...], 6, 4, causal, qkv_dec, o_dec)
    near = normed(y_one[...], vec, 8, width, active).astype(low_type)
    q_cross[...] = matmul(near, weight(6)[...]).astype(low_type)
    kv_cross[...] = matmul(memory[...], weight(7)[...]).astype(low_type)
    o_cross[...] = attention(
        q_cross[...], kv_cross[:, 0:D], kv_cross[:, D : 2 * D], same, keep
    )
    y_two[...] = y_one[...] + matmul(o_cross[...], weight(8)[...]) * width
    y_three[...] = feed_part(y_two[...], 10, 9, h_dec)
    final[...] = normed(y_three[...], vec, 12, width, active).astype(low_type)
    for number in range(11):
        pltpu.make_async_copy(held[number], stored[number], leave.at[number]).wait()


def in_vmem(count):
    return [pl.BlockSpec(memory_space=pltpu.VMEM)] * count


def in_hbm(count):
    return [pl.BlockSpec(memory_space=pltpu.HBM)] * count


SMEM = pl.BlockSpec(memory_space=pltpu.SMEM)


def run_forward(slots, order, x_zero, y_zero, vec, width, keep, unit, allowed):
    def like(cols, kind):
        return jax.ShapeDtypeStruct((HALF, cols), kind)

    small = (
        [like(D, low_type)]
        + [like(D, wide_type)] * 5
        + [like(3 * D, low_type)] * 2
        + [like(D, low_type), like(2 * D, low_type)]
        + [like(D, low_type)] * 4
        + [like(FF, wide_type)] * 2
    )
    mats = [jax.ShapeDtypeStruct(shape, low_type) for shape in shapes()]
    return pl.pallas_call(
        forward_kernel,
        out_shape=small + mats,
        in_specs=in_hbm(1) + [SMEM] + in_vmem(7),
        out_specs=in_vmem(len(small)) + in_hbm(len(mats)),
        scratch_shapes=[pltpu.VMEM(shape, low_type) for shape in shapes()]
        + [pltpu.VMEM((HALF, FF), low_type)]
        + [pltpu.SemaphoreType.DMA((11,))] * 2,
        compiler_params=pltpu.CompilerParams(vmem_limit_bytes=56 * MIB),
    )(slots, order, x_zero, y_zero, vec, width, keep, unit, allowed)


def backward_kernel(*refs):
    order, d_final, x_zero, y_zero, vec, width, keep, unit, allowed = refs[:9]
    x_one, x_two, y_one, y_two, y_three = refs[9:14]
    qkv_enc, qkv_dec, q_cross, kv_cross, o_enc, o_dec, o_cross, memory = refs[14:22]
    h_enc, h_dec = refs[22:24]
    stored = refs[24:35]
    slots, vec_grad, d_rows = refs[35:38]
    held = refs[38:49]
    zeros, d_pack, arrive, leave, blank = refs[49:]
    uses = (10, 9, 8, 7, 6, 5, 4, 3, 2, 1, 0)
    for number in uses:
        pltpu.make_async_copy(stored[number], held[number], arrive.at[number]).start()
    zeros[...] = jnp.zeros_like(zeros)
    empty = order.shape[0] - NBLK
    for k in range(empty):
        pltpu.make_async_copy(zeros, slots.at[order[NBLK + k]], blank).start()
    width, keep, vec = width[...], keep[...], vec[...]
    active = jnp.sum(width)
    same, causal = allowed[0] > 0.5, allowed[1] > 0.5

    def weight(number):
        pltpu.make_async_copy(stored[number], held[number], arrive.at[number]).wait()
        return held[number]

    def send(number):
        block_copies(number, slots, order, held[number], leave.at[number], True)

    def keep_grad(number, value):
        held[number][...] = value.astype(low_type)
        send(number)

    def feed_back(given, stream, row, number, hidden):
        near = normed(stream, vec, row, width, active).astype(low_type)
        branch = (given * width).astype(low_type)
        up, down = weight(number), weight(number + 1)
        pulled = jnp.zeros((HALF, D), wide_type)
        for k in range(FF // CHUNK):
            part = slice(k * CHUNK, (k + 1) * CHUNK)
            d_act = nt(branch, down[part, :])
            value, slope = gelu_parts(hidden[:, part])
            act = (value * unit[:, part]).astype(low_type)
            down[part, :] = tn(act, branch).astype(low_type)
            d_hidden = (slope * (d_act * unit[:, part])).astype(low_type)
            pulled = pulled + nt(d_hidden, up[:, part])
            up[:, part] = tn(near, d_hidden).astype(low_type)
        send(number + 1)
        send(number)
        return given + normed_back(stream, vec, row, width, active, pulled, vec_grad)

    def self_back(given, stream, row, number, mask, qkv, mixed):
        near = normed(stream, vec, row, width, active).astype(low_type)
        branch = (given * width).astype(low_type)
        d_mixed = nt(branch, weight(number + 1)[...])
        keep_grad(number + 1, tn(mixed[...], branch))
        parts = attention_back(
            d_mixed, qkv[:, 0:D], qkv[:, D : 2 * D], qkv[:, 2 * D : 3 * D], mask, keep
        )
        for k in range(3):
            d_pack[:, k * D : (k + 1) * D] = parts[k].astype(low_type)
        matrix = weight(number)
        pulled = nt(d_pack[...], matrix[...])
        for k in range(3):
            part = slice(k * D, (k + 1) * D)
            matrix[:, part] = tn(near, d_pack[:, part]).astype(low_type)
        send(number)
        return given + normed_back(stream, vec, row, width, active, pulled, vec_grad)

    d_three = normed_back(
        y_three[...], vec, 12, width, active, d_final[...].astype(wide_type), vec_grad
    )
    d_two = feed_back(d_three, y_two[...], 10, 9, h_dec)
    near = normed(y_one[...], vec, 8, width, active).astype(low_type)
    branch = (d_two * width).astype(low_type)
    d_mixed = nt(branch, weight(8)[...])
    keep_grad(8, tn(o_cross[...], branch))
    parts = attention_back(
        d_mixed, q_cross[...], kv_cross[:, 0:D], kv_cross[:, D : 2 * D], same, keep
    )
    d_query = parts[0].astype(low_type)
    for k in range(2):
        d_pack[:, k * D : (k + 1) * D] = parts[k + 1].astype(low_type)
    d_memory = nt(d_pack[:, 0 : 2 * D], weight(7)[...])
    keep_grad(7, tn(memory[...], d_pack[:, 0 : 2 * D]))
    pulled = nt(d_query, weight(6)[...])
    keep_grad(6, tn(near, d_query))
    d_one = d_two + normed_back(y_one[...], vec, 8, width, active, pulled, vec_grad)
    d_target = self_back(d_one, y_zero[...], 6, 4, causal, qkv_dec, o_dec)
    d_enc = normed_back(x_two[...], vec, 4, width, active, d_memory, vec_grad)
    d_enc = feed_back(d_enc, x_one[...], 2, 2, h_enc)
    d_source = self_back(d_enc, x_zero[...], 0, 0, same, qkv_enc, o_enc)
    piece = HALF // 4
    for half, value in ((0, d_source), (1, d_target)):
        value = (value * width * math.sqrt(D)).astype(low_type)
        for k in range(4):
            at = (2 * k + half) * piece
            d_rows[at : at + piece] = value[k * piece : (k + 1) * piece]
    vec_grad[14:16] = jnp.zeros((2, D), wide_type)
    for number in range(11):
        pltpu.make_async_copy(held[number], stored[number], leave.at[number]).wait()
    blanks = slots.at[pl.ds(0, empty)]
    pltpu.make_async_copy(blanks, blanks, blank).wait()


def run_backward(order, d_final, x_zero, y_zero, vec, width, keep, unit, allowed, small, mats):
    return pl.pallas_call(
        backward_kernel,
        out_shape=[
            jax.ShapeDtypeStruct((order.shape[0], BLK, BLK), low_type),
            jax.ShapeDtypeStruct((16, D), wide_type),
            jax.ShapeDtypeStruct((2 * HALF, D), low_type),
        ],
        in_specs=[SMEM] + in_vmem(8 + len(small)) + in_hbm(len(mats)),
        out_specs=in_hbm(1) + in_vmem(2),
        scratch_shapes=[pltpu.VMEM(shape, low_type) for shape in shapes()]
        + [pltpu.VMEM((BLK, BLK), low_type), pltpu.VMEM((HALF, 3 * D), low_type)]
        + [pltpu.SemaphoreType.DMA((11,))] * 2
        + [pltpu.SemaphoreType.DMA],
        compiler_params=pltpu.CompilerParams(vmem_limit_bytes=56 * MIB),
    )(order, d_final, x_zero, y_zero, vec, width, keep, unit, allowed, *small, *mats)


def adamw(param, grad, first, second, rate):
    first = beta_one * first + (1.0 - beta_one) * grad
    second = beta_two * second + (1.0 - beta_two) * grad * grad
    fixed_first = first / (1.0 - beta_one**STEP)
    fixed_second = second / (1.0 - beta_two**STEP)
    return (
        param - rate * (fixed_first / (jnp.sqrt(fixed_second) + adam_eps) + decay_rate * param),
        first,
        second,
    )


def on_device(
    token_ids,
    target_ids,
    doc_lengths,
    width_tiles,
    head_mask,
    ffn_tiles,
    slot_block,
    master,
    momentum,
    left_stat,
    right_stat,
    left_root,
    right_root,
    table,
    table_m,
    table_v,
    vec,
    vec_m,
    vec_v,
):
    group = lax.axis_index("sub")
    place = lax.axis_index(TOK)
    groups = lax.axis_size("sub")
    shards = lax.axis_size(TOK)
    shard_rows = table.shape[0]
    piece = HALF // groups
    doc_of, offset, inside = doc_layout(doc_lengths)
    mine = jnp.concatenate(
        [
            quarter(token_ids[:HALF], group, piece),
            quarter(token_ids[HALF:], group, piece),
            quarter(jnp.where(inside > 0, target_ids, -1), group, piece),
            jnp.broadcast_to(jnp.sum(inside), (HALF - 3 * piece,)),
        ]
    )
    table_low = table.astype(low_type)
    heads_up, rows, slots = open_exchange(
        mine.reshape(1, HALF),
        table_low,
        master.astype(low_type).reshape(-1, BLK),
        1,
        WEIGHT_WAYS,
        both_ways(2 * piece),
        2 * piece,
    )
    heads_up = heads_up.reshape(shards, HALF)
    slots = slots.reshape(-1, BLK, BLK)
    rows = rows.astype(jnp.float32)
    all_targets = heads_up[:, 2 * piece : 3 * piece]
    weight = (all_targets >= 0).astype(jnp.float32)
    token_count = jnp.sum(heads_up[:, 3 * piece]).astype(jnp.float32)
    first_row = place * shard_rows
    local = (heads_up[:, : 2 * piece] - first_row).reshape(-1)
    picks = (local[:, None] == jnp.arange(shard_rows, dtype=jnp.int32)).astype(low_type)
    rows = rows.reshape(groups, 2, piece, D).transpose(1, 0, 2, 3).reshape(2, HALF, D)
    used = slot_block < NBLK
    ranks = jnp.cumsum(1 - used.astype(jnp.int32)) - 1
    keys = jnp.where(used, slot_block, NBLK + ranks)
    numbers = jnp.arange(slot_block.shape[0], dtype=jnp.int32)
    order = jnp.sum(jnp.where(keys[None, :] == numbers[:, None], numbers[None, :], 0), 1)
    width = jnp.repeat(width_tiles[group], BLK).astype(jnp.float32)[None]
    keep = jnp.repeat(head_mask[group], HEAD).astype(jnp.float32)[None]
    unit = jnp.repeat(ffn_tiles[group], BLK).astype(jnp.float32)[None]
    wave = sinusoid(offset)
    source = (math.sqrt(D) * rows[0] + wave) * width
    target = (math.sqrt(D) * rows[1] + wave) * width
    same = doc_of[:, None] == doc_of[None, :]
    causal = same & (offset[None, :] <= offset[:, None])
    allowed = jnp.stack([same, causal]).astype(jnp.float32)
    common = (source, target, vec, width, keep, unit, allowed)
    final, *kept = run_forward(slots, order, *common)
    kept, mats = kept[:-11], kept[-11:]
    hidden = gather_tok(final, 4, both_ways(HALF), "rows").reshape(-1, D)
    logits = jnp.einsum("td,vd->tv", hidden, table_low, preferred_element_type=wide_type)
    logits = logits.reshape(shards, groups, piece, shard_rows)
    teacher = logits[:, :1]
    peak = jnp.max(logits, -1)
    total = jnp.sum(jnp.exp(logits - peak[..., None]), -1)
    hits = all_targets[..., None] - first_row == jnp.arange(shard_rows, dtype=jnp.int32)
    hit = jnp.sum(jnp.where(hits, logits[:, 0], 0.0), -1)
    gap = jnp.sum(jnp.exp(teacher - peak[:, :1, :, None]) * (teacher - logits[:, 1:]), -1)
    stats = jnp.concatenate([peak, total, hit[:, None], gap], 1).transpose(1, 0, 2)
    stats = sum_all(stats.reshape(-1, BLK), 5, TOK[::-1], merged)
    stats = stats.reshape(-1, shards, piece).transpose(1, 0, 2)
    logs = stats[:, :groups] + jnp.log(stats[:, groups : 2 * groups])
    hit = stats[:, 2 * groups]
    gap = stats[:, 2 * groups + 1 :] / stats[:, groups : groups + 1]
    token_loss = logs[:, 0] - hit + jnp.sum(logs[:, 1:] + gap - logs[:, :1], 1)
    loss_part = jnp.sum(token_loss * weight)
    target_dist = jnp.concatenate(
        [
            hits.astype(jnp.float32)[:, None],
            jnp.broadcast_to(
                jnp.exp(teacher - logs[:, :1, :, None]),
                (shards, groups - 1, piece, shard_rows),
            ),
        ],
        1,
    )
    back = (jnp.exp(logits - logs[..., None]) - target_dist) * (weight / token_count)[
        :, None, :, None
    ]
    back = back.astype(low_type).reshape(-1, shard_rows)
    d_hidden = matmul(back, table_low).astype(low_type).reshape(4, 4, 2, groups * piece, D)
    d_final = scatter_tok(d_hidden, 6, both_ways(HALF), "swap", 32 * MIB)
    table_grad = jnp.einsum("tv,td->vd", back, hidden, preferred_element_type=wide_type)
    slot_grads, vec_grad, d_rows = run_backward(
        order, d_final.reshape(HALF, D), *common, kept, mats
    )
    vec_grad = vec_grad[: vec.shape[0]]
    all_rows = gather_tok(d_rows, 7, both_ways(2 * piece), "sum").reshape(-1, D)
    table_grad = table_grad + jnp.einsum(
        "rv,rd->vd", picks, all_rows, preferred_element_type=wide_type
    )
    own, table_grad = scatter_tok(
        slot_grads.reshape(4, 4, 2, -1, BLK), 8, GRAD_WAYS, "gather", 60 * MIB, table_grad
    )
    own = own.reshape(master.shape)
    square = jnp.sum(own * own) + jnp.sum(table_grad * table_grad)
    small = jnp.concatenate(
        [
            vec_grad.reshape(-1),
            jnp.broadcast_to(square / groups, (BLK,)),
            jnp.broadcast_to(loss_part / shards, (BLK,)),
        ]
    )
    small = sum_all(small.reshape(-1, BLK), 9, (*TOK[::-1], "sub")).reshape(-1)
    vec_grad = small[: vec.size].reshape(vec.shape)
    loss_sum = small[vec.size + BLK]
    grad_norm = jnp.sqrt(small[vec.size] + jnp.sum(vec_grad * vec_grad))
    scale = jnp.minimum(1.0, clip_limit / grad_norm)
    grad = own * scale
    new_left = beta_stat * left_stat + (1.0 - beta_stat) * jnp.einsum(
        "sij,skj->sik", grad, grad, precision=high
    )
    new_right = beta_stat * right_stat + (1.0 - beta_stat) * jnp.einsum(
        "sji,sjk->sik", grad, grad, precision=high
    )
    new_momentum = beta_one * momentum + (1.0 - beta_one) * grad
    direction = jnp.einsum("sij,sjk->sik", left_root, new_momentum, precision=high)
    direction = jnp.einsum("sik,skl->sil", direction, right_root, precision=high)
    new_master = master - rate_blocks * (direction + decay_rate * master)
    new_table, new_table_m, new_table_v = adamw(
        table, table_grad * scale, table_m, table_v, rate_table
    )
    new_vec, new_vec_m, new_vec_v = adamw(vec, vec_grad * scale, vec_m, vec_v, rate_gains)
    return (
        loss_sum,
        token_count,
        grad_norm,
        new_master,
        new_momentum,
        new_left,
        new_right,
        new_table,
        new_table_m,
        new_table_v,
        new_vec,
        new_vec_m,
        new_vec_v,
    )


def solution(mesh):
    split = Mesh(
        mesh.devices.reshape(mesh.shape["sub"], 4, 4, 2), ("sub", "tok_0", "tok_1", "tok_2")
    )
    placed = (
        P(TOK),
        P(TOK),
        P(TOK),
        P(),
        P(),
        P(),
        P(),
        P(TOK, None, None),
        P(TOK, None, None),
        P(TOK, None, None),
        P(TOK, None, None),
        P(TOK, None, None),
        P(TOK, None, None),
        P(TOK, None),
        P(TOK, None),
        P(TOK, None),
        P(),
        P(),
        P(),
    )
    return jax.shard_map(
        on_device,
        mesh=split,
        in_specs=placed,
        out_specs=(
            P(),
            P(),
            P(),
            P(TOK, None, None),
            P(TOK, None, None),
            P(TOK, None, None),
            P(TOK, None, None),
            P(TOK, None),
            P(TOK, None),
            P(TOK, None),
            P(),
            P(),
            P(),
        ),
        check_vma=False,
    )
```

```python
import functools
import heapq
import math

import jax
import jax.numpy as jnp
from jax import lax
from jax.experimental import pallas as pl
from jax.experimental.pallas import tpu as pltpu
from jax.sharding import Mesh
from jax.sharding import PartitionSpec as P

D = 640
HEADS = 8
HEAD = 80
FF = 3072
BLK = 128
DOCS = 16
STEP = 10
HALF = 128
NBLK = 780
TOK = ("tok_0", "tok_1", "tok_2")


eps_norm = 1e-05
clip_limit = 0.02
beta_one = 0.9
beta_two = 0.98
beta_stat = 0.95
decay_rate = 0.01
adam_eps = 1e-08
rate_table = 0.05
rate_gains = 0.3
rate_blocks = 0.05
high = lax.Precision.HIGHEST
low_type = jnp.bfloat16
wide_type = jnp.float32


def quarter(value, part, count):
    return lax.dynamic_slice_in_dim(value, part * count, count, 0)


MESH = pl.DeviceIdType.MESH
RING = {"z": "tok_0", "x": "tok_1", "y": "sub"}
CORE = "tok_2"
MIB = 1 << 20


def around(axis):
    count = lax.axis_size(axis)
    me = lax.axis_index(axis)
    return me, lax.rem(me + 1, count), lax.rem(me + count - 1, count), lax.rem(me + 2, count)


def greet(axes):
    barrier = pltpu.get_barrier_semaphore()
    peers = 0
    for axis in axes:
        me = lax.axis_index(axis)
        count = lax.axis_size(axis)
        for k in range(1, count):
            pl.semaphore_signal(
                barrier,
                inc=1,
                device_id={axis: lax.rem(me + k, count)},
                device_id_type=MESH,
            )
        peers += count - 1
    pl.semaphore_wait(barrier, peers)


class Copies:
    def __init__(self, send, recv, local):
        self.send, self.recv, self.local = send, recv, local
        self.sent, self.inside = [], 0

    def push(self, source, target, axis, peer):
        k = len(self.sent)
        copy = pltpu.make_async_remote_copy(
            src_ref=source,
            dst_ref=target,
            send_sem=self.send.at[k],
            recv_sem=self.recv.at[k],
            device_id={axis: peer},
            device_id_type=MESH,
        )
        copy.start()
        self.sent.append(copy)
        return copy

    def move(self, source, target):
        copy = pltpu.make_async_copy(source, target, self.local.at[self.inside])
        self.inside += 1
        copy.start()
        return copy

    def finish(self):
        for copy in self.sent:
            copy.wait_send()


def in_turn(steps):
    heap, number, left = [], 0, {}
    for step in steps:
        heap.append((0, number, step, None))
        number += 1
    heapq.heapify(heap)
    while heap:
        now, own, step, parent = heapq.heappop(heap)
        try:
            given = next(step)
        except StopIteration:
            if parent is not None:
                left[parent][0] -= 1
                if left[parent][0] == 0:
                    heapq.heappush(heap, (now, *left.pop(parent)[1]))
            continue
        if isinstance(given, list):
            left[own] = [len(given), (own, step, parent)]
            for child in given:
                heapq.heappush(heap, (now, number, child, own))
                number += 1
        else:
            heapq.heappush(heap, (now + given, own, step, parent))


def size_of(ref):
    return math.prod(ref.shape) * jnp.dtype(ref.dtype).itemsize


def rows_of(start, count, half):
    if half is None:
        return start, count
    return start + half * (count // 2), count // 2


def view(ref, lead, rows):
    start, count = rows
    if not isinstance(start, int):
        start = pl.multiple_of(start, 16)
    return ref.at[(*lead, pl.ds(start, count))]


def places(order, stage, rows, by_sub):
    start, count = rows
    axis = order[stage]

    def part(i, half, settled):
        lead = []
        for name in ("z", "x"):
            if name == axis:
                lead.append(i)
            elif (name in order[:stage]) == settled:
                lead.append(slice(None))
            else:
                lead.append(lax.axis_index(RING[name]))
        if not by_sub:
            span = rows_of(start, count, half)
        else:
            piece = count // 4
            if axis == "y":
                span = rows_of(start + i * piece, piece, half)
            elif ("y" in order[:stage]) == settled:
                span = rows_of(start, count, half)
            else:
                span = rows_of(start + lax.axis_index("sub") * piece, piece, half)
        return tuple(lead), span

    return part


def ring_gather(part, axis, copies, arrived):
    me, right, left, far = around(axis)
    block = size_of(part(me, None))
    first = copies.push(part(me, None), part(me, None), axis, right)
    second = copies.push(part(me, None), part(me, None), axis, left)
    yield block
    first.wait_recv()
    third = copies.push(part(left, 0), part(left, 0), axis, right)
    arrived(part(left, None))
    yield 0
    second.wait_recv()
    fourth = copies.push(part(right, 1), part(right, 1), axis, left)
    arrived(part(right, None))
    yield block // 2
    third.wait_recv()
    fourth.wait_recv()
    arrived(part(far, None))
    yield 0


def gather_flows(colours, value, out, copies, hold=0):
    z, x, c = (lax.axis_index(a) for a in ("tok_0", "tok_1", CORE))
    crossing = []

    def arrived(ref):
        crossing.append(copies.push(ref, ref, CORE, 1 - c))

    own = []
    for order, (start, count) in colours:
        if "y" in order:
            count = count // 4
            start = start + lax.axis_index("sub") * count
        own.append(
            (
                view(value, (), (start, count)),
                view(out, (z, x, c), (start, count)),
            )
        )
    for copy in [copies.move(*pair) for pair in own]:
        copy.wait()

    def run(order, rows, ref):
        by_sub = "y" in order
        for stage, name in enumerate(order):
            part = places(order, stage, rows, by_sub)

            def here(i, half, part=part):
                (first, second), span = part(i, half, True)
                return view(out, (first, second, c), span)

            steps = ring_gather(here, RING[name], copies, arrived)
            if stage == 0:
                yield next(steps)
                arrived(ref)
            elif stage == 1 and hold:
                yield hold
            yield from steps

    return [run(*colour, ref) for colour, (_, ref) in zip(colours, own)], crossing


def gather_kernel(colours, swap, axes, value, *refs):
    if swap:
        out, mine, joined, *refs = refs
    else:
        out, *refs = refs
    copies = Copies(*refs)
    greet(axes)
    if swap:
        me = lax.axis_index("sub")
        piece = value.shape[0] // 4

        def part_of(ref, k):
            return ref.at[pl.ds(pl.multiple_of(k * piece, 16), piece)]

        local = copies.move(part_of(value, me), part_of(mine, me))
        arrivals = [
            copies.push(part_of(value, peer), part_of(mine, me), "sub", peer)
            for peer in (lax.rem(me + k, 4) for k in (1, 3, 2))
        ]
        local.wait()
        for copy in arrivals:
            copy.wait_recv()
        value = mine
        if swap == "sum":
            added = mine[pl.ds(0, piece)].astype(jnp.float32)
            for k in range(1, 4):
                added = added + mine[pl.ds(k * piece, piece)].astype(jnp.float32)
            joined[...] = added.astype(joined.dtype)
            value = joined
    flows, crossing = gather_flows(colours, value, out, copies)
    in_turn(flows)
    for copy in crossing:
        copy.wait_recv()
    copies.finish()


def semaphores(count, inside):
    return [
        pltpu.SemaphoreType.DMA((count,)),
        pltpu.SemaphoreType.DMA((count,)),
        pltpu.SemaphoreType.DMA((inside,)),
    ]


def gather_tok(value, number, colours, swap=None):
    stages = sum(len(order) for order, _ in colours)
    rows, lanes = value.shape
    scratch = []
    if swap:
        scratch = [pltpu.VMEM((n, lanes), value.dtype) for n in (rows, rows // 4)]
        rows = rows // 4 if swap == "sum" else rows
    axes = (CORE, "tok_0", "tok_1")
    if swap or any("y" in order for order, _ in colours):
        axes += ("sub",)
    return pl.pallas_call(
        functools.partial(gather_kernel, colours, swap, axes),
        out_shape=jax.ShapeDtypeStruct((4, 4, 2, rows, lanes), value.dtype),
        in_specs=[pl.BlockSpec(memory_space=pltpu.HBM)],
        out_specs=pl.BlockSpec(memory_space=pltpu.HBM),
        scratch_shapes=scratch + semaphores(7 * stages + 8, 4),
        compiler_params=pltpu.CompilerParams(
            collective_id=number, has_side_effects=True, vmem_limit_bytes=16 * MIB
        ),
    )(value)


def add_to(target, *sources):
    lead = target.shape[:-2]
    total = math.prod(lead)

    def step(k, carry):
        spot = []
        for size in reversed(lead):
            spot.append(lax.rem(k, size))
            k = lax.div(k, size)
        spot = tuple(reversed(spot))
        value = target[spot]
        for source in sources:
            value = value + source[spot]
        target[spot] = value
        return carry

    if lead:
        lax.fori_loop(0, total, step, 0)
    else:
        value = target[...]
        for source in sources:
            value = value + source[...]
        target[...] = value


def ring_scatter(here, slots, axis, copies, ready, done):
    me, right, left, far = around(axis)
    r1_in, l1_in, r2_in, l2_in, r3_in, l3_in = slots
    half = size_of(r1_in)
    ready(0)
    r1 = copies.push(here(far, 0), r1_in, axis, right)
    l1 = copies.push(here(far, 1), l1_in, axis, left)
    yield 0
    ready(1)
    r2 = copies.push(here(right, 1), r2_in, axis, right)
    yield 0
    ready(2)
    l2 = copies.push(here(left, 0), l2_in, axis, left)
    yield half
    r1.wait_recv()
    add_to(here(right, 0), r1_in)
    r3 = copies.push(here(right, 0), r3_in, axis, right)
    yield 0
    l1.wait_recv()
    add_to(here(left, 1), l1_in)
    l3 = copies.push(here(left, 1), l3_in, axis, left)
    yield half
    ready(3)
    l2.wait_recv()
    r2.wait_recv()
    yield half
    r3.wait_recv()
    done(0, l2_in, r3_in)
    yield 0
    l3.wait_recv()
    done(1, r2_in, l3_in)
    yield 0


def scatter_flows(colours, ending, value, out, mine, total, other, slots, copies):
    c = lax.axis_index(CORE)
    pending = {}

    def issue(k, turn):
        order, rows = colours[k]
        part = places(order, 0, rows, "y" in order)
        i = around(RING[order[0]])[(3, 1, 2, 0)[turn]]
        (first, second), span = part(i, None, False)
        ours = view(total, (first, second), span)
        theirs = view(other, (first, second), span)
        pending[k, turn] = (
            copies.push(view(value, (first, second, 1 - c), span), theirs, CORE, 1 - c),
            copies.move(view(value, (first, second, c), span), ours),
            ours,
            theirs,
        )

    for turn in range(2):
        for k in range(len(colours)):
            issue(k, turn)

    def run(k, order, rows):
        at = 6 * sum(len(o) for o, _ in colours[:k])

        def nothing(turn):
            pass

        def ready(turn):
            across, inside, ours, theirs = pending[k, turn]
            inside.wait()
            across.wait_recv()
            if turn < 2:
                issue(k, turn + 2)
            add_to(ours, theirs)

        for stage, name in enumerate(order):
            part = places(order, stage, rows, "y" in order)
            axis = RING[name]
            me = lax.axis_index(axis)

            def here(i, half, part=part):
                lead, span = part(i, half, False)
                return view(total, lead, span)

            def done(half, one, two, part=part, here=here, me=me, stage=stage):
                if stage < len(order) - 1:
                    add_to(here(me, half), one, two)
                    return
                _, (start, size) = part(me, half, False)
                value = here(me, half)[...].astype(jnp.float32)
                value = value + one[...].astype(jnp.float32) + two[...].astype(jnp.float32)
                if not isinstance(start, int):
                    start = pl.multiple_of(start, 16)
                if ending != "gather":
                    mine[pl.ds(start, size)] = value.astype(mine.dtype)
                else:
                    out[pl.ds(start, size)] = value

            yield from ring_scatter(
                here, slots[at : at + 6], axis, copies, nothing if stage else ready, done
            )
            at += 6

    return [run(k, order, rows) for k, (order, rows) in enumerate(colours)]


def to_sub(ending, mine, out, copies):
    me = lax.axis_index("sub")
    piece = mine.shape[0] // 4

    def given(peer):
        if ending == "spread":
            return mine
        return mine.at[pl.ds(pl.multiple_of(peer * piece, 16), piece)]

    local = copies.move(given(me), out.at[me])
    arrivals = [
        copies.push(given(peer), out.at[me], "sub", peer)
        for peer in (lax.rem(me + k, 4) for k in (1, 3, 2))
    ]
    yield size_of(mine)
    local.wait()
    for copy in arrivals:
        copy.wait_recv()


def scatter_kernel(colours, ending, value, out, total, other, *refs):
    count = sum(len(order) for order, _ in colours) * 6
    slots, (mine, *refs) = refs[:count], refs[count:]
    copies = Copies(*refs)
    greet((CORE, "tok_0", "tok_1", "sub"))
    in_turn(scatter_flows(colours, ending, value, out, mine, total, other, slots, copies))
    in_turn([to_sub(ending, mine, out, copies)])
    copies.finish()


def swap_flow(value, mine, copies):
    me = lax.axis_index("sub")
    piece = value.shape[0] // 4

    def part_of(ref, k):
        return ref.at[pl.ds(pl.multiple_of(k * piece, 16), piece)]

    local = copies.move(part_of(value, me), part_of(mine, me))
    arrivals = [
        copies.push(part_of(value, peer), part_of(mine, me), "sub", peer)
        for peer in (lax.rem(me + k, 4) for k in (1, 3, 2))
    ]
    yield 1
    local.wait()
    for copy in arrivals:
        copy.wait_recv()


def close_kernel(colours, row_ways, grads, table, rows, ids, part, *refs):
    own, table_out, sums, total, other, table_in, mine, joined, gathered, *refs = refs
    boards, refs = refs[:4], refs[4:]
    count = sum(len(order) for order, _ in colours) * 6
    slots, refs = refs[:count], refs[count:]
    table_slots, refs = refs[:6], refs[6:]
    copies = Copies(*refs)
    greet((CORE, "tok_0", "tok_1", "sub"))
    loaded = copies.move(table, table_in)
    in_turn([swap_flow(rows, mine, copies)])
    piece = rows.shape[0] // 4
    summed = mine[pl.ds(0, piece)].astype(jnp.float32)
    for k in range(1, 4):
        summed = summed + mine[pl.ds(k * piece, piece)].astype(jnp.float32)
    joined[...] = summed.astype(joined.dtype)
    row_flows, crossing = gather_flows(row_ways, joined, gathered, copies)
    shard_rows, lanes = table.shape
    me_y = lax.axis_index("sub")
    high_rows = shard_rows // 4

    def here(i, half):
        return view(table_in, (), rows_of(i * high_rows, high_rows, half))

    def there(i, half):
        return view(table_out, (), rows_of(i * high_rows, high_rows, half))

    def table_flow():
        yield row_flows
        for copy in crossing:
            copy.wait_recv()
        loaded.wait()
        first_row = lax.axis_index(("tok_0", "tok_1", CORE)) * shard_rows
        numbers = lax.broadcasted_iota(jnp.int32, (shard_rows, HALF), 0) + first_row

        def put(z, carry):
            hits = [
                (numbers == ids[z, x]).astype(jnp.float32).astype(low_type) for x in range(4)
            ]
            found = gathered[z].reshape(4 * HALF, lanes)
            table_in[...] = table_in[...] + matmul(jnp.concatenate(hits, 1), found)
            return carry

        lax.fori_loop(0, 4, put, 0)

        def done(half, one, two):
            there(me_y, half)[...] = here(me_y, half)[...] + one[...] + two[...]

        yield from ring_scatter(here, table_slots, "sub", copies, lambda turn: None, done)

    def block_flow(flow):
        yield 1 << 20
        yield from flow

    def own_part(rows):
        start, size = rows

        def held(i, half):
            return view(own, (), rows_of(start + i * (size // 4), size // 4, half))

        return held

    def norm_flow():
        square = jnp.zeros((1, BLK), jnp.float32)
        for ref in [there(me_y, None)] + [own_part(rows)(me_y, None) for _, rows in colours]:
            value = ref[...]
            value = jnp.sum(value * value, 0, keepdims=True)
            for k in range(value.shape[1] // BLK):
                square = square + value[:, k * BLK : (k + 1) * BLK]
        line = lax.broadcasted_iota(jnp.int32, part.shape, 0)
        sums[...] = part[...] + jnp.where(line == part.shape[0] - 2, square, 0.0)
        for axis, board in zip((CORE, "tok_1", "tok_0", "sub"), boards):
            size = lax.axis_size(axis)
            me = lax.axis_index(axis)
            board[me] = sums[...]
            arrivals = [
                copies.push(board.at[me], board.at[me], axis, lax.rem(me + k, size))
                for k in range(1, size)
            ]
            yield 1
            for copy in arrivals:
                copy.wait_recv()
            sums[...] = added([board[k] for k in range(size)])

    def whole():
        flows = scatter_flows(colours, "gather", grads, own, None, total, other, slots, copies)
        yield [table_flow(), *[block_flow(flow) for flow in flows]]
        ends = [there] + [own_part(rows) for _, rows in colours]
        yield [norm_flow()] + [ring_gather(e, "sub", copies, lambda ref: None) for e in ends]

    in_turn([whole()])
    copies.finish()


def close_exchange(grads, table, rows, ids, part, number, colours, row_ways):
    slots = scatter_slots(colours, BLK, low_type)
    height, lanes = table.shape
    piece = rows.shape[0] // 4
    stages = len(slots) // 6
    vmem = pl.BlockSpec(memory_space=pltpu.VMEM)
    hbm = pl.BlockSpec(memory_space=pltpu.HBM)
    return pl.pallas_call(
        functools.partial(close_kernel, colours, row_ways),
        out_shape=[
            jax.ShapeDtypeStruct(grads.shape[3:], jnp.float32),
            jax.ShapeDtypeStruct(table.shape, jnp.float32),
            jax.ShapeDtypeStruct(part.shape, jnp.float32),
        ],
        in_specs=[hbm, hbm, vmem, vmem, vmem],
        out_specs=[vmem] * 3,
        scratch_shapes=[pltpu.VMEM((4, 4, *grads.shape[3:]), low_type)] * 2
        + [
            pltpu.VMEM(table.shape, jnp.float32),
            pltpu.VMEM(rows.shape, low_type),
            pltpu.VMEM((piece, lanes), low_type),
            pltpu.VMEM((4, 4, 2, piece, lanes), low_type),
        ]
        + [pltpu.VMEM((n, *part.shape), jnp.float32) for n in (2, 4, 4, 4)]
        + slots
        + [pltpu.VMEM((height // 8, lanes), jnp.float32)] * 6
        + semaphores(6 * stages + 8 * len(colours) + 7 * 4 + 3 + 6 + 12 + 10 + 8, 20),
        compiler_params=pltpu.CompilerParams(
            collective_id=number, has_side_effects=True, vmem_limit_bytes=61 * MIB
        ),
    )(grads, table, rows, ids, part)


def scatter_slots(colours, lanes, kind):
    slots = []
    for order, (_, size) in colours:
        piece = size // 4 if "y" in order else size
        lead = {"z": 4, "x": 4}
        seen_y = "y" not in order
        for name in order:
            lead.pop(name, None)
            seen_y = seen_y or name == "y"
            height = (piece if seen_y else size) // 2
            slots += [pltpu.VMEM((*lead.values(), height, lanes), kind)] * 6
    return slots


def scatter_tok(value, number, colours, ending, limit):
    rows, lanes = value.shape[3:]
    slots = scatter_slots(colours, lanes, value.dtype)
    stages = len(slots) // 6
    shape = {"spread": (4, rows, lanes), "swap": (4, rows // 4, lanes)}
    return pl.pallas_call(
        functools.partial(scatter_kernel, colours, ending),
        out_shape=jax.ShapeDtypeStruct(shape[ending], value.dtype),
        in_specs=[pl.BlockSpec(memory_space=pltpu.HBM)],
        out_specs=pl.BlockSpec(memory_space=pltpu.VMEM),
        scratch_shapes=[pltpu.VMEM((4, 4, rows, lanes), value.dtype)] * 2
        + slots
        + [pltpu.VMEM((rows, lanes), value.dtype)]
        + semaphores(6 * stages + 8 * len(colours) + 4, 4 * len(colours) + 2),
        compiler_params=pltpu.CompilerParams(
            collective_id=number, has_side_effects=True, vmem_limit_bytes=limit
        ),
    )(value)


def open_kernel(weight_ways, row_ways, mine, table, blocks, ids, rows, slots, *refs):
    picked, total, other, held, *refs = refs
    count = sum(len(order) for order, _ in row_ways) * 6
    inbox, refs = refs[:count], refs[count:]
    copies = Copies(*refs)
    greet((CORE, "tok_0", "tok_1", "sub"))
    axes = ("tok_0", "tok_1", CORE)
    shard_rows = table.shape[0]
    slot_rows = picked.shape[3]

    def id_flow():
        spot = tuple(lax.axis_index(axis) for axis in axes)
        copies.move(mine, ids.at[spot]).wait()
        for depth in reversed(range(3)):
            axis = axes[depth]
            block = ids.at[spot[: depth + 1]]
            arrivals = [
                copies.push(block, block, axis, lax.rem(spot[depth] + k, lax.axis_size(axis)))
                for k in range(1, lax.axis_size(axis))
            ]
            yield 1
            for copy in arrivals:
                copy.wait_recv()

    in_turn([id_flow()])
    flows, crossing = gather_flows(weight_ways, blocks, slots, copies, 1 << 20)

    def row_flow():
        yield 1
        first_row = lax.axis_index(axes) * shard_rows
        numbers = lax.broadcasted_iota(jnp.int32, (shard_rows, HALF), 0) + first_row

        def pick(k, carry):
            z, x, c = lax.div(k, 8), lax.rem(lax.div(k, 2), 4), lax.rem(k, 2)
            hits = (numbers == ids[z, x, c]).astype(jnp.float32).astype(low_type)
            found = tn(hits, table[...])
            picked[z, x, c] = found[:slot_rows].astype(low_type)
            return carry

        lax.fori_loop(0, 32, pick, 0)
        yield scatter_flows(row_ways, "spread", picked, None, held, total, other, inbox, copies)
        yield from to_sub("spread", held, rows, copies)

    in_turn([*flows, row_flow()])
    for copy in crossing:
        copy.wait_recv()
    copies.finish()


def open_exchange(mine, table, blocks, number, weight_ways, row_ways, slot_rows):
    lanes = table.shape[1]
    inbox = scatter_slots(row_ways, lanes, low_type)
    stages = sum(len(order) for order, _ in weight_ways)
    return pl.pallas_call(
        functools.partial(open_kernel, weight_ways, row_ways),
        out_shape=[
            jax.ShapeDtypeStruct((4, 4, 2, *mine.shape), mine.dtype),
            jax.ShapeDtypeStruct((4, slot_rows, lanes), low_type),
            jax.ShapeDtypeStruct((4, 4, 2, *blocks.shape), blocks.dtype),
        ],
        in_specs=[pl.BlockSpec(memory_space=pltpu.VMEM)] * 2
        + [pl.BlockSpec(memory_space=pltpu.HBM)],
        out_specs=[pl.BlockSpec(memory_space=pltpu.VMEM)] * 2
        + [pl.BlockSpec(memory_space=pltpu.HBM)],
        scratch_shapes=[
            pltpu.VMEM((4, 4, 2, slot_rows, lanes), low_type),
            pltpu.VMEM((4, 4, slot_rows, lanes), low_type),
            pltpu.VMEM((4, 4, slot_rows, lanes), low_type),
            pltpu.VMEM((slot_rows, lanes), low_type),
        ]
        + inbox
        + semaphores(7 * stages + 8 + 7 + len(inbox) + 8 + 4, 16),
        compiler_params=pltpu.CompilerParams(
            collective_id=number, has_side_effects=True, vmem_limit_bytes=56 * MIB
        ),
    )(mine, table, blocks)


def added(values):
    total = values[0]
    for value in values[1:]:
        total = total + value
    return total


def merged(values):
    peaks = [value[0:32] for value in values]
    peak = functools.reduce(jnp.maximum, peaks)
    scales = [jnp.exp(p - peak) for p in peaks]
    total = added([value[32:64] * scale for value, scale in zip(values, scales)])
    hit = added([value[64:72] for value in values])
    gaps = [
        added([value[k : k + 8] * scale[0:8] for value, scale in zip(values, scales)])
        for k in (72, 80, 88)
    ]
    return jnp.concatenate([peak, total, hit, *gaps], 0)


def sum_kernel(axes, combine, value, out, *refs):
    slots, (send, recv) = refs[: len(axes)], refs[len(axes) :]
    greet(axes)
    copies = Copies(send, recv, None)
    out[...] = value[...]
    for axis, slot in zip(axes, slots):
        count = lax.axis_size(axis)
        me = lax.axis_index(axis)
        slot[me] = out[...]
        arrivals = [
            copies.push(slot.at[me], slot.at[me], axis, lax.rem(me + k, count))
            for k in range(1, count)
        ]
        for copy in arrivals:
            copy.wait_recv()
        out[...] = combine([slot[k] for k in range(count)])
    copies.finish()


def sum_all(value, number, axes, combine=added):
    counts = [lax.axis_size(axis) for axis in axes]
    sends = sum(counts) - len(axes)
    return pl.pallas_call(
        functools.partial(sum_kernel, axes, combine),
        out_shape=jax.ShapeDtypeStruct(value.shape, value.dtype),
        in_specs=[pl.BlockSpec(memory_space=pltpu.VMEM)],
        out_specs=pl.BlockSpec(memory_space=pltpu.VMEM),
        scratch_shapes=[pltpu.VMEM((n, *value.shape), value.dtype) for n in counts]
        + [pltpu.SemaphoreType.DMA((sends,))] * 2,
        compiler_params=pltpu.CompilerParams(
            collective_id=number, has_side_effects=True, vmem_limit_bytes=16 * MIB
        ),
    )(value)


def both_ways(rows):
    return ((("z", "x"), (0, rows // 2)), (("x", "z"), (rows // 2, rows // 2)))


def three_ways(first, second, last, orders):
    starts = (0, first, first + second)
    return tuple((o, (s, n)) for o, s, n in zip(orders, starts, (first, second, last)))


WEIGHT_WAYS = three_ways(896, 896, 1408, (("z", "x"), ("x", "z"), ("x", "z", "y")))
GRAD_WAYS = ((("z", "x", "y"), (0, 1664)), (("x", "z", "y"), (1664, 1536)))


def doc_layout(lengths):
    ends = jnp.cumsum(lengths, axis=-1)
    starts = ends - lengths
    place = jnp.arange(HALF, dtype=jnp.int32)
    member = (
        (place[:, None] >= starts[..., None, :]) & (place[:, None] < ends[..., None, :])
    ).astype(jnp.int32)
    inside = jnp.sum(member, -1)
    doc_of = jnp.sum(member * jnp.arange(DOCS, dtype=jnp.int32), -1) + DOCS * (1 - inside)
    offset = place - jnp.sum(member * starts[..., None, :], -1)
    return (doc_of, offset, inside)


def sinusoid(offset):
    half = D // 2
    freq = jnp.exp(jnp.arange(half, dtype=jnp.float32) * (-2.0 * math.log(10000.0) / D))
    angle = offset.astype(jnp.float32)[..., None] * freq
    return jnp.stack([jnp.sin(angle), jnp.cos(angle)], -1).reshape(offset.shape + (D,))


def layout():
    wide = D // BLK
    deep = FF // BLK
    return [
        (wide, 3 * wide),
        (wide, wide),
        (wide, deep),
        (deep, wide),
        (wide, 3 * wide),
        (wide, wide),
        (wide, wide),
        (wide, 2 * wide),
        (wide, wide),
        (wide, deep),
        (deep, wide),
    ]


def matmul(left, right):
    return jnp.dot(left, right, preferred_element_type=wide_type)


def shapes():
    return [(rows * BLK, cols * BLK) for rows, cols in layout()]


def first_block(number):
    return sum(rows * cols for rows, cols in layout()[:number])


def nt(left, right):
    return lax.dot_general(left, right, (((1,), (1,)), ((), ())), preferred_element_type=wide_type)


def tn(left, right):
    return lax.dot_general(left, right, (((0,), (0,)), ((), ())), preferred_element_type=wide_type)


def block_copies(number, slots, order, matrix, semaphore, outward):
    rows, cols = layout()[number]
    start = first_block(number)

    def step(k, carry):
        place = matrix.at[
            pl.ds(pl.multiple_of(lax.div(k, cols) * BLK, BLK), BLK),
            pl.ds(pl.multiple_of(lax.rem(k, cols) * BLK, BLK), BLK),
        ]
        slot = slots.at[order[start + k]]
        pair = (place, slot) if outward else (slot, place)
        pltpu.make_async_copy(*pair, semaphore).start()
        return carry

    lax.fori_loop(0, rows * cols, step, 0, unroll=5)


def mean_parts(stream, width, active):
    centre = jnp.sum(stream * width, -1, keepdims=True) / active
    centred = (stream - centre) * width
    spread = jnp.sum(centred * centred, -1, keepdims=True) / active
    return centred, lax.rsqrt(spread + eps_norm)


def normed(stream, vec, row, width, active):
    centred, rate = mean_parts(stream, width, active)
    return (centred * rate * vec[row : row + 1] + vec[row + 1 : row + 2]) * width


def normed_back(stream, vec, row, width, active, cotangent, vec_grad):
    centred, rate = mean_parts(stream, width, active)
    given = cotangent * width
    vec_grad[row : row + 1] = jnp.sum(given * centred * rate, 0, keepdims=True)
    vec_grad[row + 1 : row + 2] = jnp.sum(given, 0, keepdims=True)
    scaled = given * vec[row : row + 1]
    along = jnp.sum(scaled * centred, -1, keepdims=True) / active
    pulled = (scaled * rate - centred * (rate * rate * rate * along)) * width
    return pulled - width * (jnp.sum(pulled, -1, keepdims=True) / active)


def windows():
    for head in range(HEADS):
        low, high_end = head * HEAD, (head + 1) * HEAD
        first, last = low // BLK, (high_end - 1) // BLK + 1
        yield head, low, high_end, first, last


def lanes_between(low, high_end, first, last):
    lane = lax.broadcasted_iota(jnp.int32, (1, (last - first) * BLK), 1) + first * BLK
    return ((lane >= low) & (lane < high_end)).astype(jnp.float32).astype(low_type)


def tile_add(tiles, first, value):
    for k in range(value.shape[1] // BLK):
        part = value[:, k * BLK : (k + 1) * BLK]
        spot = first + k
        tiles[spot] = part if tiles[spot] is None else tiles[spot] + part


def weights_of(query, keys, mask, first, last, allowed):
    span = slice(first * BLK, last * BLK)
    scores = nt(query[:, span] * mask, keys[:, span]) * HEAD ** (-0.5)
    scores = jnp.where(allowed, scores, -1e30)
    expo = jnp.exp(scores - jnp.max(scores, -1, keepdims=True))
    return expo / jnp.sum(expo, -1, keepdims=True)


def attention(query, keys, values, allowed, keep):
    tiles = [None] * (D // BLK)
    for _, low, high_end, first, last in windows():
        mask = lanes_between(low, high_end, first, last)
        probs = weights_of(query, keys, mask, first, last, allowed).astype(low_type)
        tile_add(tiles, first, matmul(probs, values[:, first * BLK : last * BLK] * mask))
    return (jnp.concatenate(tiles, 1) * keep).astype(low_type)


def attention_back(d_rows, query, keys, values, allowed, keep):
    d_mixed = (d_rows * keep).astype(low_type)
    d_query, d_keys, d_values = ([None] * (D // BLK) for _ in range(3))
    for _, low, high_end, first, last in windows():
        mask = lanes_between(low, high_end, first, last)
        span = slice(first * BLK, last * BLK)
        probs = weights_of(query, keys, mask, first, last, allowed)
        given = d_mixed[:, span] * mask
        g_probs = nt(given, values[:, span])
        tile_add(d_values, first, tn(probs.astype(low_type), given))
        along = jnp.sum(probs * g_probs, -1, keepdims=True)
        d_scores = (probs * (g_probs - along)).astype(low_type)
        tile_add(d_query, first, matmul(d_scores, keys[:, span] * mask))
        tile_add(d_keys, first, tn(d_scores, query[:, span] * mask))
    scale = HEAD ** (-0.5)
    return (
        jnp.concatenate(d_query, 1) * scale,
        jnp.concatenate(d_keys, 1) * scale,
        jnp.concatenate(d_values, 1),
    )


GELU_RATE = math.sqrt(2.0 / math.pi)
CHUNK = 768


def gelu_parts(value):
    square = value * value
    bend = jnp.tanh(GELU_RATE * (value + 0.044715 * value * square))
    gate = 0.5 * (1.0 + bend)
    slope = gate + value * (
        0.5 * (1.0 - bend * bend) * GELU_RATE * (1.0 + 3.0 * 0.044715 * square)
    )
    return value * gate, slope


def forward_kernel(*refs):
    slots, order, x_zero, y_zero, vec, width, keep, unit, allowed = refs[:9]
    final, x_one, x_two, y_one, y_two, y_three = refs[9:15]
    qkv_enc, qkv_dec, q_cross, kv_cross, o_enc, o_dec, o_cross, memory = refs[15:23]
    h_enc, h_dec = refs[23:25]
    stored, held = refs[25:36], refs[36:47]
    act, arrive, leave = refs[47:]
    for number in (0, 1, 2, 3, 4, 5, 6, 7, 8, 9, 10):
        block_copies(number, slots, order, held[number], arrive.at[number], False)
    width, keep, vec = width[...], keep[...], vec[...]
    active = jnp.sum(width)
    same, causal = allowed[0] > 0.5, allowed[1] > 0.5

    def weight(number):
        pltpu.make_async_copy(stored[number], held[number], arrive.at[number]).wait()
        pltpu.make_async_copy(held[number], stored[number], leave.at[number]).start()
        return held[number]

    def self_part(stream, row, number, mask, qkv, mixed):
        near = normed(stream, vec, row, width, active).astype(low_type)
        matrix = weight(number)
        for k in range(3):
            part = slice(k * D, (k + 1) * D)
            qkv[:, part] = matmul(near, matrix[:, part]).astype(low_type)
        mixed[...] = attention(
            qkv[:, 0:D], qkv[:, D : 2 * D], qkv[:, 2 * D : 3 * D], mask, keep
        )
        return stream + matmul(mixed[...], weight(number + 1)[...]) * width

    def feed_part(stream, row, number, hidden):
        near = normed(stream, vec, row, width, active).astype(low_type)
        matrix = weight(number)
        for k in range(FF // CHUNK):
            part = slice(k * CHUNK, (k + 1) * CHUNK)
            value = matmul(near, matrix[:, part])
            hidden[:, part] = value
            act[:, part] = (gelu_parts(value)[0] * unit[:, part]).astype(low_type)
        return stream + matmul(act[...], weight(number + 1)[...]) * width

    x_one[...] = self_part(x_zero[...], 0, 0, same, qkv_enc, o_enc)
    x_two[...] = feed_part(x_one[...], 2, 2, h_enc)
    memory[...] = normed(x_two[...], vec, 4, width, active).astype(low_type)
    y_one[...] = self_part(y_zero[...], 6, 4, causal, qkv_dec, o_dec)
    near = normed(y_one[...], vec, 8, width, active).astype(low_type)
    q_cross[...] = matmul(near, weight(6)[...]).astype(low_type)
    kv_cross[...] = matmul(memory[...], weight(7)[...]).astype(low_type)
    o_cross[...] = attention(
        q_cross[...], kv_cross[:, 0:D], kv_cross[:, D : 2 * D], same, keep
    )
    y_two[...] = y_one[...] + matmul(o_cross[...], weight(8)[...]) * width
    y_three[...] = feed_part(y_two[...], 10, 9, h_dec)
    final[...] = normed(y_three[...], vec, 12, width, active).astype(low_type)
    for number in range(11):
        pltpu.make_async_copy(held[number], stored[number], leave.at[number]).wait()


def in_vmem(count):
    return [pl.BlockSpec(memory_space=pltpu.VMEM)] * count


def in_hbm(count):
    return [pl.BlockSpec(memory_space=pltpu.HBM)] * count


SMEM = pl.BlockSpec(memory_space=pltpu.SMEM)


def run_forward(slots, order, x_zero, y_zero, vec, width, keep, unit, allowed):
    def like(cols, kind):
        return jax.ShapeDtypeStruct((HALF, cols), kind)

    small = (
        [like(D, low_type)]
        + [like(D, wide_type)] * 5
        + [like(3 * D, low_type)] * 2
        + [like(D, low_type), like(2 * D, low_type)]
        + [like(D, low_type)] * 4
        + [like(FF, wide_type)] * 2
    )
    mats = [jax.ShapeDtypeStruct(shape, low_type) for shape in shapes()]
    return pl.pallas_call(
        forward_kernel,
        out_shape=small + mats,
        in_specs=in_hbm(1) + [SMEM] + in_vmem(7),
        out_specs=in_vmem(len(small)) + in_hbm(len(mats)),
        scratch_shapes=[pltpu.VMEM(shape, low_type) for shape in shapes()]
        + [pltpu.VMEM((HALF, FF), low_type)]
        + [pltpu.SemaphoreType.DMA((11,))] * 2,
        compiler_params=pltpu.CompilerParams(vmem_limit_bytes=56 * MIB),
    )(slots, order, x_zero, y_zero, vec, width, keep, unit, allowed)


def backward_kernel(*refs):
    order, d_final, x_zero, y_zero, vec, width, keep, unit, allowed = refs[:9]
    x_one, x_two, y_one, y_two, y_three = refs[9:14]
    qkv_enc, qkv_dec, q_cross, kv_cross, o_enc, o_dec, o_cross, memory = refs[14:22]
    h_enc, h_dec = refs[22:24]
    stored = refs[24:35]
    slots, vec_grad, d_rows = refs[35:38]
    held = refs[38:49]
    zeros, d_pack, arrive, leave, blank = refs[49:]
    uses = (10, 9, 8, 7, 6, 5, 4, 3, 2, 1, 0)
    for number in uses:
        pltpu.make_async_copy(stored[number], held[number], arrive.at[number]).start()
    zeros[...] = jnp.zeros_like(zeros)
    empty = order.shape[0] - NBLK
    for k in range(empty):
        pltpu.make_async_copy(zeros, slots.at[order[NBLK + k]], blank).start()
    width, keep, vec = width[...], keep[...], vec[...]
    active = jnp.sum(width)
    same, causal = allowed[0] > 0.5, allowed[1] > 0.5

    def weight(number):
        pltpu.make_async_copy(stored[number], held[number], arrive.at[number]).wait()
        return held[number]

    def send(number):
        block_copies(number, slots, order, held[number], leave.at[number], True)

    def keep_grad(number, value):
        held[number][...] = value.astype(low_type)
        send(number)

    def feed_back(given, stream, row, number, hidden):
        near = normed(stream, vec, row, width, active).astype(low_type)
        branch = (given * width).astype(low_type)
        up, down = weight(number), weight(number + 1)
        pulled = jnp.zeros((HALF, D), wide_type)
        for k in range(FF // CHUNK):
            part = slice(k * CHUNK, (k + 1) * CHUNK)
            d_act = nt(branch, down[part, :])
            value, slope = gelu_parts(hidden[:, part])
            act = (value * unit[:, part]).astype(low_type)
            down[part, :] = tn(act, branch).astype(low_type)
            d_hidden = (slope * (d_act * unit[:, part])).astype(low_type)
            pulled = pulled + nt(d_hidden, up[:, part])
            up[:, part] = tn(near, d_hidden).astype(low_type)
        send(number + 1)
        send(number)
        return given + normed_back(stream, vec, row, width, active, pulled, vec_grad)

    def self_back(given, stream, row, number, mask, qkv, mixed):
        near = normed(stream, vec, row, width, active).astype(low_type)
        branch = (given * width).astype(low_type)
        d_mixed = nt(branch, weight(number + 1)[...])
        keep_grad(number + 1, tn(mixed[...], branch))
        parts = attention_back(
            d_mixed, qkv[:, 0:D], qkv[:, D : 2 * D], qkv[:, 2 * D : 3 * D], mask, keep
        )
        for k in range(3):
            d_pack[:, k * D : (k + 1) * D] = parts[k].astype(low_type)
        matrix = weight(number)
        pulled = nt(d_pack[...], matrix[...])
        for k in range(3):
            part = slice(k * D, (k + 1) * D)
            matrix[:, part] = tn(near, d_pack[:, part]).astype(low_type)
        send(number)
        return given + normed_back(stream, vec, row, width, active, pulled, vec_grad)

    d_three = normed_back(
        y_three[...], vec, 12, width, active, d_final[...].astype(wide_type), vec_grad
    )
    d_two = feed_back(d_three, y_two[...], 10, 9, h_dec)
    near = normed(y_one[...], vec, 8, width, active).astype(low_type)
    branch = (d_two * width).astype(low_type)
    d_mixed = nt(branch, weight(8)[...])
    keep_grad(8, tn(o_cross[...], branch))
    parts = attention_back(
        d_mixed, q_cross[...], kv_cross[:, 0:D], kv_cross[:, D : 2 * D], same, keep
    )
    d_query = parts[0].astype(low_type)
    for k in range(2):
        d_pack[:, k * D : (k + 1) * D] = parts[k + 1].astype(low_type)
    d_memory = nt(d_pack[:, 0 : 2 * D], weight(7)[...])
    keep_grad(7, tn(memory[...], d_pack[:, 0 : 2 * D]))
    pulled = nt(d_query, weight(6)[...])
    keep_grad(6, tn(near, d_query))
    d_one = d_two + normed_back(y_one[...], vec, 8, width, active, pulled, vec_grad)
    d_target = self_back(d_one, y_zero[...], 6, 4, causal, qkv_dec, o_dec)
    d_enc = normed_back(x_two[...], vec, 4, width, active, d_memory, vec_grad)
    d_enc = feed_back(d_enc, x_one[...], 2, 2, h_enc)
    d_source = self_back(d_enc, x_zero[...], 0, 0, same, qkv_enc, o_enc)
    piece = HALF // 4
    for half, value in ((0, d_source), (1, d_target)):
        value = (value * width * math.sqrt(D)).astype(low_type)
        for k in range(4):
            at = (2 * k + half) * piece
            d_rows[at : at + piece] = value[k * piece : (k + 1) * piece]
    vec_grad[14:16] = jnp.zeros((2, D), wide_type)
    for number in range(11):
        pltpu.make_async_copy(held[number], stored[number], leave.at[number]).wait()
    blanks = slots.at[pl.ds(0, empty)]
    pltpu.make_async_copy(blanks, blanks, blank).wait()


def run_backward(order, d_final, x_zero, y_zero, vec, width, keep, unit, allowed, small, mats):
    return pl.pallas_call(
        backward_kernel,
        out_shape=[
            jax.ShapeDtypeStruct((order.shape[0], BLK, BLK), low_type),
            jax.ShapeDtypeStruct((16, D), wide_type),
            jax.ShapeDtypeStruct((2 * HALF, D), low_type),
        ],
        in_specs=[SMEM] + in_vmem(8 + len(small)) + in_hbm(len(mats)),
        out_specs=in_hbm(1) + in_vmem(2),
        scratch_shapes=[pltpu.VMEM(shape, low_type) for shape in shapes()]
        + [pltpu.VMEM((BLK, BLK), low_type), pltpu.VMEM((HALF, 3 * D), low_type)]
        + [pltpu.SemaphoreType.DMA((11,))] * 2
        + [pltpu.SemaphoreType.DMA],
        compiler_params=pltpu.CompilerParams(vmem_limit_bytes=56 * MIB),
    )(order, d_final, x_zero, y_zero, vec, width, keep, unit, allowed, *small, *mats)


def adamw(param, grad, first, second, rate):
    first = beta_one * first + (1.0 - beta_one) * grad
    second = beta_two * second + (1.0 - beta_two) * grad * grad
    fixed_first = first / (1.0 - beta_one**STEP)
    fixed_second = second / (1.0 - beta_two**STEP)
    return (
        param - rate * (fixed_first / (jnp.sqrt(fixed_second) + adam_eps) + decay_rate * param),
        first,
        second,
    )


def on_device(
    token_ids,
    target_ids,
    doc_lengths,
    width_tiles,
    head_mask,
    ffn_tiles,
    slot_block,
    master,
    momentum,
    left_stat,
    right_stat,
    left_root,
    right_root,
    table,
    table_m,
    table_v,
    vec,
    vec_m,
    vec_v,
):
    group = lax.axis_index("sub")
    place = lax.axis_index(TOK)
    groups = lax.axis_size("sub")
    shards = lax.axis_size(TOK)
    shard_rows = table.shape[0]
    piece = HALF // groups
    doc_of, offset, inside = doc_layout(doc_lengths)
    mine = jnp.concatenate(
        [
            quarter(token_ids[:HALF], group, piece),
            quarter(token_ids[HALF:], group, piece),
            quarter(jnp.where(inside > 0, target_ids, -1), group, piece),
            jnp.broadcast_to(jnp.sum(inside), (HALF - 3 * piece,)),
        ]
    )
    table_low = table.astype(low_type)
    heads_up, rows, slots = open_exchange(
        mine.reshape(1, HALF),
        table_low,
        master.astype(low_type).reshape(-1, BLK),
        1,
        WEIGHT_WAYS,
        both_ways(2 * piece),
        2 * piece,
    )
    heads_up = heads_up.reshape(shards, HALF)
    slots = slots.reshape(-1, BLK, BLK)
    rows = rows.astype(jnp.float32)
    all_targets = heads_up[:, 2 * piece : 3 * piece]
    weight = (all_targets >= 0).astype(jnp.float32)
    token_count = jnp.sum(heads_up[:, 3 * piece]).astype(jnp.float32)
    first_row = place * shard_rows
    rows = rows.reshape(groups, 2, piece, D).transpose(1, 0, 2, 3).reshape(2, HALF, D)
    used = slot_block < NBLK
    ranks = jnp.cumsum(1 - used.astype(jnp.int32)) - 1
    keys = jnp.where(used, slot_block, NBLK + ranks)
    numbers = jnp.arange(slot_block.shape[0], dtype=jnp.int32)
    order = jnp.sum(jnp.where(keys[None, :] == numbers[:, None], numbers[None, :], 0), 1)
    width = jnp.repeat(width_tiles[group], BLK).astype(jnp.float32)[None]
    keep = jnp.repeat(head_mask[group], HEAD).astype(jnp.float32)[None]
    unit = jnp.repeat(ffn_tiles[group], BLK).astype(jnp.float32)[None]
    wave = sinusoid(offset)
    source = (math.sqrt(D) * rows[0] + wave) * width
    target = (math.sqrt(D) * rows[1] + wave) * width
    same = doc_of[:, None] == doc_of[None, :]
    causal = same & (offset[None, :] <= offset[:, None])
    allowed = jnp.stack([same, causal]).astype(jnp.float32)
    common = (source, target, vec, width, keep, unit, allowed)
    final, *kept = run_forward(slots, order, *common)
    kept, mats = kept[:-11], kept[-11:]
    hidden = gather_tok(final, 4, both_ways(HALF), "rows").reshape(-1, D)
    logits = jnp.einsum("td,vd->tv", hidden, table_low, preferred_element_type=wide_type)
    logits = logits.reshape(shards, groups, piece, shard_rows)
    teacher = logits[:, :1]
    peak = jnp.max(logits, -1)
    total = jnp.sum(jnp.exp(logits - peak[..., None]), -1)
    hits = all_targets[..., None] - first_row == jnp.arange(shard_rows, dtype=jnp.int32)
    hit = jnp.sum(jnp.where(hits, logits[:, 0], 0.0), -1)
    gap = jnp.sum(jnp.exp(teacher - peak[:, :1, :, None]) * (teacher - logits[:, 1:]), -1)
    stats = jnp.concatenate([peak, total, hit[:, None], gap], 1).transpose(1, 0, 2)
    stats = sum_all(stats.reshape(-1, BLK), 5, TOK[::-1], merged)
    stats = stats.reshape(-1, shards, piece).transpose(1, 0, 2)
    logs = stats[:, :groups] + jnp.log(stats[:, groups : 2 * groups])
    hit = stats[:, 2 * groups]
    gap = stats[:, 2 * groups + 1 :] / stats[:, groups : groups + 1]
    token_loss = logs[:, 0] - hit + jnp.sum(logs[:, 1:] + gap - logs[:, :1], 1)
    loss_part = jnp.sum(token_loss * weight)
    target_dist = jnp.concatenate(
        [
            hits.astype(jnp.float32)[:, None],
            jnp.broadcast_to(
                jnp.exp(teacher - logs[:, :1, :, None]),
                (shards, groups - 1, piece, shard_rows),
            ),
        ],
        1,
    )
    back = (jnp.exp(logits - logs[..., None]) - target_dist) * (weight / token_count)[
        :, None, :, None
    ]
    back = back.astype(low_type).reshape(-1, shard_rows)
    d_hidden = matmul(back, table_low).astype(low_type).reshape(4, 4, 2, groups * piece, D)
    d_final = scatter_tok(d_hidden, 6, both_ways(HALF), "swap", 32 * MIB)
    table_grad = jnp.einsum("tv,td->vd", back, hidden, preferred_element_type=wide_type)
    slot_grads, vec_grad, d_rows = run_backward(
        order, d_final.reshape(HALF, D), *common, kept, mats
    )
    vec_grad = vec_grad[: vec.shape[0]]
    part = jnp.concatenate(
        [
            vec_grad.reshape(-1),
            jnp.zeros((BLK,), wide_type),
            jnp.broadcast_to(loss_part / shards, (BLK,)),
        ]
    )
    own, table_grad, small = close_exchange(
        slot_grads.reshape(4, 4, 2, -1, BLK),
        table_grad,
        d_rows,
        heads_up[:, : 2 * piece].reshape(4, 4, 1, HALF),
        part.reshape(-1, BLK),
        8,
        GRAD_WAYS,
        both_ways(2 * piece),
    )
    own = own.reshape(master.shape)
    small = small.reshape(-1)
    vec_grad = small[: vec.size].reshape(vec.shape)
    loss_sum = small[vec.size + BLK]
    square = jnp.sum(small[vec.size : vec.size + BLK])
    grad_norm = jnp.sqrt(square + jnp.sum(vec_grad * vec_grad))
    scale = jnp.minimum(1.0, clip_limit / grad_norm)
    grad = own * scale
    new_left = beta_stat * left_stat + (1.0 - beta_stat) * jnp.einsum(
        "sij,skj->sik", grad, grad, precision=high
    )
    new_right = beta_stat * right_stat + (1.0 - beta_stat) * jnp.einsum(
        "sji,sjk->sik", grad, grad, precision=high
    )
    new_momentum = beta_one * momentum + (1.0 - beta_one) * grad
    direction = jnp.einsum("sij,sjk->sik", left_root, new_momentum, precision=high)
    direction = jnp.einsum("sik,skl->sil", direction, right_root, precision=high)
    new_master = master - rate_blocks * (direction + decay_rate * master)
    new_table, new_table_m, new_table_v = adamw(
        table, table_grad * scale, table_m, table_v, rate_table
    )
    new_vec, new_vec_m, new_vec_v = adamw(vec, vec_grad * scale, vec_m, vec_v, rate_gains)
    return (
        loss_sum,
        token_count,
        grad_norm,
        new_master,
        new_momentum,
        new_left,
        new_right,
        new_table,
        new_table_m,
        new_table_v,
        new_vec,
        new_vec_m,
        new_vec_v,
    )


def solution(mesh):
    split = Mesh(
        mesh.devices.reshape(mesh.shape["sub"], 4, 4, 2), ("sub", "tok_0", "tok_1", "tok_2")
    )
    placed = (
        P(TOK),
        P(TOK),
        P(TOK),
        P(),
        P(),
        P(),
        P(),
        P(TOK, None, None),
        P(TOK, None, None),
        P(TOK, None, None),
        P(TOK, None, None),
        P(TOK, None, None),
        P(TOK, None, None),
        P(TOK, None),
        P(TOK, None),
        P(TOK, None),
        P(),
        P(),
        P(),
    )
    return jax.shard_map(
        on_device,
        mesh=split,
        in_specs=placed,
        out_specs=(
            P(),
            P(),
            P(),
            P(TOK, None, None),
            P(TOK, None, None),
            P(TOK, None, None),
            P(TOK, None, None),
            P(TOK, None),
            P(TOK, None),
            P(TOK, None),
            P(),
            P(),
            P(),
        ),
        check_vma=False,
    )
```

```python
import functools
import heapq
import math

import jax
import jax.numpy as jnp
from jax import lax
from jax.experimental import pallas as pl
from jax.experimental.pallas import tpu as pltpu
from jax.sharding import Mesh
from jax.sharding import PartitionSpec as P

D = 640
HEADS = 8
HEAD = 80
FF = 3072
BLK = 128
DOCS = 16
STEP = 10
HALF = 128
NBLK = 780
TOK = ("tok_0", "tok_1", "tok_2")


eps_norm = 1e-05
clip_limit = 0.02
beta_one = 0.9
beta_two = 0.98
beta_stat = 0.95
decay_rate = 0.01
adam_eps = 1e-08
rate_table = 0.05
rate_gains = 0.3
rate_blocks = 0.05
high = lax.Precision.HIGHEST
low_type = jnp.bfloat16
wide_type = jnp.float32


def quarter(value, part, count):
    return lax.dynamic_slice_in_dim(value, part * count, count, 0)


MESH = pl.DeviceIdType.MESH
RING = {"z": "tok_0", "x": "tok_1", "y": "sub"}
CORE = "tok_2"
MIB = 1 << 20


def around(axis):
    count = lax.axis_size(axis)
    me = lax.axis_index(axis)
    return me, lax.rem(me + 1, count), lax.rem(me + count - 1, count), lax.rem(me + 2, count)


def greet(axes):
    barrier = pltpu.get_barrier_semaphore()
    peers = 0
    for axis in axes:
        me = lax.axis_index(axis)
        count = lax.axis_size(axis)
        for k in range(1, count):
            pl.semaphore_signal(
                barrier,
                inc=1,
                device_id={axis: lax.rem(me + k, count)},
                device_id_type=MESH,
            )
        peers += count - 1
    pl.semaphore_wait(barrier, peers)


class Copies:
    def __init__(self, send, recv, local):
        self.send, self.recv, self.local = send, recv, local
        self.sent, self.inside = [], 0

    def push(self, source, target, axis, peer):
        k = len(self.sent)
        copy = pltpu.make_async_remote_copy(
            src_ref=source,
            dst_ref=target,
            send_sem=self.send.at[k],
            recv_sem=self.recv.at[k],
            device_id={axis: peer},
            device_id_type=MESH,
        )
        copy.start()
        self.sent.append(copy)
        return copy

    def move(self, source, target):
        copy = pltpu.make_async_copy(source, target, self.local.at[self.inside])
        self.inside += 1
        copy.start()
        return copy

    def finish(self):
        for copy in self.sent:
            copy.wait_send()


def in_turn(steps):
    heap, number, left = [], 0, {}
    for step in steps:
        heap.append((0, number, step, None))
        number += 1
    heapq.heapify(heap)
    while heap:
        now, own, step, parent = heapq.heappop(heap)
        try:
            given = next(step)
        except StopIteration:
            if parent is not None:
                left[parent][0] -= 1
                if left[parent][0] == 0:
                    heapq.heappush(heap, (now, *left.pop(parent)[1]))
            continue
        if isinstance(given, list):
            left[own] = [len(given), (own, step, parent)]
            for child in given:
                heapq.heappush(heap, (now, number, child, own))
                number += 1
        else:
            heapq.heappush(heap, (now + given, own, step, parent))


def size_of(ref):
    return math.prod(ref.shape) * jnp.dtype(ref.dtype).itemsize


def rows_of(start, count, half):
    if half is None:
        return start, count
    return start + half * (count // 2), count // 2


def view(ref, lead, rows):
    start, count = rows
    if not isinstance(start, int):
        start = pl.multiple_of(start, 16)
    return ref.at[(*lead, pl.ds(start, count))]


def places(order, stage, rows, by_sub):
    start, count = rows
    axis = order[stage]

    def part(i, half, settled):
        lead = []
        for name in ("z", "x"):
            if name == axis:
                lead.append(i)
            elif (name in order[:stage]) == settled:
                lead.append(slice(None))
            else:
                lead.append(lax.axis_index(RING[name]))
        if not by_sub:
            span = rows_of(start, count, half)
        else:
            piece = count // 4
            if axis == "y":
                span = rows_of(start + i * piece, piece, half)
            elif ("y" in order[:stage]) == settled:
                span = rows_of(start, count, half)
            else:
                span = rows_of(start + lax.axis_index("sub") * piece, piece, half)
        return tuple(lead), span

    return part


def about(size, lag=3000):
    return lag + size // 45


def ring_gather(part, axis, copies, arrived, lag=3000):
    me, right, left, far = around(axis)
    block = size_of(part(me, None))
    first = copies.push(part(me, None), part(me, None), axis, right)
    second = copies.push(part(me, None), part(me, None), axis, left)
    yield about(block, lag)
    first.wait_recv()
    third = copies.push(part(left, 0), part(left, 0), axis, right)
    arrived(part(left, None))
    yield 0
    second.wait_recv()
    fourth = copies.push(part(right, 1), part(right, 1), axis, left)
    arrived(part(right, None))
    yield about(block // 2, lag)
    third.wait_recv()
    fourth.wait_recv()
    arrived(part(far, None))
    yield 0


def gather_flows(colours, value, out, copies, lag=3000):
    z, x, c = (lax.axis_index(a) for a in ("tok_0", "tok_1", CORE))
    crossing = []

    def arrived(ref):
        crossing.append(copies.push(ref, ref, CORE, 1 - c))

    own = []
    for order, (start, count) in colours:
        if "y" in order:
            count = count // 4
            start = start + lax.axis_index("sub") * count
        own.append(
            (
                view(value, (), (start, count)),
                view(out, (z, x, c), (start, count)),
            )
        )
    for copy in [copies.move(*pair) for pair in own]:
        copy.wait()

    def run(order, rows, ref):
        by_sub = "y" in order
        for stage, name in enumerate(order):
            part = places(order, stage, rows, by_sub)

            def here(i, half, part=part):
                (first, second), span = part(i, half, True)
                return view(out, (first, second, c), span)

            steps = ring_gather(here, RING[name], copies, arrived, lag)
            if stage == 0:
                yield next(steps)
                arrived(ref)
            yield from steps

    return [run(*colour, ref) for colour, (_, ref) in zip(colours, own)], crossing


def gather_kernel(colours, swap, axes, value, *refs):
    if swap:
        out, mine, joined, *refs = refs
    else:
        out, *refs = refs
    copies = Copies(*refs)
    greet(axes)
    if swap:
        me = lax.axis_index("sub")
        piece = value.shape[0] // 4

        def part_of(ref, k):
            return ref.at[pl.ds(pl.multiple_of(k * piece, 16), piece)]

        local = copies.move(part_of(value, me), part_of(mine, me))
        arrivals = [
            copies.push(part_of(value, peer), part_of(mine, me), "sub", peer)
            for peer in (lax.rem(me + k, 4) for k in (1, 3, 2))
        ]
        local.wait()
        for copy in arrivals:
            copy.wait_recv()
        value = mine
        if swap == "sum":
            added = mine[pl.ds(0, piece)].astype(jnp.float32)
            for k in range(1, 4):
                added = added + mine[pl.ds(k * piece, piece)].astype(jnp.float32)
            joined[...] = added.astype(joined.dtype)
            value = joined
    flows, crossing = gather_flows(colours, value, out, copies)
    in_turn(flows)
    for copy in crossing:
        copy.wait_recv()
    copies.finish()


def semaphores(count, inside):
    return [
        pltpu.SemaphoreType.DMA((count,)),
        pltpu.SemaphoreType.DMA((count,)),
        pltpu.SemaphoreType.DMA((inside,)),
    ]


def gather_tok(value, number, colours, swap=None):
    stages = sum(len(order) for order, _ in colours)
    rows, lanes = value.shape
    scratch = []
    if swap:
        scratch = [pltpu.VMEM((n, lanes), value.dtype) for n in (rows, rows // 4)]
        rows = rows // 4 if swap == "sum" else rows
    axes = (CORE, "tok_0", "tok_1")
    if swap or any("y" in order for order, _ in colours):
        axes += ("sub",)
    return pl.pallas_call(
        functools.partial(gather_kernel, colours, swap, axes),
        out_shape=jax.ShapeDtypeStruct((4, 4, 2, rows, lanes), value.dtype),
        in_specs=[pl.BlockSpec(memory_space=pltpu.HBM)],
        out_specs=pl.BlockSpec(memory_space=pltpu.HBM),
        scratch_shapes=scratch + semaphores(7 * stages + 8, 4),
        compiler_params=pltpu.CompilerParams(
            collective_id=number, has_side_effects=True, vmem_limit_bytes=16 * MIB
        ),
    )(value)


def add_to(target, *sources):
    lead = target.shape[:-2]
    total = math.prod(lead)

    def step(k, carry):
        spot = []
        for size in reversed(lead):
            spot.append(lax.rem(k, size))
            k = lax.div(k, size)
        spot = tuple(reversed(spot))
        value = target[spot]
        for source in sources:
            value = value + source[spot]
        target[spot] = value
        return carry

    if lead:
        lax.fori_loop(0, total, step, 0)
    else:
        value = target[...]
        for source in sources:
            value = value + source[...]
        target[...] = value


def ring_scatter(here, slots, axis, copies, ready, done, lag=3000, turn=0):
    me, right, left, far = around(axis)
    r1_in, l1_in, r2_in, l2_in, r3_in, l3_in = slots
    half = about(size_of(r1_in), lag)
    yield turn
    ready(0)
    r1 = copies.push(here(far, 0), r1_in, axis, right)
    l1 = copies.push(here(far, 1), l1_in, axis, left)
    yield turn
    ready(1)
    r2 = copies.push(here(right, 1), r2_in, axis, right)
    yield turn
    ready(2)
    l2 = copies.push(here(left, 0), l2_in, axis, left)
    yield max(0, half - 2 * turn)
    r1.wait_recv()
    add_to(here(right, 0), r1_in)
    r3 = copies.push(here(right, 0), r3_in, axis, right)
    yield 0
    l1.wait_recv()
    add_to(here(left, 1), l1_in)
    l3 = copies.push(here(left, 1), l3_in, axis, left)
    yield max(turn, half)
    ready(3)
    l2.wait_recv()
    r2.wait_recv()
    yield half
    r3.wait_recv()
    done(0, l2_in, r3_in)
    yield 0
    l3.wait_recv()
    done(1, r2_in, l3_in)
    yield 0


def scatter_flows(
    colours, ending, value, out, mine, total, other, slots, copies, lag=3000
):
    c = lax.axis_index(CORE)
    pending = {}

    def issue(k, turn):
        order, rows = colours[k]
        part = places(order, 0, rows, "y" in order)
        i = around(RING[order[0]])[(3, 1, 2, 0)[turn]]
        (first, second), span = part(i, None, False)
        ours = view(total, (first, second), span)
        theirs = view(other, (first, second), span)
        pending[k, turn] = (
            copies.push(view(value, (first, second, 1 - c), span), theirs, CORE, 1 - c),
            copies.move(view(value, (first, second, c), span), ours),
            ours,
            theirs,
        )

    for turn in range(2):
        for k in range(len(colours)):
            issue(k, turn)

    def run(k, order, rows):
        at = 6 * sum(len(o) for o, _ in colours[:k])

        def nothing(turn):
            pass

        def ready(turn):
            across, inside, ours, theirs = pending[k, turn]
            inside.wait()
            across.wait_recv()
            if turn < 2:
                issue(k, turn + 2)
            add_to(ours, theirs)

        for stage, name in enumerate(order):
            part = places(order, stage, rows, "y" in order)
            axis = RING[name]
            me = lax.axis_index(axis)

            def here(i, half, part=part):
                lead, span = part(i, half, False)
                return view(total, lead, span)

            def done(half, one, two, part=part, here=here, me=me, stage=stage):
                if stage < len(order) - 1:
                    add_to(here(me, half), one, two)
                    return
                _, (start, size) = part(me, half, False)
                value = here(me, half)[...].astype(jnp.float32)
                value = value + one[...].astype(jnp.float32) + two[...].astype(jnp.float32)
                if not isinstance(start, int):
                    start = pl.multiple_of(start, 16)
                if ending != "gather":
                    mine[pl.ds(start, size)] = value.astype(mine.dtype)
                else:
                    out[pl.ds(start, size)] = value

            turn = 0 if stage else len(colours) * size_of(pending[k, 0][2]) // 280
            yield from ring_scatter(
                here, slots[at : at + 6], axis, copies, nothing if stage else ready, done, lag, turn
            )
            at += 6

    return [run(k, order, rows) for k, (order, rows) in enumerate(colours)]


def to_sub(ending, mine, out, copies):
    me = lax.axis_index("sub")
    piece = mine.shape[0] // 4

    def given(peer):
        if ending == "spread":
            return mine
        return mine.at[pl.ds(pl.multiple_of(peer * piece, 16), piece)]

    local = copies.move(given(me), out.at[me])
    arrivals = [
        copies.push(given(peer), out.at[me], "sub", peer)
        for peer in (lax.rem(me + k, 4) for k in (1, 3, 2))
    ]
    yield about(size_of(mine), 5000)
    local.wait()
    for copy in arrivals:
        copy.wait_recv()


def scatter_kernel(colours, ending, value, out, total, other, *refs):
    count = sum(len(order) for order, _ in colours) * 6
    slots, (mine, *refs) = refs[:count], refs[count:]
    copies = Copies(*refs)
    greet((CORE, "tok_0", "tok_1", "sub"))
    in_turn(scatter_flows(colours, ending, value, out, mine, total, other, slots, copies))
    in_turn([to_sub(ending, mine, out, copies)])
    copies.finish()


def swap_flow(value, mine, copies):
    me = lax.axis_index("sub")
    piece = value.shape[0] // 4

    def part_of(ref, k):
        return ref.at[pl.ds(pl.multiple_of(k * piece, 16), piece)]

    local = copies.move(part_of(value, me), part_of(mine, me))
    arrivals = [
        copies.push(part_of(value, peer), part_of(mine, me), "sub", peer)
        for peer in (lax.rem(me + k, 4) for k in (1, 3, 2))
    ]
    yield 1
    local.wait()
    for copy in arrivals:
        copy.wait_recv()


def close_kernel(colours, row_ways, grads, table, rows, ids, part, *refs):
    own, table_out, sums, total, other, table_in, mine, joined, gathered, *refs = refs
    boards, refs = refs[:4], refs[4:]
    count = sum(len(order) for order, _ in colours) * 6
    slots, refs = refs[:count], refs[count:]
    table_slots, refs = refs[:6], refs[6:]
    copies = Copies(*refs)
    greet((CORE, "tok_0", "tok_1", "sub"))
    loaded = copies.move(table, table_in)
    in_turn([swap_flow(rows, mine, copies)])
    piece = rows.shape[0] // 4
    summed = mine[pl.ds(0, piece)].astype(jnp.float32)
    for k in range(1, 4):
        summed = summed + mine[pl.ds(k * piece, piece)].astype(jnp.float32)
    joined[...] = summed.astype(joined.dtype)
    row_flows, crossing = gather_flows(row_ways, joined, gathered, copies)
    shard_rows, lanes = table.shape
    me_y = lax.axis_index("sub")
    high_rows = shard_rows // 4

    def here(i, half):
        return view(table_in, (), rows_of(i * high_rows, high_rows, half))

    def there(i, half):
        return view(table_out, (), rows_of(i * high_rows, high_rows, half))

    def table_flow():
        yield row_flows
        for copy in crossing:
            copy.wait_recv()
        loaded.wait()
        first_row = lax.axis_index(("tok_0", "tok_1", CORE)) * shard_rows
        numbers = lax.broadcasted_iota(jnp.int32, (shard_rows, HALF), 0) + first_row

        def put(z, carry):
            hits = [
                (numbers == ids[z, x]).astype(jnp.float32).astype(low_type) for x in range(4)
            ]
            found = gathered[z].reshape(4 * HALF, lanes)
            table_in[...] = table_in[...] + matmul(jnp.concatenate(hits, 1), found)
            return carry

        lax.fori_loop(0, 4, put, 0)
        yield 8000

        def done(half, one, two):
            there(me_y, half)[...] = here(me_y, half)[...] + one[...] + two[...]

        yield from ring_scatter(here, table_slots, "sub", copies, lambda turn: None, done)

    def own_part(rows):
        start, size = rows

        def held(i, half):
            return view(own, (), rows_of(start + i * (size // 4), size // 4, half))

        return held

    def norm_flow():
        square = jnp.zeros((1, BLK), jnp.float32)
        for ref in [there(me_y, None)] + [own_part(rows)(me_y, None) for _, rows in colours]:
            value = ref[...]
            value = jnp.sum(value * value, 0, keepdims=True)
            for k in range(value.shape[1] // BLK):
                square = square + value[:, k * BLK : (k + 1) * BLK]
        line = lax.broadcasted_iota(jnp.int32, part.shape, 0)
        sums[...] = part[...] + jnp.where(line == part.shape[0] - 2, square, 0.0)
        for axis, board in zip((CORE, "tok_1", "tok_0", "sub"), boards):
            size = lax.axis_size(axis)
            me = lax.axis_index(axis)
            board[me] = sums[...]
            arrivals = [
                copies.push(board.at[me], board.at[me], axis, lax.rem(me + k, size))
                for k in range(1, size)
            ]
            yield 3500
            for copy in arrivals:
                copy.wait_recv()
            sums[...] = added([board[k] for k in range(size)])

    def whole():
        flows = scatter_flows(colours, "gather", grads, own, None, total, other, slots, copies)
        yield [table_flow(), *flows]
        ends = [there] + [own_part(rows) for _, rows in colours]
        yield [norm_flow()] + [ring_gather(e, "sub", copies, lambda ref: None) for e in ends]

    in_turn([whole()])
    copies.finish()


def close_exchange(grads, table, rows, ids, part, number, colours, row_ways):
    slots = scatter_slots(colours, BLK, low_type)
    height, lanes = table.shape
    piece = rows.shape[0] // 4
    stages = len(slots) // 6
    vmem = pl.BlockSpec(memory_space=pltpu.VMEM)
    hbm = pl.BlockSpec(memory_space=pltpu.HBM)
    return pl.pallas_call(
        functools.partial(close_kernel, colours, row_ways),
        out_shape=[
            jax.ShapeDtypeStruct(grads.shape[3:], jnp.float32),
            jax.ShapeDtypeStruct(table.shape, jnp.float32),
            jax.ShapeDtypeStruct(part.shape, jnp.float32),
        ],
        in_specs=[hbm, hbm, vmem, vmem, vmem],
        out_specs=[vmem] * 3,
        scratch_shapes=[pltpu.VMEM((4, 4, *grads.shape[3:]), low_type)] * 2
        + [
            pltpu.VMEM(table.shape, jnp.float32),
            pltpu.VMEM(rows.shape, low_type),
            pltpu.VMEM((piece, lanes), low_type),
            pltpu.VMEM((4, 4, 2, piece, lanes), low_type),
        ]
        + [pltpu.VMEM((n, *part.shape), jnp.float32) for n in (2, 4, 4, 4)]
        + slots
        + [pltpu.VMEM((height // 8, lanes), jnp.float32)] * 6
        + semaphores(6 * stages + 8 * len(colours) + 7 * 4 + 3 + 6 + 12 + 10 + 8, 20),
        compiler_params=pltpu.CompilerParams(
            collective_id=number, has_side_effects=True, vmem_limit_bytes=61 * MIB
        ),
    )(grads, table, rows, ids, part)


def scatter_slots(colours, lanes, kind):
    slots = []
    for order, (_, size) in colours:
        piece = size // 4 if "y" in order else size
        lead = {"z": 4, "x": 4}
        seen_y = "y" not in order
        for name in order:
            lead.pop(name, None)
            seen_y = seen_y or name == "y"
            height = (piece if seen_y else size) // 2
            slots += [pltpu.VMEM((*lead.values(), height, lanes), kind)] * 6
    return slots


def scatter_tok(value, number, colours, ending, limit):
    rows, lanes = value.shape[3:]
    slots = scatter_slots(colours, lanes, value.dtype)
    stages = len(slots) // 6
    shape = {"spread": (4, rows, lanes), "swap": (4, rows // 4, lanes)}
    return pl.pallas_call(
        functools.partial(scatter_kernel, colours, ending),
        out_shape=jax.ShapeDtypeStruct(shape[ending], value.dtype),
        in_specs=[pl.BlockSpec(memory_space=pltpu.HBM)],
        out_specs=pl.BlockSpec(memory_space=pltpu.VMEM),
        scratch_shapes=[pltpu.VMEM((4, 4, rows, lanes), value.dtype)] * 2
        + slots
        + [pltpu.VMEM((rows, lanes), value.dtype)]
        + semaphores(6 * stages + 8 * len(colours) + 4, 4 * len(colours) + 2),
        compiler_params=pltpu.CompilerParams(
            collective_id=number, has_side_effects=True, vmem_limit_bytes=limit
        ),
    )(value)


def open_kernel(weight_ways, row_ways, mine, table, blocks, ids, rows, slots, *refs):
    picked, total, other, held, *refs = refs
    count = sum(len(order) for order, _ in row_ways) * 6
    inbox, refs = refs[:count], refs[count:]
    copies = Copies(*refs)
    greet((CORE, "tok_0", "tok_1", "sub"))
    axes = ("tok_0", "tok_1", CORE)
    shard_rows = table.shape[0]
    slot_rows = picked.shape[3]

    def id_flow():
        spot = tuple(lax.axis_index(axis) for axis in axes)
        copies.move(mine, ids.at[spot]).wait()
        for depth in reversed(range(3)):
            axis = axes[depth]
            block = ids.at[spot[: depth + 1]]
            arrivals = [
                copies.push(block, block, axis, lax.rem(spot[depth] + k, lax.axis_size(axis)))
                for k in range(1, lax.axis_size(axis))
            ]
            yield 1
            for copy in arrivals:
                copy.wait_recv()

    in_turn([id_flow()])
    flows, crossing = gather_flows(weight_ways, blocks, slots, copies)

    def row_flow():
        yield 1
        first_row = lax.axis_index(axes) * shard_rows
        numbers = lax.broadcasted_iota(jnp.int32, (shard_rows, HALF), 0) + first_row

        def pick(k, carry):
            z, x, c = lax.div(k, 8), lax.rem(lax.div(k, 2), 4), lax.rem(k, 2)
            hits = (numbers == ids[z, x, c]).astype(jnp.float32).astype(low_type)
            found = tn(hits, table[...])
            picked[z, x, c] = found[:slot_rows].astype(low_type)
            return carry

        lax.fori_loop(0, 32, pick, 0)
        yield 10000
        yield scatter_flows(
            row_ways, "spread", picked, None, held, total, other, inbox, copies, 5000
        )
        yield from to_sub("spread", held, rows, copies)

    in_turn([*flows, row_flow()])
    for copy in crossing:
        copy.wait_recv()
    copies.finish()


def open_exchange(mine, table, blocks, number, weight_ways, row_ways, slot_rows):
    lanes = table.shape[1]
    inbox = scatter_slots(row_ways, lanes, low_type)
    stages = sum(len(order) for order, _ in weight_ways)
    return pl.pallas_call(
        functools.partial(open_kernel, weight_ways, row_ways),
        out_shape=[
            jax.ShapeDtypeStruct((4, 4, 2, *mine.shape), mine.dtype),
            jax.ShapeDtypeStruct((4, slot_rows, lanes), low_type),
            jax.ShapeDtypeStruct((4, 4, 2, *blocks.shape), blocks.dtype),
        ],
        in_specs=[pl.BlockSpec(memory_space=pltpu.VMEM)] * 2
        + [pl.BlockSpec(memory_space=pltpu.HBM)],
        out_specs=[pl.BlockSpec(memory_space=pltpu.VMEM)] * 2
        + [pl.BlockSpec(memory_space=pltpu.HBM)],
        scratch_shapes=[
            pltpu.VMEM((4, 4, 2, slot_rows, lanes), low_type),
            pltpu.VMEM((4, 4, slot_rows, lanes), low_type),
            pltpu.VMEM((4, 4, slot_rows, lanes), low_type),
            pltpu.VMEM((slot_rows, lanes), low_type),
        ]
        + inbox
        + semaphores(7 * stages + 8 + 7 + len(inbox) + 8 + 4, 16),
        compiler_params=pltpu.CompilerParams(
            collective_id=number, has_side_effects=True, vmem_limit_bytes=56 * MIB
        ),
    )(mine, table, blocks)


def added(values):
    total = values[0]
    for value in values[1:]:
        total = total + value
    return total


def merged(values):
    peaks = [value[0:32] for value in values]
    peak = functools.reduce(jnp.maximum, peaks)
    scales = [jnp.exp(p - peak) for p in peaks]
    total = added([value[32:64] * scale for value, scale in zip(values, scales)])
    hit = added([value[64:72] for value in values])
    gaps = [
        added([value[k : k + 8] * scale[0:8] for value, scale in zip(values, scales)])
        for k in (72, 80, 88)
    ]
    return jnp.concatenate([peak, total, hit, *gaps], 0)


def sum_kernel(axes, combine, value, out, *refs):
    slots, (send, recv) = refs[: len(axes)], refs[len(axes) :]
    greet(axes)
    copies = Copies(send, recv, None)
    out[...] = value[...]
    for axis, slot in zip(axes, slots):
        count = lax.axis_size(axis)
        me = lax.axis_index(axis)
        slot[me] = out[...]
        arrivals = [
            copies.push(slot.at[me], slot.at[me], axis, lax.rem(me + k, count))
            for k in range(1, count)
        ]
        for copy in arrivals:
            copy.wait_recv()
        out[...] = combine([slot[k] for k in range(count)])
    copies.finish()


def sum_all(value, number, axes, combine=added):
    counts = [lax.axis_size(axis) for axis in axes]
    sends = sum(counts) - len(axes)
    return pl.pallas_call(
        functools.partial(sum_kernel, axes, combine),
        out_shape=jax.ShapeDtypeStruct(value.shape, value.dtype),
        in_specs=[pl.BlockSpec(memory_space=pltpu.VMEM)],
        out_specs=pl.BlockSpec(memory_space=pltpu.VMEM),
        scratch_shapes=[pltpu.VMEM((n, *value.shape), value.dtype) for n in counts]
        + [pltpu.SemaphoreType.DMA((sends,))] * 2,
        compiler_params=pltpu.CompilerParams(
            collective_id=number, has_side_effects=True, vmem_limit_bytes=16 * MIB
        ),
    )(value)


def both_ways(rows):
    return ((("z", "x"), (0, rows // 2)), (("x", "z"), (rows // 2, rows // 2)))


def three_ways(first, second, last, orders):
    starts = (0, first, first + second)
    return tuple((o, (s, n)) for o, s, n in zip(orders, starts, (first, second, last)))


WEIGHT_WAYS = three_ways(1088, 1088, 1024, (("z", "x"), ("x", "z"), ("x", "z", "y")))
GRAD_WAYS = ((("z", "x", "y"), (0, 1664)), (("x", "z", "y"), (1664, 1536)))


def doc_layout(lengths):
    ends = jnp.cumsum(lengths, axis=-1)
    starts = ends - lengths
    place = jnp.arange(HALF, dtype=jnp.int32)
    member = (
        (place[:, None] >= starts[..., None, :]) & (place[:, None] < ends[..., None, :])
    ).astype(jnp.int32)
    inside = jnp.sum(member, -1)
    doc_of = jnp.sum(member * jnp.arange(DOCS, dtype=jnp.int32), -1) + DOCS * (1 - inside)
    offset = place - jnp.sum(member * starts[..., None, :], -1)
    return (doc_of, offset, inside)


def sinusoid(offset):
    half = D // 2
    freq = jnp.exp(jnp.arange(half, dtype=jnp.float32) * (-2.0 * math.log(10000.0) / D))
    angle = offset.astype(jnp.float32)[..., None] * freq
    return jnp.stack([jnp.sin(angle), jnp.cos(angle)], -1).reshape(offset.shape + (D,))


def layout():
    wide = D // BLK
    deep = FF // BLK
    return [
        (wide, 3 * wide),
        (wide, wide),
        (wide, deep),
        (deep, wide),
        (wide, 3 * wide),
        (wide, wide),
        (wide, wide),
        (wide, 2 * wide),
        (wide, wide),
        (wide, deep),
        (deep, wide),
    ]


def matmul(left, right):
    return jnp.dot(left, right, preferred_element_type=wide_type)


def shapes():
    return [(rows * BLK, cols * BLK) for rows, cols in layout()]


def first_block(number):
    return sum(rows * cols for rows, cols in layout()[:number])


def nt(left, right):
    return lax.dot_general(left, right, (((1,), (1,)), ((), ())), preferred_element_type=wide_type)


def tn(left, right):
    return lax.dot_general(left, right, (((0,), (0,)), ((), ())), preferred_element_type=wide_type)


def block_copies(number, slots, order, matrix, semaphore, outward):
    rows, cols = layout()[number]
    start = first_block(number)

    def step(k, carry):
        place = matrix.at[
            pl.ds(pl.multiple_of(lax.div(k, cols) * BLK, BLK), BLK),
            pl.ds(pl.multiple_of(lax.rem(k, cols) * BLK, BLK), BLK),
        ]
        slot = slots.at[order[start + k]]
        pair = (place, slot) if outward else (slot, place)
        pltpu.make_async_copy(*pair, semaphore).start()
        return carry

    lax.fori_loop(0, rows * cols, step, 0, unroll=5)


def mean_parts(stream, width, active):
    centre = jnp.sum(stream * width, -1, keepdims=True) / active
    centred = (stream - centre) * width
    spread = jnp.sum(centred * centred, -1, keepdims=True) / active
    return centred, lax.rsqrt(spread + eps_norm)


def normed(stream, vec, row, width, active):
    centred, rate = mean_parts(stream, width, active)
    return (centred * rate * vec[row : row + 1] + vec[row + 1 : row + 2]) * width


def normed_back(stream, vec, row, width, active, cotangent, vec_grad):
    centred, rate = mean_parts(stream, width, active)
    given = cotangent * width
    vec_grad[row : row + 1] = jnp.sum(given * centred * rate, 0, keepdims=True)
    vec_grad[row + 1 : row + 2] = jnp.sum(given, 0, keepdims=True)
    scaled = given * vec[row : row + 1]
    along = jnp.sum(scaled * centred, -1, keepdims=True) / active
    pulled = (scaled * rate - centred * (rate * rate * rate * along)) * width
    return pulled - width * (jnp.sum(pulled, -1, keepdims=True) / active)


def windows():
    for head in range(HEADS):
        low, high_end = head * HEAD, (head + 1) * HEAD
        first, last = low // BLK, (high_end - 1) // BLK + 1
        yield head, low, high_end, first, last


def lanes_between(low, high_end, first, last):
    lane = lax.broadcasted_iota(jnp.int32, (1, (last - first) * BLK), 1) + first * BLK
    return ((lane >= low) & (lane < high_end)).astype(jnp.float32).astype(low_type)


def tile_add(tiles, first, value):
    for k in range(value.shape[1] // BLK):
        part = value[:, k * BLK : (k + 1) * BLK]
        spot = first + k
        tiles[spot] = part if tiles[spot] is None else tiles[spot] + part


def weights_of(query, keys, mask, first, last, allowed):
    span = slice(first * BLK, last * BLK)
    scores = nt(query[:, span] * mask, keys[:, span]) * HEAD ** (-0.5)
    scores = jnp.where(allowed, scores, -1e30)
    expo = jnp.exp(scores - jnp.max(scores, -1, keepdims=True))
    return expo / jnp.sum(expo, -1, keepdims=True)


def attention(query, keys, values, allowed, keep):
    tiles = [None] * (D // BLK)
    for _, low, high_end, first, last in windows():
        mask = lanes_between(low, high_end, first, last)
        probs = weights_of(query, keys, mask, first, last, allowed).astype(low_type)
        tile_add(tiles, first, matmul(probs, values[:, first * BLK : last * BLK] * mask))
    return (jnp.concatenate(tiles, 1) * keep).astype(low_type)


def attention_back(d_rows, query, keys, values, allowed, keep):
    d_mixed = (d_rows * keep).astype(low_type)
    d_query, d_keys, d_values = ([None] * (D // BLK) for _ in range(3))
    for _, low, high_end, first, last in windows():
        mask = lanes_between(low, high_end, first, last)
        span = slice(first * BLK, last * BLK)
        probs = weights_of(query, keys, mask, first, last, allowed)
        given = d_mixed[:, span] * mask
        g_probs = nt(given, values[:, span])
        tile_add(d_values, first, tn(probs.astype(low_type), given))
        along = jnp.sum(probs * g_probs, -1, keepdims=True)
        d_scores = (probs * (g_probs - along)).astype(low_type)
        tile_add(d_query, first, matmul(d_scores, keys[:, span] * mask))
        tile_add(d_keys, first, tn(d_scores, query[:, span] * mask))
    scale = HEAD ** (-0.5)
    return (
        jnp.concatenate(d_query, 1) * scale,
        jnp.concatenate(d_keys, 1) * scale,
        jnp.concatenate(d_values, 1),
    )


GELU_RATE = math.sqrt(2.0 / math.pi)
CHUNK = 768


def gelu_parts(value):
    square = value * value
    bend = jnp.tanh(GELU_RATE * (value + 0.044715 * value * square))
    gate = 0.5 * (1.0 + bend)
    slope = gate + value * (
        0.5 * (1.0 - bend * bend) * GELU_RATE * (1.0 + 3.0 * 0.044715 * square)
    )
    return value * gate, slope


def forward_kernel(*refs):
    slots, order, x_zero, y_zero, vec, width, keep, unit, allowed = refs[:9]
    final, x_one, x_two, y_one, y_two, y_three = refs[9:15]
    qkv_enc, qkv_dec, q_cross, kv_cross, o_enc, o_dec, o_cross, memory = refs[15:23]
    h_enc, h_dec = refs[23:25]
    stored, held = refs[25:36], refs[36:47]
    act, arrive, leave = refs[47:]
    for number in (0, 1, 2, 3, 4, 5, 6, 7, 8, 9, 10):
        block_copies(number, slots, order, held[number], arrive.at[number], False)
    width, keep, vec = width[...], keep[...], vec[...]
    active = jnp.sum(width)
    same, causal = allowed[0] > 0.5, allowed[1] > 0.5

    def weight(number):
        pltpu.make_async_copy(stored[number], held[number], arrive.at[number]).wait()
        pltpu.make_async_copy(held[number], stored[number], leave.at[number]).start()
        return held[number]

    def self_part(stream, row, number, mask, qkv, mixed):
        near = normed(stream, vec, row, width, active).astype(low_type)
        matrix = weight(number)
        for k in range(3):
            part = slice(k * D, (k + 1) * D)
            qkv[:, part] = matmul(near, matrix[:, part]).astype(low_type)
        mixed[...] = attention(
            qkv[:, 0:D], qkv[:, D : 2 * D], qkv[:, 2 * D : 3 * D], mask, keep
        )
        return stream + matmul(mixed[...], weight(number + 1)[...]) * width

    def feed_part(stream, row, number, hidden):
        near = normed(stream, vec, row, width, active).astype(low_type)
        matrix = weight(number)
        for k in range(FF // CHUNK):
            part = slice(k * CHUNK, (k + 1) * CHUNK)
            value = matmul(near, matrix[:, part])
            hidden[:, part] = value
            act[:, part] = (gelu_parts(value)[0] * unit[:, part]).astype(low_type)
        return stream + matmul(act[...], weight(number + 1)[...]) * width

    x_one[...] = self_part(x_zero[...], 0, 0, same, qkv_enc, o_enc)
    x_two[...] = feed_part(x_one[...], 2, 2, h_enc)
    memory[...] = normed(x_two[...], vec, 4, width, active).astype(low_type)
    y_one[...] = self_part(y_zero[...], 6, 4, causal, qkv_dec, o_dec)
    near = normed(y_one[...], vec, 8, width, active).astype(low_type)
    q_cross[...] = matmul(near, weight(6)[...]).astype(low_type)
    kv_cross[...] = matmul(memory[...], weight(7)[...]).astype(low_type)
    o_cross[...] = attention(
        q_cross[...], kv_cross[:, 0:D], kv_cross[:, D : 2 * D], same, keep
    )
    y_two[...] = y_one[...] + matmul(o_cross[...], weight(8)[...]) * width
    y_three[...] = feed_part(y_two[...], 10, 9, h_dec)
    final[...] = normed(y_three[...], vec, 12, width, active).astype(low_type)
    for number in range(11):
        pltpu.make_async_copy(held[number], stored[number], leave.at[number]).wait()


def in_vmem(count):
    return [pl.BlockSpec(memory_space=pltpu.VMEM)] * count


def in_hbm(count):
    return [pl.BlockSpec(memory_space=pltpu.HBM)] * count


SMEM = pl.BlockSpec(memory_space=pltpu.SMEM)


def run_forward(slots, order, x_zero, y_zero, vec, width, keep, unit, allowed):
    def like(cols, kind):
        return jax.ShapeDtypeStruct((HALF, cols), kind)

    small = (
        [like(D, low_type)]
        + [like(D, wide_type)] * 5
        + [like(3 * D, low_type)] * 2
        + [like(D, low_type), like(2 * D, low_type)]
        + [like(D, low_type)] * 4
        + [like(FF, wide_type)] * 2
    )
    mats = [jax.ShapeDtypeStruct(shape, low_type) for shape in shapes()]
    return pl.pallas_call(
        forward_kernel,
        out_shape=small + mats,
        in_specs=in_hbm(1) + [SMEM] + in_vmem(7),
        out_specs=in_vmem(len(small)) + in_hbm(len(mats)),
        scratch_shapes=[pltpu.VMEM(shape, low_type) for shape in shapes()]
        + [pltpu.VMEM((HALF, FF), low_type)]
        + [pltpu.SemaphoreType.DMA((11,))] * 2,
        compiler_params=pltpu.CompilerParams(vmem_limit_bytes=56 * MIB),
    )(slots, order, x_zero, y_zero, vec, width, keep, unit, allowed)


def backward_kernel(*refs):
    order, d_final, x_zero, y_zero, vec, width, keep, unit, allowed = refs[:9]
    x_one, x_two, y_one, y_two, y_three = refs[9:14]
    qkv_enc, qkv_dec, q_cross, kv_cross, o_enc, o_dec, o_cross, memory = refs[14:22]
    h_enc, h_dec = refs[22:24]
    stored = refs[24:35]
    slots, vec_grad, d_rows = refs[35:38]
    held = refs[38:49]
    zeros, d_pack, arrive, leave, blank = refs[49:]
    uses = (10, 9, 8, 7, 6, 5, 4, 3, 2, 1, 0)
    for number in uses:
        pltpu.make_async_copy(stored[number], held[number], arrive.at[number]).start()
    zeros[...] = jnp.zeros_like(zeros)
    empty = order.shape[0] - NBLK
    for k in range(empty):
        pltpu.make_async_copy(zeros, slots.at[order[NBLK + k]], blank).start()
    width, keep, vec = width[...], keep[...], vec[...]
    active = jnp.sum(width)
    same, causal = allowed[0] > 0.5, allowed[1] > 0.5

    def weight(number):
        pltpu.make_async_copy(stored[number], held[number], arrive.at[number]).wait()
        return held[number]

    def send(number):
        block_copies(number, slots, order, held[number], leave.at[number], True)

    def keep_grad(number, value):
        held[number][...] = value.astype(low_type)
        send(number)

    def feed_back(given, stream, row, number, hidden):
        near = normed(stream, vec, row, width, active).astype(low_type)
        branch = (given * width).astype(low_type)
        up, down = weight(number), weight(number + 1)
        pulled = jnp.zeros((HALF, D), wide_type)
        for k in range(FF // CHUNK):
            part = slice(k * CHUNK, (k + 1) * CHUNK)
            d_act = nt(branch, down[part, :])
            value, slope = gelu_parts(hidden[:, part])
            act = (value * unit[:, part]).astype(low_type)
            down[part, :] = tn(act, branch).astype(low_type)
            d_hidden = (slope * (d_act * unit[:, part])).astype(low_type)
            pulled = pulled + nt(d_hidden, up[:, part])
            up[:, part] = tn(near, d_hidden).astype(low_type)
        send(number + 1)
        send(number)
        return given + normed_back(stream, vec, row, width, active, pulled, vec_grad)

    def self_back(given, stream, row, number, mask, qkv, mixed):
        near = normed(stream, vec, row, width, active).astype(low_type)
        branch = (given * width).astype(low_type)
        d_mixed = nt(branch, weight(number + 1)[...])
        keep_grad(number + 1, tn(mixed[...], branch))
        parts = attention_back(
            d_mixed, qkv[:, 0:D], qkv[:, D : 2 * D], qkv[:, 2 * D : 3 * D], mask, keep
        )
        for k in range(3):
            d_pack[:, k * D : (k + 1) * D] = parts[k].astype(low_type)
        matrix = weight(number)
        pulled = nt(d_pack[...], matrix[...])
        for k in range(3):
            part = slice(k * D, (k + 1) * D)
            matrix[:, part] = tn(near, d_pack[:, part]).astype(low_type)
        send(number)
        return given + normed_back(stream, vec, row, width, active, pulled, vec_grad)

    d_three = normed_back(
        y_three[...], vec, 12, width, active, d_final[...].astype(wide_type), vec_grad
    )
    d_two = feed_back(d_three, y_two[...], 10, 9, h_dec)
    near = normed(y_one[...], vec, 8, width, active).astype(low_type)
    branch = (d_two * width).astype(low_type)
    d_mixed = nt(branch, weight(8)[...])
    keep_grad(8, tn(o_cross[...], branch))
    parts = attention_back(
        d_mixed, q_cross[...], kv_cross[:, 0:D], kv_cross[:, D : 2 * D], same, keep
    )
    d_query = parts[0].astype(low_type)
    for k in range(2):
        d_pack[:, k * D : (k + 1) * D] = parts[k + 1].astype(low_type)
    d_memory = nt(d_pack[:, 0 : 2 * D], weight(7)[...])
    keep_grad(7, tn(memory[...], d_pack[:, 0 : 2 * D]))
    pulled = nt(d_query, weight(6)[...])
    keep_grad(6, tn(near, d_query))
    d_one = d_two + normed_back(y_one[...], vec, 8, width, active, pulled, vec_grad)
    d_target = self_back(d_one, y_zero[...], 6, 4, causal, qkv_dec, o_dec)
    d_enc = normed_back(x_two[...], vec, 4, width, active, d_memory, vec_grad)
    d_enc = feed_back(d_enc, x_one[...], 2, 2, h_enc)
    d_source = self_back(d_enc, x_zero[...], 0, 0, same, qkv_enc, o_enc)
    piece = HALF // 4
    for half, value in ((0, d_source), (1, d_target)):
        value = (value * width * math.sqrt(D)).astype(low_type)
        for k in range(4):
            at = (2 * k + half) * piece
            d_rows[at : at + piece] = value[k * piece : (k + 1) * piece]
    vec_grad[14:16] = jnp.zeros((2, D), wide_type)
    for number in range(11):
        pltpu.make_async_copy(held[number], stored[number], leave.at[number]).wait()
    blanks = slots.at[pl.ds(0, empty)]
    pltpu.make_async_copy(blanks, blanks, blank).wait()


def run_backward(order, d_final, x_zero, y_zero, vec, width, keep, unit, allowed, small, mats):
    return pl.pallas_call(
        backward_kernel,
        out_shape=[
            jax.ShapeDtypeStruct((order.shape[0], BLK, BLK), low_type),
            jax.ShapeDtypeStruct((16, D), wide_type),
            jax.ShapeDtypeStruct((2 * HALF, D), low_type),
        ],
        in_specs=[SMEM] + in_vmem(8 + len(small)) + in_hbm(len(mats)),
        out_specs=in_hbm(1) + in_vmem(2),
        scratch_shapes=[pltpu.VMEM(shape, low_type) for shape in shapes()]
        + [pltpu.VMEM((BLK, BLK), low_type), pltpu.VMEM((HALF, 3 * D), low_type)]
        + [pltpu.SemaphoreType.DMA((11,))] * 2
        + [pltpu.SemaphoreType.DMA],
        compiler_params=pltpu.CompilerParams(vmem_limit_bytes=56 * MIB),
    )(order, d_final, x_zero, y_zero, vec, width, keep, unit, allowed, *small, *mats)


def adamw(param, grad, first, second, rate):
    first = beta_one * first + (1.0 - beta_one) * grad
    second = beta_two * second + (1.0 - beta_two) * grad * grad
    fixed_first = first / (1.0 - beta_one**STEP)
    fixed_second = second / (1.0 - beta_two**STEP)
    return (
        param - rate * (fixed_first / (jnp.sqrt(fixed_second) + adam_eps) + decay_rate * param),
        first,
        second,
    )


def on_device(
    token_ids,
    target_ids,
    doc_lengths,
    width_tiles,
    head_mask,
    ffn_tiles,
    slot_block,
    master,
    momentum,
    left_stat,
    right_stat,
    left_root,
    right_root,
    table,
    table_m,
    table_v,
    vec,
    vec_m,
    vec_v,
):
    group = lax.axis_index("sub")
    place = lax.axis_index(TOK)
    groups = lax.axis_size("sub")
    shards = lax.axis_size(TOK)
    shard_rows = table.shape[0]
    piece = HALF // groups
    doc_of, offset, inside = doc_layout(doc_lengths)
    mine = jnp.concatenate(
        [
            quarter(token_ids[:HALF], group, piece),
            quarter(token_ids[HALF:], group, piece),
            quarter(jnp.where(inside > 0, target_ids, -1), group, piece),
            jnp.broadcast_to(jnp.sum(inside), (HALF - 3 * piece,)),
        ]
    )
    table_low = table.astype(low_type)
    heads_up, rows, slots = open_exchange(
        mine.reshape(1, HALF),
        table_low,
        master.astype(low_type).reshape(-1, BLK),
        1,
        WEIGHT_WAYS,
        both_ways(2 * piece),
        2 * piece,
    )
    heads_up = heads_up.reshape(shards, HALF)
    slots = slots.reshape(-1, BLK, BLK)
    rows = rows.astype(jnp.float32)
    all_targets = heads_up[:, 2 * piece : 3 * piece]
    weight = (all_targets >= 0).astype(jnp.float32)
    token_count = jnp.sum(heads_up[:, 3 * piece]).astype(jnp.float32)
    first_row = place * shard_rows
    rows = rows.reshape(groups, 2, piece, D).transpose(1, 0, 2, 3).reshape(2, HALF, D)
    used = slot_block < NBLK
    ranks = jnp.cumsum(1 - used.astype(jnp.int32)) - 1
    keys = jnp.where(used, slot_block, NBLK + ranks)
    numbers = jnp.arange(slot_block.shape[0], dtype=jnp.int32)
    order = jnp.sum(jnp.where(keys[None, :] == numbers[:, None], numbers[None, :], 0), 1)
    width = jnp.repeat(width_tiles[group], BLK).astype(jnp.float32)[None]
    keep = jnp.repeat(head_mask[group], HEAD).astype(jnp.float32)[None]
    unit = jnp.repeat(ffn_tiles[group], BLK).astype(jnp.float32)[None]
    wave = sinusoid(offset)
    source = (math.sqrt(D) * rows[0] + wave) * width
    target = (math.sqrt(D) * rows[1] + wave) * width
    same = doc_of[:, None] == doc_of[None, :]
    causal = same & (offset[None, :] <= offset[:, None])
    allowed = jnp.stack([same, causal]).astype(jnp.float32)
    common = (source, target, vec, width, keep, unit, allowed)
    final, *kept = run_forward(slots, order, *common)
    kept, mats = kept[:-11], kept[-11:]
    hidden = gather_tok(final, 4, both_ways(HALF), "rows").reshape(-1, D)
    logits = jnp.einsum("td,vd->tv", hidden, table_low, preferred_element_type=wide_type)
    logits = logits.reshape(shards, groups, piece, shard_rows)
    teacher = logits[:, :1]
    peak = jnp.max(logits, -1)
    total = jnp.sum(jnp.exp(logits - peak[..., None]), -1)
    hits = all_targets[..., None] - first_row == jnp.arange(shard_rows, dtype=jnp.int32)
    hit = jnp.sum(jnp.where(hits, logits[:, 0], 0.0), -1)
    gap = jnp.sum(jnp.exp(teacher - peak[:, :1, :, None]) * (teacher - logits[:, 1:]), -1)
    stats = jnp.concatenate([peak, total, hit[:, None], gap], 1).transpose(1, 0, 2)
    stats = sum_all(stats.reshape(-1, BLK), 5, TOK[::-1], merged)
    stats = stats.reshape(-1, shards, piece).transpose(1, 0, 2)
    logs = stats[:, :groups] + jnp.log(stats[:, groups : 2 * groups])
    hit = stats[:, 2 * groups]
    gap = stats[:, 2 * groups + 1 :] / stats[:, groups : groups + 1]
    token_loss = logs[:, 0] - hit + jnp.sum(logs[:, 1:] + gap - logs[:, :1], 1)
    loss_part = jnp.sum(token_loss * weight)
    target_dist = jnp.concatenate(
        [
            hits.astype(jnp.float32)[:, None],
            jnp.broadcast_to(
                jnp.exp(teacher - logs[:, :1, :, None]),
                (shards, groups - 1, piece, shard_rows),
            ),
        ],
        1,
    )
    back = (jnp.exp(logits - logs[..., None]) - target_dist) * (weight / token_count)[
        :, None, :, None
    ]
    back = back.astype(low_type).reshape(-1, shard_rows)
    d_hidden = matmul(back, table_low).astype(low_type).reshape(4, 4, 2, groups * piece, D)
    d_final = scatter_tok(d_hidden, 6, both_ways(HALF), "swap", 32 * MIB)
    table_grad = jnp.einsum("tv,td->vd", back, hidden, preferred_element_type=wide_type)
    slot_grads, vec_grad, d_rows = run_backward(
        order, d_final.reshape(HALF, D), *common, kept, mats
    )
    vec_grad = vec_grad[: vec.shape[0]]
    part = jnp.concatenate(
        [
            vec_grad.reshape(-1),
            jnp.zeros((BLK,), wide_type),
            jnp.broadcast_to(loss_part / shards, (BLK,)),
        ]
    )
    own, table_grad, small = close_exchange(
        slot_grads.reshape(4, 4, 2, -1, BLK),
        table_grad,
        d_rows,
        heads_up[:, : 2 * piece].reshape(4, 4, 1, HALF),
        part.reshape(-1, BLK),
        8,
        GRAD_WAYS,
        both_ways(2 * piece),
    )
    own = own.reshape(master.shape)
    small = small.reshape(-1)
    vec_grad = small[: vec.size].reshape(vec.shape)
    loss_sum = small[vec.size + BLK]
    square = jnp.sum(small[vec.size : vec.size + BLK])
    grad_norm = jnp.sqrt(square + jnp.sum(vec_grad * vec_grad))
    scale = jnp.minimum(1.0, clip_limit / grad_norm)
    grad = own * scale
    new_left = beta_stat * left_stat + (1.0 - beta_stat) * jnp.einsum(
        "sij,skj->sik", grad, grad, precision=high
    )
    new_right = beta_stat * right_stat + (1.0 - beta_stat) * jnp.einsum(
        "sji,sjk->sik", grad, grad, precision=high
    )
    new_momentum = beta_one * momentum + (1.0 - beta_one) * grad
    direction = jnp.einsum("sij,sjk->sik", left_root, new_momentum, precision=high)
    direction = jnp.einsum("sik,skl->sil", direction, right_root, precision=high)
    new_master = master - rate_blocks * (direction + decay_rate * master)
    new_table, new_table_m, new_table_v = adamw(
        table, table_grad * scale, table_m, table_v, rate_table
    )
    new_vec, new_vec_m, new_vec_v = adamw(vec, vec_grad * scale, vec_m, vec_v, rate_gains)
    return (
        loss_sum,
        token_count,
        grad_norm,
        new_master,
        new_momentum,
        new_left,
        new_right,
        new_table,
        new_table_m,
        new_table_v,
        new_vec,
        new_vec_m,
        new_vec_v,
    )


def solution(mesh):
    split = Mesh(
        mesh.devices.reshape(mesh.shape["sub"], 4, 4, 2), ("sub", "tok_0", "tok_1", "tok_2")
    )
    placed = (
        P(TOK),
        P(TOK),
        P(TOK),
        P(),
        P(),
        P(),
        P(),
        P(TOK, None, None),
        P(TOK, None, None),
        P(TOK, None, None),
        P(TOK, None, None),
        P(TOK, None, None),
        P(TOK, None, None),
        P(TOK, None),
        P(TOK, None),
        P(TOK, None),
        P(),
        P(),
        P(),
    )
    return jax.shard_map(
        on_device,
        mesh=split,
        in_specs=placed,
        out_specs=(
            P(),
            P(),
            P(),
            P(TOK, None, None),
            P(TOK, None, None),
            P(TOK, None, None),
            P(TOK, None, None),
            P(TOK, None),
            P(TOK, None),
            P(TOK, None),
            P(),
            P(),
            P(),
        ),
        check_vma=False,
    )
```
